128 devices in a mesh: sec: 16 (over x_lo, y, core), tile: 8 (over z, x_hi).
Axes of the slice: x: 4 (x_hi: 2, x_lo: 2; x = x_hi * 2 + x_lo), y: 4, z: 4, core: 2. Of those that a mesh axis runs over, the one named last changes fastest.
Arguments:
- sections: float32 [16, 8, 128, 128, 128], P('sec', None, 'tile'), may hold values from -6 to 6
- node_mask: int32 [16, 8, 128], P('sec', None, 'tile'), may hold values 0 or 1
- box_row: int32 [16, 8, 128, 4], P('sec', None, 'tile'), may hold values from 0 to 7, as said below
- box_shift: int32 [16, 8, 128, 4], P('sec', None, 'tile'), may hold values from -2 to 2
- box_count: int32 [16, 8, 128], P('sec', None, 'tile'), may hold values from 1 to 4, as said below
- blend_weight: float32 [16, 8, 128, 4], P('sec', None, 'tile'), may hold values from 0.25 to 4
Outputs:
- rendered: bfloat16 [16, 8, 128, 128, 128], P('sec', None, 'tile')
- node_field: float32 [16, 2, 8, 128], P('sec', None, None, 'tile')
The draws below stay inside these ranges and needn't reach their ends.
Inputs may be any that keep to these rules, and one draw needn't show every extreme that they name: Within a cell's 4 slots the pairs (box_row, box_shift) are all different. `box_count`: in every section a band of columns around a drawn centre (wrapping around, a quarter of the width to each side) has 3 or 4 live boxes per cell, all other cells 1 or 2.
All inputs are finite; a program needn't handle non-finite values. No bound on the sum of `node_mask` on one device may be relied on, other than what follows from the above.
Results may differ from the reference program's by a relative error of at most 0.0054.
Values may be sent and summed in bfloat16 or wider, within the bound.
No kernel may reach another device: no remote copies, remote signals or barrier semaphores. Data moves between devices by JAX's collectives and lax.ppermute only.
A program may use at most 192 MiB of HBM per device.

```python
import math
import jax
import jax.numpy as jnp
from jax import lax

PATCH = 128
K = 4
HB = 2
STEPS = 3
PY = 8
NSEC = 16
PX_ALL = 128


def choose_boxes(key):
    options = PY * (2 * HB + 1)
    scores = jax.random.randint(key, (NSEC, PY, PX_ALL, options), 0, 2 ** 20) * options + jnp.arange(options)
    order = jnp.argsort(scores, axis=-1)
    return order[..., :K].astype(jnp.int32)


def draw_box_row(key, part):
    picked = choose_boxes(key)
    return (picked // (2 * HB + 1)).astype(jnp.int32)


def draw_box_shift(key, part):
    picked = choose_boxes(key)
    return (picked % (2 * HB + 1) - HB).astype(jnp.int32)


def draw_box_count(key, part):
    key = jax.random.fold_in(key, 7)
    first, second, third = jax.random.split(key, 3)
    centre = jax.random.randint(first, (NSEC, 1, 1), 0, PX_ALL)
    columns = jnp.arange(PX_ALL)[None, None, :]
    apart = jnp.abs(columns - centre)
    apart = jnp.minimum(apart, PX_ALL - apart)
    tissue = apart < PX_ALL // 4
    dense = jax.random.randint(second, (NSEC, PY, PX_ALL), K - 1, K + 1)
    sparse = jax.random.randint(third, (NSEC, PY, PX_ALL), 1, 3)
    count = jnp.where(tissue, dense, sparse)
    rows = jnp.arange(PY)[None, :, None]
    count = jnp.where((rows == 0) & (apart == 0), K, count)
    count = jnp.where((rows == 0) & (apart == PX_ALL // 2), 1, count)
    return count.astype(jnp.int32)


def set_ends(values, stream_key, smallest, top_value):
    longest = values.shape.index(max(values.shape))
    spots = []
    for shift in (0, 1):
        where = [jax.random.randint(jax.random.fold_in(stream_key, axis), (), 0, length) for axis, length in enumerate(values.shape)]
        where[longest] = (where[longest] + shift) % values.shape[longest]
        spots.append(tuple(where))
    return values.at[spots[0]].set(smallest).at[spots[1]].set(top_value)


def steps_of(rng, shape, shards, low, high):
    loudness = 1.0
    for position, shards_of in shards:
        draws = jax.random.uniform(jax.random.fold_in(jax.random.fold_in(rng, 6), position), (shards_of,), jnp.float32, low / len(shards), high / len(shards))
        loudness = loudness * jnp.repeat(jnp.exp(draws), shape[position] // shards_of).reshape((-1,) + (1,) * (len(shape) - 1 - position))
    return loudness


def scatter_about(stream_key, dims, deviation, limit, cuts=(), kind=jnp.bfloat16):
    loudness = steps_of(stream_key, dims, cuts, -0.22, 0.18) if cuts else 1.0
    result = jax.random.normal(stream_key, dims, jnp.float32) * deviation * loudness
    return jnp.minimum(jnp.maximum(result, -limit), limit).astype(kind)


def setup_inputs(seed: int = 0) -> dict:
    streams_of = jax.random.split(jax.random.key(seed), 7)
    return {
        "sections": scatter_about(streams_of[0], (NSEC, PY, PX_ALL, PATCH, PATCH), 1.0, 6.0, ((0, 16), (2, 8)), jnp.float32),
        "node_mask": set_ends((jax.random.randint(streams_of[1], (NSEC, PY, PX_ALL), 0, 4) < 3).astype(jnp.int32), jax.random.fold_in(streams_of[1], 1), 0, 1),
        "box_row": draw_box_row(jax.random.fold_in(streams_of[6], 71), 0),
        "box_shift": draw_box_shift(jax.random.fold_in(streams_of[6], 71), 0),
        "box_count": draw_box_count(jax.random.fold_in(streams_of[6], 71), 0),
        "blend_weight": jnp.clip(jnp.exp(math.log(4.0) - 2.7725887 * jax.random.uniform(streams_of[5], (NSEC, PY, PX_ALL, K), jnp.float32) ** steps_of(streams_of[5], (NSEC, PY, PX_ALL, K), ((0, 16), (2, 8)), -0.2, 0.2)), 0.25, 4.0),
    }


spring_rate = 0.2
epsilon = 1e-6


def offsets(count):
    positions = jnp.arange(count)
    return ((positions + count // 2) % count - count // 2).astype(jnp.float32)


def correlate(first, second):
    spectrum = jnp.fft.fft2(first) * jnp.conj(jnp.fft.fft2(second))
    return jnp.real(jnp.fft.ifft2(spectrum))


def flow_of(corr):
    power = corr * corr
    total = power.sum((-2, -1)) + epsilon
    shifts = offsets(corr.shape[-1])
    along_rows = (power.sum(-1) * shifts).sum(-1) / total
    along_cols = (power.sum(-2) * shifts).sum(-1) / total
    return jnp.stack((along_rows, along_cols))


def laplace(field):
    widths = [(0, 0)] * (field.ndim - 2) + [(1, 1), (1, 1)]
    padded = jnp.pad(field, widths)
    beside_all = padded[..., 2:, 1:-1] + padded[..., :-2, 1:-1]
    beside_all = beside_all + padded[..., 1:-1, 2:] + padded[..., 1:-1, :-2]
    return beside_all - 4.0 * field


def hat(shift, size):
    rows = jnp.arange(size).astype(jnp.float32)[:, None]
    cols = jnp.arange(size).astype(jnp.float32)[None, :]
    return jnp.maximum(0.0, 1.0 - jnp.abs(cols - rows - shift[..., None, None]))


def reference(sections, node_mask, box_row, box_shift, box_count, blend_weight):
    following = jnp.concatenate((sections[1:], jnp.zeros_like(sections[:1])), axis=0)

    def section_flow(pair):
        return flow_of(correlate(pair[0], pair[1]).astype(jnp.float32))

    flow = lax.map(section_flow, (sections, following))
    trust = node_mask.astype(jnp.float32)[:, None]
    node_field = trust * flow
    for step in range(STEPS):
        node_field = node_field + spring_rate * (laplace(node_field) + trust * (flow - node_field))
    live = jnp.arange(K)[None, None, None, :] < box_count[..., None]
    weights = jnp.where(live, blend_weight, 0.0)
    share = (weights / weights.sum(-1, keepdims=True)).astype(jnp.bfloat16)

    def render(pieces):
        picture, rows, moves, parts, field = pieces
        source = jnp.pad(picture.astype(jnp.bfloat16), ((0, 0), (HB, HB), (0, 0), (0, 0)))
        columns = (jnp.arange(PX_ALL)[None, :, None] + moves + HB).astype(jnp.int32)
        picked = source[rows.astype(jnp.int32), columns]
        blended = jnp.einsum('yxk,yxkij->yxij', parts.astype(jnp.float32), picked.astype(jnp.float32), precision=lax.Precision.HIGHEST)
        row_hat = hat(field[0], PATCH)
        col_hat = hat(field[1], PATCH)
        warped = jnp.einsum('yxij,yxjl->yxil', row_hat, blended, precision=lax.Precision.HIGHEST)
        warped = jnp.einsum('yxil,yxml->yxim', warped, col_hat, precision=lax.Precision.HIGHEST)
        return warped.astype(jnp.bfloat16)

    rendered = lax.map(render, (sections, box_row, box_shift, share, node_field))
    return rendered, node_field
```

```python
import functools

import jax
import jax.numpy as jnp
import numpy as np
from jax import lax
from jax.experimental import pallas as pl
from jax.experimental.pallas import tpu as pltpu
from jax.sharding import PartitionSpec as P

K = 4
HB = 2
STEPS = 3
N = 128
HALF = N // 2
PAD = 72
SPRING = 0.2
EPS = 1e-06
MIB = 1024 * 1024


def split(x):
    high = x.astype(jnp.bfloat16)
    return high, (x - high.astype(jnp.float32)).astype(jnp.bfloat16)


def tables():
    grid = np.arange(N)[:, None] * np.arange(N)[None, :] % N
    cosine = np.cos(2.0 * np.pi * grid / N)
    sine = np.sin(2.0 * np.pi * grid / N)
    rows = np.concatenate([cosine[:HALF], sine[:HALF]])
    rows[HALF] = cosine[HALF]
    cols = np.block([[cosine, -sine], [-sine, -cosine]])
    back_cols = np.block([[cosine, sine], [-sine, cosine]]) / N
    weight = np.where(np.arange(HALF) == 0, 1.0, 2.0)
    back_rows = np.concatenate([cosine[:, :HALF] * weight, -2.0 * sine[:, :HALF]], axis=1) / N
    back_rows[:, HALF] = cosine[:, HALF] / N
    return [jnp.asarray(t, jnp.float32) for t in (rows, cols, back_cols, back_rows)]


def first_row(shape):
    return lax.broadcasted_iota(jnp.int32, shape, len(shape) - 2) == 0


def dot(a, b):
    return jnp.dot(a, b, preferred_element_type=jnp.float32)


def forward_kernel(x_ref, rows_ref, cols_ref, spec_ref, src_ref):
    patches = x_ref.shape[2]
    rows2 = rows_ref[...]
    cols = cols_ref[...]
    for pair in range(patches // 2):
        x = jnp.concatenate([x_ref[0, 0, 2 * pair], x_ref[0, 0, 2 * pair + 1]], axis=1)
        high, low = split(x)
        src_ref[0, 2 * pair] = high[:, :N]
        src_ref[0, 2 * pair + 1] = high[:, N:]
        y = dot(rows2, jnp.concatenate([high, low], axis=0))
        left = jnp.concatenate([y[:HALF, :N], y[HALF:, :N]], axis=1)
        right = jnp.concatenate([y[:HALF, N:], y[HALF:, N:]], axis=1)
        lines = jnp.concatenate([left, right], axis=0)
        lines_high, lines_low = split(lines)
        freq = dot(lines_high, cols) + dot(lines_low, cols)
        freq = freq.reshape(2, HALF, 2 * N)
        keep = lines.reshape(2, HALF, 2 * N)
        out = jnp.where(first_row(freq.shape), keep, freq)
        spec_ref[0, 2 * pair] = out[0].astype(jnp.bfloat16)
        spec_ref[0, 2 * pair + 1] = out[1].astype(jnp.bfloat16)


def forward(sections, rows, cols):
    _, ny, nx, _, _ = sections.shape
    rows2 = jnp.concatenate([rows, rows], axis=1).astype(jnp.bfloat16)
    whole = lambda shape: pl.BlockSpec(shape, lambda y: (0,) * len(shape))
    return pl.pallas_call(
        forward_kernel,
        grid=(ny,),
        in_specs=[
            pl.BlockSpec((1, 1, nx, N, N), lambda y: (0, y, 0, 0, 0)),
            whole((N, 2 * N)),
            whole((2 * N, 2 * N)),
        ],
        out_specs=[
            pl.BlockSpec((1, nx, HALF, 2 * N), lambda y: (y, 0, 0, 0)),
            pl.BlockSpec((1, nx, N, N), lambda y: (y, 0, 0, 0)),
        ],
        out_shape=[
            jax.ShapeDtypeStruct((ny, nx, HALF, 2 * N), jnp.bfloat16),
            jax.ShapeDtypeStruct((ny, nx, N, N), jnp.bfloat16),
        ],
        compiler_params=pltpu.CompilerParams(vmem_limit_bytes=32 * MIB),
        cost_estimate=pl.CostEstimate(flops=4_000_000_000, bytes_accessed=16 * MIB, transcendentals=0),
        name="forward",
    )(sections, rows2, cols.astype(jnp.bfloat16))


def times_conj(a, b, sign):
    ar, ai, br, bi = a[:, :N], a[:, N:], b[:, :N], b[:, N:]
    real = ar * br + ai * bi
    imag = ai * br - ar * bi if sign > 0 else ar * bi - ai * br
    return jnp.concatenate([real, imag], axis=1).astype(jnp.bfloat16)


def flow_kernel(sign, own_ref, other_ref, cols_ref, back_cols_ref, back_rows_ref, flow_ref, sums, moments):
    y = pl.program_id(0)
    patches = own_ref.shape[1]
    cols = cols_ref[...]
    back_cols = back_cols_ref[...]
    back_rows = back_rows_ref[...]
    own = own_ref[0]
    other = other_ref[0]
    lines = jnp.concatenate(
        [r[:, 0, :].astype(jnp.float32) for r in (own, other)], axis=0
    ).astype(jnp.bfloat16)
    edge = jnp.concatenate([lines[:, :N], lines[:, N:]], axis=0)
    edge = dot(edge, cols[:N])
    quarter = edge.reshape(4, patches, 2 * N)
    low = times_conj(quarter[0], quarter[1], sign)
    high = times_conj(quarter[2], quarter[3], sign)
    sides = dot(jnp.concatenate([low, high], axis=0), back_cols[:, :N])
    shift_rows = lax.broadcasted_iota(jnp.int32, (N, N), 0)
    offset_rows = (((shift_rows + HALF) % N) - HALF).astype(jnp.float32)
    offset_rows = jnp.concatenate([offset_rows, offset_rows], axis=1)
    for pair in range(patches // 2):
        a = own_ref[0, 2 * pair : 2 * pair + 2].reshape(2 * HALF, 2 * N).astype(jnp.float32)
        b = other_ref[0, 2 * pair : 2 * pair + 2].reshape(2 * HALF, 2 * N).astype(jnp.float32)
        back = dot(times_conj(a, b, sign), back_cols)
        halves = []
        for side in range(2):
            p = 2 * pair + side
            real = back[side * HALF : (side + 1) * HALF, :N]
            imag = back[side * HALF : (side + 1) * HALF, N:]
            real = jnp.where(first_row(real.shape), sides[p : p + 1], real)
            imag = jnp.where(first_row(imag.shape), sides[patches + p : patches + p + 1], imag)
            halves.append(jnp.concatenate([real, imag], axis=0).astype(jnp.bfloat16))
        corr = dot(back_rows, jnp.concatenate(halves, axis=1))
        power = corr * corr
        total = power.sum(0, keepdims=True)
        moment = (power * offset_rows).sum(0, keepdims=True)
        for side in range(2):
            p = 2 * pair + side
            sums[p : p + 1, :] = total[:, side * N : (side + 1) * N]
            moments[p : p + 1, :] = moment[:, side * N : (side + 1) * N]
    lane = lax.broadcasted_iota(jnp.int32, (8, N), 1)
    row = lax.broadcasted_iota(jnp.int32, (8, N), 0)
    offset_cols = (((lane + HALF) % N) - HALF).astype(jnp.float32)
    reduce_by = jnp.where(row == 0, 1.0, jnp.where(row == 1, offset_cols, 0.0))
    over_lanes = lambda m: lax.dot_general(
        reduce_by, m, (((1,), (1,)), ((), ())),
        precision=lax.Precision.HIGHEST, preferred_element_type=jnp.float32,
    )
    by_sums = over_lanes(sums[...])
    by_moments = over_lanes(moments[...])
    total = by_sums[0:1] + EPS
    flow_ref[0, pl.ds(y, 1), :] = by_moments[0:1] / total
    flow_ref[1, pl.ds(y, 1), :] = by_sums[1:2] / total


def flow_of(own, first, other, sign, cols, back_cols, back_rows):
    ny, nx = other.shape[:2]
    whole = lambda shape: pl.BlockSpec(shape, lambda y: (0,) * len(shape))
    block = (1, nx, HALF, 2 * N)
    return pl.pallas_call(
        functools.partial(flow_kernel, sign),
        grid=(ny,),
        in_specs=[
            pl.BlockSpec(block, lambda y: (y + first, 0, 0, 0)),
            pl.BlockSpec(block, lambda y: (y, 0, 0, 0)),
            whole((2 * N, 2 * N)),
            whole((2 * N, 2 * N)),
            whole((N, N)),
        ],
        out_specs=whole((2, ny, nx)),
        out_shape=jax.ShapeDtypeStruct((2, ny, nx), jnp.float32),
        scratch_shapes=[pltpu.VMEM((nx, N), jnp.float32), pltpu.VMEM((nx, N), jnp.float32)],
        compiler_params=pltpu.CompilerParams(vmem_limit_bytes=32 * MIB),
        cost_estimate=pl.CostEstimate(flops=2_000_000_000, bytes_accessed=8 * MIB, transcendentals=0),
        name="flow",
    )(own, other, *(t.astype(jnp.bfloat16) for t in (cols, back_cols, back_rows)))


def blend_kernel(target_ref, share_ref, src_ref, low_ref, high_ref, out_ref, window, sems):
    y = pl.program_id(0)
    nx = src_ref.shape[1]

    @pl.when(y == 0)
    def _():
        copies = [
            pltpu.make_async_copy(src_ref, window.at[:, HB : HB + nx], sems.at[0]),
            pltpu.make_async_copy(low_ref, window.at[:, :HB], sems.at[1]),
            pltpu.make_async_copy(high_ref, window.at[:, HB + nx :], sems.at[2]),
        ]
        for copy in copies:
            copy.start()
        for copy in copies:
            copy.wait()

    def cell(x, carry):
        base = (y * nx + x) * K
        total = None
        for k in range(K):
            spot = target_ref[base + k]
            piece = window[spot // (nx + 2 * HB), spot % (nx + 2 * HB)].astype(jnp.float32) * share_ref[base + k]
            total = piece if total is None else total + piece
        out_ref[0, x] = total
        return carry

    lax.fori_loop(0, nx, cell, 0, unroll=2)


def blend(target, share, source, low, high):
    ny, nx = source.shape[:2]
    return pl.pallas_call(
        blend_kernel,
        grid=(ny,),
        in_specs=[
            pl.BlockSpec(memory_space=pltpu.SMEM),
            pl.BlockSpec(memory_space=pltpu.SMEM),
            pl.BlockSpec(memory_space=pl.ANY),
            pl.BlockSpec(memory_space=pl.ANY),
            pl.BlockSpec(memory_space=pl.ANY),
        ],
        out_specs=pl.BlockSpec((1, nx, N, N), lambda y: (y, 0, 0, 0)),
        out_shape=jax.ShapeDtypeStruct((ny, nx, N, N), jnp.float32),
        scratch_shapes=[
            pltpu.VMEM((ny, nx + 2 * HB, N, N), jnp.bfloat16),
            pltpu.SemaphoreType.DMA((3,)),
        ],
        compiler_params=pltpu.CompilerParams(vmem_limit_bytes=32 * MIB),
        cost_estimate=pl.CostEstimate(flops=20_000_000, bytes_accessed=13 * MIB, transcendentals=0),
        name="blend",
    )(target, share, source, low, high)


def relax_kernel(flow_ref, trust_ref, valid_ref, out_ref):
    ny = flow_ref.shape[1]
    trust = trust_ref[...]
    valid = valid_ref[...]
    row = lax.broadcasted_iota(jnp.int32, trust.shape, 0)
    for component in range(2):
        flow = flow_ref[component]
        field = trust * flow
        for _ in range(STEPS):
            below = jnp.where(row == 0, 0.0, pltpu.roll(field, 1, 0))
            above = jnp.where(row == ny - 1, 0.0, pltpu.roll(field, ny - 1, 0))
            beside = pltpu.roll(field, 1, 1) + pltpu.roll(field, field.shape[1] - 1, 1)
            lap = above + below + beside - 4.0 * field
            field = (field + SPRING * (lap + trust * (flow - field))) * valid
        out_ref[component] = field


def relax(flow, trust, valid):
    return pl.pallas_call(
        relax_kernel,
        out_shape=jax.ShapeDtypeStruct(flow.shape, jnp.float32),
        name="relax",
    )(flow, trust, valid)


def warp_kernel(field_ref, blended_ref, out_ref, padded, sems):
    y = pl.program_id(0)
    ny = pl.num_programs(0)
    nx = out_ref.shape[2]
    slot = y % 2

    def fetch(row, into):
        return pltpu.make_async_copy(
            blended_ref.at[row], padded.at[into, :, PAD : PAD + N], sems.at[into]
        )

    @pl.when(y == 0)
    def _():
        padded[:, :, :PAD] = jnp.zeros((2, nx, PAD, N), jnp.float32)
        padded[:, :, PAD + N :] = jnp.zeros((2, nx, PAD, N), jnp.float32)
        fetch(0, 0).start()

    @pl.when(y + 1 < ny)
    def _():
        fetch(y + 1, 1 - slot).start()

    fetch(y, slot).wait()
    lane = lax.broadcasted_iota(jnp.int32, (1, N), 1)

    def whole_and_part(shift):
        whole = jnp.clip((shift + 256.0).astype(jnp.int32) - 256, 4 - PAD, PAD - 6)
        return whole, shift - whole.astype(jnp.float32)

    def cell(x, carry):
        down, part = whole_and_part(field_ref[0, y, x])
        upper = padded[slot, x, pl.ds(PAD + down, N), :]
        lower = padded[slot, x, pl.ds(PAD + 1 + down, N), :]
        image = upper + part * (lower - upper)
        right, part = whole_and_part(field_ref[1, y, x])
        spot = lane + right
        near = jnp.where((spot >= 0) & (spot < N), 1.0 - part, 0.0)
        far = jnp.where((spot >= -1) & (spot < N - 1), part, 0.0)
        turn = (2 * N - right) % N
        turned = pltpu.roll(image, turn, 1)
        out = turned * near + pltpu.roll(turned, N - 1, 1) * far
        out_ref[0, 0, x] = out.astype(jnp.bfloat16)
        return carry

    lax.fori_loop(0, nx, cell, 0, unroll=2)


def warp(field, blended):
    ny, nx = blended.shape[:2]
    return pl.pallas_call(
        warp_kernel,
        grid=(ny,),
        in_specs=[
            pl.BlockSpec(memory_space=pltpu.SMEM),
            pl.BlockSpec(memory_space=pl.ANY),
        ],
        out_specs=pl.BlockSpec((1, 1, nx, N, N), lambda y: (0, y, 0, 0, 0)),
        out_shape=jax.ShapeDtypeStruct((1, ny, nx, N, N), jnp.bfloat16),
        scratch_shapes=[
            pltpu.VMEM((2, nx, 2 * PAD + N, N), jnp.float32),
            pltpu.SemaphoreType.DMA((2,)),
        ],
        compiler_params=pltpu.CompilerParams(vmem_limit_bytes=32 * MIB),
        cost_estimate=pl.CostEstimate(flops=20_000_000, bytes_accessed=12 * MIB, transcendentals=0),
        name="warp",
    )(field, blended)


def from_behind(x, axis, by):
    length = lax.axis_size(axis)
    pairs = [(i, i + by) for i in range(length) if 0 <= i + by < length]
    return lax.ppermute(x, axis, pairs)


def bordered(x, width):
    low = from_behind(x[..., x.shape[-1] - width :], "tile", 1)
    high = from_behind(x[..., :width], "tile", -1)
    return jnp.concatenate([low, x, high], axis=-1)


def to_lanes(x):
    return jnp.pad(x, ((0, 0),) * (x.ndim - 1) + ((0, N - x.shape[-1]),))


def per_device(sections, node_mask, box_row, box_shift, box_count, blend_weight):
    ny, nx = sections.shape[1:3]
    rows, cols, back_cols, back_rows = tables()
    half = ny // 2
    spectra, source = forward(sections, rows, cols)
    from_next = from_behind(spectra[:half], "sec", -1)
    from_last = from_behind(spectra[half:], "sec", 1)
    low = from_behind(source[:, nx - HB :], "tile", 1)
    high = from_behind(source[:, :HB], "tile", -1)
    trust = node_mask[0].astype(jnp.float32)
    known = to_lanes(bordered(jnp.stack([trust, jnp.ones_like(trust)]), STEPS))

    live = jnp.arange(K)[None, None, :] < box_count[0][..., None]
    weights = jnp.where(live, blend_weight[0], 0.0)
    share = (weights / weights.sum(-1, keepdims=True)).astype(jnp.bfloat16).astype(jnp.float32)
    local_col = jnp.arange(nx)[None, :, None]
    target = box_row[0] * (nx + 2 * HB) + local_col + HB + box_shift[0]
    blended = blend(target.reshape(-1), share.reshape(-1), source, low, high)

    flow_high = flow_of(spectra, half, from_last, -1, cols, back_cols, back_rows)
    flow_high = from_behind(flow_high, "sec", -1)
    flow_low = flow_of(spectra, 0, from_next, 1, cols, back_cols, back_rows)
    flow = to_lanes(bordered(jnp.concatenate([flow_low, flow_high], axis=1), STEPS))
    field = relax(flow, known[0], known[1])[:, :, STEPS : STEPS + nx]
    rendered = warp(field, blended)
    return (rendered, field[None])


def solution(mesh):
    return jax.shard_map(
        per_device,
        mesh=mesh,
        in_specs=(
            P("sec", None, "tile", None, None),
            P("sec", None, "tile"),
            P("sec", None, "tile", None),
            P("sec", None, "tile", None),
            P("sec", None, "tile"),
            P("sec", None, "tile", None),
        ),
        out_specs=(P("sec", None, "tile", None, None), P("sec", None, None, "tile")),
        check_vma=False,
    )
```

```python
import functools

import jax
import jax.numpy as jnp
import numpy as np
from jax import lax
from jax.experimental import pallas as pl
from jax.experimental.pallas import tpu as pltpu
from jax.sharding import PartitionSpec as P

K = 4
HB = 2
STEPS = 3
N = 128
HALF = N // 2
PAD = 72
ROW = 32
DEPTH = 3
SPRING = 0.2
EPS = 1e-06
MIB = 1024 * 1024
VMEM = 56 * MIB


def split(x):
    high = x.astype(jnp.bfloat16)
    return high, (x - high.astype(jnp.float32)).astype(jnp.bfloat16)


def tables():
    grid = np.arange(N)[:, None] * np.arange(N)[None, :] % N
    cosine = np.cos(2.0 * np.pi * grid / N)
    sine = np.sin(2.0 * np.pi * grid / N)
    rows = np.concatenate([cosine[:HALF], sine[:HALF]])
    rows[HALF] = cosine[HALF]
    cols = np.block([[cosine, -sine], [-sine, -cosine]])
    back_cols = np.block([[cosine, sine], [-sine, cosine]]) / N
    weight = np.where(np.arange(HALF) == 0, 1.0, 2.0)
    back_rows = np.concatenate([cosine[:, :HALF] * weight, -2.0 * sine[:, :HALF]], axis=1) / N
    back_rows[:, HALF] = cosine[:, HALF] / N
    return [jnp.asarray(t, jnp.float32) for t in (rows, cols, back_cols, back_rows)]


def first_row(shape):
    return lax.broadcasted_iota(jnp.int32, shape, len(shape) - 2) == 0


def dot(a, b):
    return jnp.dot(a, b, preferred_element_type=jnp.float32)


def ahead(fetch, rows, depth):
    y = pl.program_id(0)

    @pl.when(y == 0)
    def _():
        for row in range(depth):
            for copy in fetch(row):
                copy.start()

    @pl.when(y + depth < rows)
    def _():
        for copy in fetch(y + depth):
            copy.start()

    for copy in fetch(y):
        copy.wait()


def wait_all(copies):
    @pl.when(pl.program_id(0) == pl.num_programs(0) - 1)
    def _():
        for copy in copies:
            copy.wait()


def forward_kernel(x_hbm, rows_ref, cols_ref, *refs):
    *out_hbm, x_ref, lines_ref, spec, strip, in_sems, out_sems = refs
    y = pl.program_id(0)
    ny, patches = x_ref.shape[:2]
    half = ny // 2
    fetch = lambda row: [pltpu.make_async_copy(x_hbm.at[0, row], x_ref.at[row], in_sems.at[row])]
    ahead(fetch, ny, DEPTH)

    rows2 = rows_ref[...]
    cols = cols_ref[...]
    cols2 = jnp.concatenate([cols, cols], axis=0)
    for pair in range(patches // 2):
        x = jnp.concatenate([x_ref[y, 2 * pair], x_ref[y, 2 * pair + 1]], axis=1)
        high, low = split(x)
        part = {0: 0, 1: 1, patches // 2 - 2: 2, patches // 2 - 1: 3}.get(pair)
        if part is not None:
            strip[y, part, 0] = high[:, :N]
            strip[y, part, 1] = high[:, N:]
        both = dot(rows2, jnp.concatenate([high, low], axis=0))
        for side in range(2):
            here = both[:, side * N : (side + 1) * N]
            lines = jnp.concatenate([here[:HALF], here[HALF:]], axis=1)
            first = (2 * pair + side) * HALF
            high, low = split(lines)
            lines_ref[first : first + HALF, : 2 * N] = high
            lines_ref[first : first + HALF, 2 * N :] = low
    step = 4
    for first in range(0, patches, step):
        lines = lines_ref[first * HALF : (first + step) * HALF, :]
        freq = dot(lines, cols2).reshape(step, HALF, 2 * N)
        keep = lines[:, : 2 * N].astype(jnp.float32).reshape(step, HALF, 2 * N)
        out = jnp.where(first_row(freq.shape), keep, freq)
        spec[y, first : first + step] = out.astype(jnp.bfloat16)

    def spectra_to(row):
        ref = out_hbm[0].at[row] if row < half else out_hbm[1].at[row - half]
        return pltpu.make_async_copy(spec.at[row], ref, out_sems.at[row])

    strips_to = [
        pltpu.make_async_copy(strip.at[:, i], ref, out_sems.at[ny + i]) for i, ref in enumerate(out_hbm[2:])
    ]
    for row in range(ny):
        pl.when(y == row)(spectra_to(row).start)
    pl.when(y == ny - 1)(lambda: [copy.start() for copy in strips_to] and None)
    wait_all([spectra_to(row) for row in range(ny)] + strips_to)


def forward(sections, rows, cols):
    _, ny, nx, _, _ = sections.shape
    half = ny // 2
    rows2 = jnp.concatenate([rows, rows], axis=1).astype(jnp.bfloat16)
    whole = lambda shape: pl.BlockSpec(shape, lambda y: (0,) * len(shape))
    return pl.pallas_call(
        forward_kernel,
        grid=(ny,),
        in_specs=[
            pl.BlockSpec(memory_space=pl.ANY),
            whole((N, 2 * N)),
            whole((2 * N, 2 * N)),
        ],
        out_specs=[pl.BlockSpec(memory_space=pl.ANY)] * 6,
        out_shape=[jax.ShapeDtypeStruct((half, nx, HALF, 2 * N), jnp.bfloat16)] * 2
        + [jax.ShapeDtypeStruct((ny, HB, N, N), jnp.bfloat16)] * 4,
        scratch_shapes=[
            pltpu.VMEM(sections.shape[1:], jnp.float32),
            pltpu.VMEM((nx * HALF, 4 * N), jnp.bfloat16),
            pltpu.VMEM((ny, nx, HALF, 2 * N), jnp.bfloat16),
            pltpu.VMEM((ny, 4, HB, N, N), jnp.bfloat16),
            pltpu.SemaphoreType.DMA((ny,)),
            pltpu.SemaphoreType.DMA((ny + 4,)),
        ],
        compiler_params=pltpu.CompilerParams(vmem_limit_bytes=VMEM),
        cost_estimate=pl.CostEstimate(flops=4_000_000_000, bytes_accessed=14 * MIB, transcendentals=0),
        name="forward",
    )(sections, rows2, cols.astype(jnp.bfloat16))


def times_conj(a, b, sign):
    ar, ai, br, bi = a[:, :N], a[:, N:], b[:, :N], b[:, N:]
    real = ar * br + ai * bi
    imag = ai * br - ar * bi if sign > 0 else ar * bi - ai * br
    return jnp.concatenate([real, imag], axis=1).astype(jnp.bfloat16)


def flow_kernel(sign, own_hbm, other_hbm, cols_ref, back_cols_ref, back_rows_ref, flow_ref, sums, moments, product_ref, own_all, other_all, sems):
    y = pl.program_id(0)
    ny, patches = own_all.shape[:2]
    fetch = lambda row: [
        pltpu.make_async_copy(source.at[row], target.at[row], sems.at[row, i])
        for i, (source, target) in enumerate(((own_hbm, own_all), (other_hbm, other_all)))
    ]
    ahead(fetch, ny, DEPTH)
    own_ref = own_all.at[pl.ds(y, 1)]
    other_ref = other_all.at[pl.ds(y, 1)]
    cols = cols_ref[...]
    back_cols = back_cols_ref[...]
    back_rows = back_rows_ref[...]
    own = own_ref[0]
    other = other_ref[0]
    lines = jnp.concatenate(
        [r[:, 0, :].astype(jnp.float32) for r in (own, other)], axis=0
    ).astype(jnp.bfloat16)
    edge = jnp.concatenate([lines[:, :N], lines[:, N:]], axis=0)
    edge = dot(edge, cols[:N])
    quarter = edge.reshape(4, patches, 2 * N)
    low = times_conj(quarter[0], quarter[1], sign)
    high = times_conj(quarter[2], quarter[3], sign)
    sides = dot(jnp.concatenate([low, high], axis=0), back_cols[:, :N])
    shift_rows = lax.broadcasted_iota(jnp.int32, (N, N), 0)
    offset_rows = (((shift_rows + HALF) % N) - HALF).astype(jnp.float32)
    offset_rows = jnp.concatenate([offset_rows, offset_rows], axis=1)
    step = 4
    for first in range(0, patches, step):
        a = own_ref[0, first : first + step].reshape(step * HALF, 2 * N).astype(jnp.float32)
        b = other_ref[0, first : first + step].reshape(step * HALF, 2 * N).astype(jnp.float32)
        product_ref[first * HALF : (first + step) * HALF, :] = times_conj(a, b, sign)
    for first in range(0, patches, step):
        back = dot(product_ref[first * HALF : (first + step) * HALF, :], back_cols)
        halves = []
        for p in range(first, first + step):
            here = back[(p - first) * HALF : (p - first + 1) * HALF]
            parts = []
            for i, side in enumerate((p, patches + p)):
                part = here[:, i * N : (i + 1) * N]
                top = jnp.where(first_row((16, N)), sides[side : side + 1], part[:16])
                parts += [top.astype(jnp.bfloat16), part[16:].astype(jnp.bfloat16)]
            halves.append(jnp.concatenate(parts, axis=0))
        for i in range(0, step, 2):
            corr = dot(back_rows, jnp.concatenate(halves[i : i + 2], axis=1))
            power = corr * corr
            total = power.sum(0, keepdims=True)
            moment = (power * offset_rows).sum(0, keepdims=True)
            for side in range(2):
                p = first + i + side
                sums[p : p + 1, :] = total[:, side * N : (side + 1) * N]
                moments[p : p + 1, :] = moment[:, side * N : (side + 1) * N]
    lane = lax.broadcasted_iota(jnp.int32, (8, N), 1)
    row = lax.broadcasted_iota(jnp.int32, (8, N), 0)
    offset_cols = (((lane + HALF) % N) - HALF).astype(jnp.float32)
    reduce_by = jnp.where(row == 0, 1.0, jnp.where(row == 1, offset_cols, 0.0))
    over_lanes = lambda m: lax.dot_general(
        reduce_by, m, (((1,), (1,)), ((), ())),
        precision=lax.Precision.HIGHEST, preferred_element_type=jnp.float32,
    )
    by_sums = over_lanes(sums[...])
    by_moments = over_lanes(moments[...])
    total = by_sums[0:1] + EPS
    flow_ref[0, pl.ds(y, 1), :] = by_moments[0:1] / total
    flow_ref[1, pl.ds(y, 1), :] = by_sums[1:2] / total


def flow_of(own, other, sign, cols, back_cols, back_rows):
    ny, nx = other.shape[:2]
    whole = lambda shape: pl.BlockSpec(shape, lambda y: (0,) * len(shape))
    return pl.pallas_call(
        functools.partial(flow_kernel, sign),
        grid=(ny,),
        in_specs=[
            pl.BlockSpec(memory_space=pl.ANY),
            pl.BlockSpec(memory_space=pl.ANY),
            whole((2 * N, 2 * N)),
            whole((2 * N, 2 * N)),
            whole((N, N)),
        ],
        out_specs=whole((2, ny, nx)),
        out_shape=jax.ShapeDtypeStruct((2, ny, nx), jnp.float32),
        scratch_shapes=[
            pltpu.VMEM((nx, N), jnp.float32),
            pltpu.VMEM((nx, N), jnp.float32),
            pltpu.VMEM((nx * HALF, 2 * N), jnp.bfloat16),
            pltpu.VMEM(own.shape, own.dtype),
            pltpu.VMEM(own.shape, own.dtype),
            pltpu.SemaphoreType.DMA((ny, 2)),
        ],
        compiler_params=pltpu.CompilerParams(vmem_limit_bytes=VMEM),
        cost_estimate=pl.CostEstimate(flops=2_000_000_000, bytes_accessed=8 * MIB, transcendentals=0),
        name="flow",
    )(own, other, *(t.astype(jnp.bfloat16) for t in (cols, back_cols, back_rows)))


def slots_kernel(rows_ref, shifts_ref, count_ref, weight_ref, target_ref, share_ref):
    ny, _, nx = rows_ref.shape[1:]
    live = [k < count_ref[0] for k in range(K)]
    weights = [jnp.where(live[k], weight_ref[0, :, k, :], 0.0) for k in range(K)]
    total = weights[0] + weights[1] + weights[2] + weights[3]
    share = [(w / total).astype(jnp.bfloat16).astype(jnp.float32) for w in weights]
    column = lax.broadcasted_iota(jnp.int32, (ny, nx), 1) + HB
    target = [rows_ref[0, :, k, :] * ROW + column + shifts_ref[0, :, k, :] for k in range(K)]
    rest = N - K * nx
    share_ref[...] = jnp.concatenate(share + [jnp.zeros((ny, rest), jnp.float32)], axis=1)
    target_ref[...] = jnp.concatenate(target + [jnp.zeros((ny, rest), jnp.int32)], axis=1)


def slots_of(box_row, box_shift, box_count, blend_weight):
    ny = box_row.shape[1]
    slots_first = lambda x: jnp.transpose(x, (0, 1, 3, 2))
    return pl.pallas_call(
        slots_kernel,
        out_shape=[
            jax.ShapeDtypeStruct((ny, N), jnp.int32),
            jax.ShapeDtypeStruct((ny, N), jnp.float32),
        ],
        compiler_params=pltpu.CompilerParams(vmem_limit_bytes=VMEM),
        name="slots",
    )(slots_first(box_row), slots_first(box_shift), box_count, slots_first(blend_weight))


def blend_cell(y, x, nx, target_ref, share_ref, window):
    total = None
    for k in range(K):
        spot = target_ref[y, k * nx + x]
        piece = window[spot // ROW, spot % ROW].astype(jnp.float32) * share_ref[y, k * nx + x]
        total = piece if total is None else total + piece
    return total


def blend_kernel(target_ref, share_ref, x_hbm, out_hbm, window, staging, mid, in_sems, out_sems):
    y = pl.program_id(0)
    ny, nx = staging.shape[:2]

    @pl.when(y == 0)
    def _():
        copies = [
            pltpu.make_async_copy(x_hbm.at[0, row], staging.at[row], in_sems.at[row]) for row in range(ny)
        ]
        for copy in copies:
            copy.start()
        for row, copy in enumerate(copies):
            copy.wait()
            for x in range(nx):
                window[row, HB + x] = staging[row, x].astype(jnp.bfloat16)

    for x in range(HB, nx - HB):
        mid[y, x - HB] = blend_cell(y, x, nx, target_ref, share_ref, window)
    store = lambda row: pltpu.make_async_copy(mid.at[row], out_hbm.at[row], out_sems.at[row])
    store(y).start()
    wait_all([store(row) for row in range(ny)])


def blend(target, share, sections):
    _, ny, nx, _, _ = sections.shape
    mid = (ny, nx - 2 * HB, N, N)
    return pl.pallas_call(
        blend_kernel,
        grid=(ny,),
        in_specs=[pl.BlockSpec(memory_space=pltpu.SMEM)] * 2 + [pl.BlockSpec(memory_space=pl.ANY)],
        out_specs=pl.BlockSpec(memory_space=pl.ANY),
        out_shape=jax.ShapeDtypeStruct(mid, jnp.float32),
        scratch_shapes=[
            pltpu.VMEM((ny, nx + 2 * HB, N, N), jnp.bfloat16),
            pltpu.VMEM(sections.shape[1:], jnp.float32),
            pltpu.VMEM(mid, jnp.float32),
            pltpu.SemaphoreType.DMA((ny,)),
            pltpu.SemaphoreType.DMA((ny,)),
        ],
        compiler_params=pltpu.CompilerParams(vmem_limit_bytes=VMEM),
        cost_estimate=pl.CostEstimate(flops=20_000_000, bytes_accessed=14 * MIB, transcendentals=0),
        name="blend",
    )(target, share, sections)


def relax_kernel(low_ref, high_ref, mask_ref, left_ref, right_ref, out_ref):
    ny, nx = mask_ref.shape[1:]
    rest = jnp.zeros((ny, N - nx - 2 * STEPS), jnp.float32)

    def across(left, own, right):
        return jnp.concatenate([left[:, nx - STEPS :], own, right[:, :STEPS], rest], axis=1)

    known = across(left_ref[2], mask_ref[0].astype(jnp.float32) + 1.0, right_ref[2])
    valid = jnp.where(known > 0.5, 1.0, 0.0)
    trust = jnp.where(known > 1.5, 1.0, 0.0)
    row = lax.broadcasted_iota(jnp.int32, trust.shape, 0)
    for component in range(2):
        own = jnp.concatenate([low_ref[component], high_ref[component]], axis=0)
        flow = across(left_ref[component], own, right_ref[component])
        field = trust * flow
        for _ in range(STEPS):
            below = jnp.where(row == 0, 0.0, pltpu.roll(field, 1, 0))
            above = jnp.where(row == ny - 1, 0.0, pltpu.roll(field, ny - 1, 0))
            beside = pltpu.roll(field, 1, 1) + pltpu.roll(field, N - 1, 1)
            lap = above + below + beside - 4.0 * field
            field = (field + SPRING * (lap + trust * (flow - field))) * valid
        out_ref[0, component] = field[:, STEPS : STEPS + nx]


def relax(low, high, mask, left, right):
    return pl.pallas_call(
        relax_kernel,
        out_shape=jax.ShapeDtypeStruct((1, 2) + mask.shape[1:], jnp.float32),
        compiler_params=pltpu.CompilerParams(vmem_limit_bytes=VMEM),
        name="relax",
    )(low, high, mask, left, right)


def warp_kernel(field_ref, target_ref, share_ref, mid_hbm, *refs):
    *strips, out_hbm, window, padded, out, in_sems, out_sems = refs
    y = pl.program_id(0)
    ny, nx = out.shape[:2]
    places = (0, HB, 2 * HB, nx - HB, nx, nx + HB)
    strip_copies = [
        pltpu.make_async_copy(ref, window.at[:, into : into + HB], in_sems.at[ny + i])
        for i, (ref, into) in enumerate(zip(strips, places, strict=True))
    ]
    fetch = lambda row: [
        pltpu.make_async_copy(
            mid_hbm.at[row], padded.at[row, HB : nx - HB, PAD : PAD + N], in_sems.at[row]
        )
    ]

    @pl.when(y == 0)
    def _():
        for copy in strip_copies:
            copy.start()

    ahead(fetch, ny, DEPTH)
    padded[y, :, :PAD] = jnp.zeros((nx, PAD, N), jnp.float32)
    padded[y, :, PAD + N :] = jnp.zeros((nx, PAD, N), jnp.float32)

    @pl.when(y == 0)
    def _():
        for copy in strip_copies:
            copy.wait()

    for x in (*range(HB), *range(nx - HB, nx)):
        padded[y, x, PAD : PAD + N] = blend_cell(y, x, nx, target_ref, share_ref, window)
    apart = lax.broadcasted_iota(jnp.int32, (N, N), 0) - lax.broadcasted_iota(jnp.int32, (N, N), 1)
    apart = apart.astype(jnp.float32)
    for x in range(nx):
        shift = field_ref[0, 0, y, x]
        down = jnp.clip((shift + 256.0).astype(jnp.int32) - 256, 4 - PAD, PAD - 6)
        part = shift - down.astype(jnp.float32)
        upper = padded[y, x, pl.ds(PAD + down, N), :]
        lower = padded[y, x, pl.ds(PAD + 1 + down, N), :]
        image = upper + part * (lower - upper)
        hat = jnp.maximum(0.0, 1.0 - jnp.abs(apart - field_ref[0, 1, y, x])).astype(jnp.bfloat16)
        warped = dot(jnp.concatenate(split(image), axis=1), jnp.concatenate([hat, hat], axis=0))
        out[y, x] = warped.astype(jnp.bfloat16)
    store = lambda row: pltpu.make_async_copy(out.at[row], out_hbm.at[0, row], out_sems.at[row])
    store(y).start()
    wait_all([store(row) for row in range(ny)])


def warp(field, target, share, mid, strips):
    ny, nx = field.shape[2:]
    return pl.pallas_call(
        warp_kernel,
        grid=(ny,),
        in_specs=[pl.BlockSpec(memory_space=pltpu.SMEM)] * 3
        + [pl.BlockSpec(memory_space=pl.ANY)] * (1 + len(strips)),
        out_specs=pl.BlockSpec(memory_space=pl.ANY),
        out_shape=jax.ShapeDtypeStruct((1, ny, nx, N, N), jnp.bfloat16),
        scratch_shapes=[
            pltpu.VMEM((ny, nx + 2 * HB, N, N), jnp.bfloat16),
            pltpu.VMEM((ny, nx, 2 * PAD + N, N), jnp.float32),
            pltpu.VMEM((ny, nx, N, N), jnp.bfloat16),
            pltpu.SemaphoreType.DMA((ny + len(strips),)),
            pltpu.SemaphoreType.DMA((ny,)),
        ],
        compiler_params=pltpu.CompilerParams(vmem_limit_bytes=VMEM),
        cost_estimate=pl.CostEstimate(flops=20_000_000, bytes_accessed=12 * MIB, transcendentals=0),
        name="warp",
    )(field, target, share, mid, *strips)


def from_behind(x, axis, by):
    length = lax.axis_size(axis)
    pairs = [(i, i + by) for i in range(length) if 0 <= i + by < length]
    return lax.ppermute(x, axis, pairs)


def per_device(sections, node_mask, box_row, box_shift, box_count, blend_weight):
    ny, nx = sections.shape[1:3]
    rows, cols, back_cols, back_rows = tables()
    half = ny // 2
    spectra_low, spectra_high, left, after, before, right = forward(sections, rows, cols)
    from_next = from_behind(spectra_low, "sec", -1)
    from_last = from_behind(spectra_high, "sec", 1)
    low = from_behind(right, "tile", 1)
    high = from_behind(left, "tile", -1)
    target, share = slots_of(box_row, box_shift, box_count, blend_weight)
    mid = blend(target, share, sections)

    flow_low = flow_of(spectra_low, from_next, 1, cols, back_cols, back_rows)
    flow_high = flow_of(spectra_high, from_last, -1, cols, back_cols, back_rows)
    flow_high = from_behind(flow_high, "sec", -1)
    flow = jnp.concatenate([flow_low, flow_high], axis=1)
    flow = jnp.concatenate([flow, node_mask.astype(jnp.float32) + 1.0], axis=0)
    flow_left = from_behind(flow, "tile", 1)
    flow_right = from_behind(flow, "tile", -1)
    strips = (low, left, after, before, right, high)
    field = relax(flow_low, flow_high, node_mask, flow_left, flow_right)
    return (warp(field, target, share, mid, strips), field)


def solution(mesh):
    return jax.shard_map(
        per_device,
        mesh=mesh,
        in_specs=(
            P("sec", None, "tile", None, None),
            P("sec", None, "tile"),
            P("sec", None, "tile", None),
            P("sec", None, "tile", None),
            P("sec", None, "tile"),
            P("sec", None, "tile", None),
        ),
        out_specs=(P("sec", None, "tile", None, None), P("sec", None, None, "tile")),
        check_vma=False,
    )
```

```python
import functools

import jax
import jax.numpy as jnp
import numpy as np
from jax import lax
from jax.experimental import pallas as pl
from jax.experimental.pallas import tpu as pltpu
from jax.sharding import PartitionSpec as P

K = 4
HB = 2
STEPS = 3
N = 128
HALF = N // 2
PAD = 72
ROW = 32
DEPTH = 3
SPRING = 0.2
EPS = 1e-06
MIB = 1024 * 1024
VMEM = 60 * MIB


def split(x):
    high = x.astype(jnp.bfloat16)
    return high, (x - high.astype(jnp.float32)).astype(jnp.bfloat16)


def tables():
    grid = np.arange(N)[:, None] * np.arange(N)[None, :] % N
    cosine = np.cos(2.0 * np.pi * grid / N)
    sine = np.sin(2.0 * np.pi * grid / N)
    rows = np.concatenate([cosine[:HALF], sine[:HALF]])
    rows[HALF] = cosine[HALF]
    cols = np.block([[cosine, -sine], [-sine, -cosine]])
    back_cols = np.block([[cosine, sine], [-sine, cosine]]) / N
    weight = np.where(np.arange(HALF) == 0, 1.0, 2.0)
    back_rows = np.concatenate([cosine[:, :HALF] * weight, -2.0 * sine[:, :HALF]], axis=1) / N
    back_rows[:, HALF] = cosine[:, HALF] / N
    return [jnp.asarray(t, jnp.float32) for t in (rows, cols, back_cols, back_rows)]


def first_row(shape):
    return lax.broadcasted_iota(jnp.int32, shape, len(shape) - 2) == 0


def dot(a, b):
    return jnp.dot(a, b, preferred_element_type=jnp.float32)


def ahead(fetch, rows, depth):
    y = pl.program_id(0)

    @pl.when(y == 0)
    def _():
        for row in range(depth):
            for copy in fetch(row):
                copy.start()

    @pl.when(y + depth < rows)
    def _():
        for copy in fetch(y + depth):
            copy.start()

    for copy in fetch(y):
        copy.wait()


def wait_all(copies):
    @pl.when(pl.program_id(0) == pl.num_programs(0) - 1)
    def _():
        for copy in copies:
            copy.wait()


def forward_kernel(x_hbm, rows_ref, cols_ref, low_hbm, high_hbm, x_ref, lines_ref, ends_ref, spec, in_sems, out_sems):
    y = pl.program_id(0)
    ny, patches = x_ref.shape[:2]
    half = ny // 2
    fetch = lambda row: [pltpu.make_async_copy(x_hbm.at[0, row], x_ref.at[row], in_sems.at[row])]
    ahead(fetch, ny, DEPTH)

    rows2 = rows_ref[...]
    cols = cols_ref[...]
    cols2 = jnp.concatenate([cols, cols], axis=0)
    for pair in range(patches // 2):
        x = jnp.concatenate([x_ref[y, 2 * pair], x_ref[y, 2 * pair + 1]], axis=1)
        both = dot(rows2, jnp.concatenate(split(x), axis=0))
        for side in range(2):
            here = both[:, side * N : (side + 1) * N]
            p = 2 * pair + side
            ends_ref[p : p + 1, :N] = here[:1]
            ends_ref[p : p + 1, N:] = here[HALF : HALF + 1]
            lines = jnp.concatenate([here[:HALF], here[HALF:]], axis=1)
            high, low = split(lines)
            lines_ref[p * HALF : (p + 1) * HALF, : 2 * N] = high
            lines_ref[p * HALF : (p + 1) * HALF, 2 * N :] = low
    part, row = y // half, y % half
    step = 4
    for first in range(0, patches, step):
        lines = lines_ref[first * HALF : (first + step) * HALF, :]
        freq = dot(lines, cols2).reshape(step, HALF, 2 * N)
        spec[part, pl.ds(row * patches + first, step)] = freq.astype(jnp.bfloat16)
    last = half * patches
    ends = ends_ref[...].astype(jnp.bfloat16)
    spec[part, last, pl.ds(pl.multiple_of(row * patches, patches), patches), :] = ends

    def spectra_to(row):
        first = row % half * patches
        count = patches + (row % half == half - 1)
        return pltpu.make_async_copy(
            spec.at[row // half, pl.ds(first, count)],
            (low_hbm, high_hbm)[row // half].at[pl.ds(first, count)],
            out_sems.at[row],
        )

    for row in range(ny):
        pl.when(y == row)(spectra_to(row).start)
    wait_all([spectra_to(row) for row in range(ny)])


def forward(sections, rows, cols):
    _, ny, nx, _, _ = sections.shape
    half = ny // 2
    rows2 = jnp.concatenate([rows, rows], axis=1).astype(jnp.bfloat16)
    whole = lambda shape: pl.BlockSpec(shape, lambda y: (0,) * len(shape))
    spectra = (half * nx + 1, HALF, 2 * N)
    return pl.pallas_call(
        forward_kernel,
        grid=(ny,),
        in_specs=[
            pl.BlockSpec(memory_space=pl.ANY),
            whole((N, 2 * N)),
            whole((2 * N, 2 * N)),
        ],
        out_specs=[pl.BlockSpec(memory_space=pl.ANY)] * 2,
        out_shape=[jax.ShapeDtypeStruct(spectra, jnp.bfloat16)] * 2,
        scratch_shapes=[
            pltpu.VMEM(sections.shape[1:], jnp.float32),
            pltpu.VMEM((nx * HALF, 4 * N), jnp.bfloat16),
            pltpu.VMEM((nx, 2 * N), jnp.float32),
            pltpu.VMEM((2,) + spectra, jnp.bfloat16),
            pltpu.SemaphoreType.DMA((ny,)),
            pltpu.SemaphoreType.DMA((ny,)),
        ],
        compiler_params=pltpu.CompilerParams(vmem_limit_bytes=VMEM),
        cost_estimate=pl.CostEstimate(flops=4_000_000_000, bytes_accessed=12 * MIB, transcendentals=0),
        name="forward",
    )(sections, rows2, cols.astype(jnp.bfloat16))


def times_conj(a, b, sign):
    ar, ai, br, bi = a[:, :N], a[:, N:], b[:, :N], b[:, N:]
    real = ar * br + ai * bi
    imag = ai * br - ar * bi if sign > 0 else ar * bi - ai * br
    return jnp.concatenate([real, imag], axis=1).astype(jnp.bfloat16)


def flow_kernel(sign, own_hbm, other_hbm, cols_ref, back_cols_ref, back_rows_ref, flow_ref, own, other, sides, sums, moments, sems):
    y = pl.program_id(0)
    ny, patches = sums.shape[:2]
    last = ny * patches
    pairs = ((own_hbm, own), (other_hbm, other))
    fetch = lambda row: [
        pltpu.make_async_copy(
            source.at[pl.ds(row * patches, patches)], target.at[pl.ds(row * patches, patches)], sems.at[row, i]
        )
        for i, (source, target) in enumerate(pairs)
    ]
    ends = [
        pltpu.make_async_copy(source.at[last], target.at[last], sems.at[ny, i])
        for i, (source, target) in enumerate(pairs)
    ]

    @pl.when(y == 0)
    def _():
        for copy in ends:
            copy.start()

    ahead(fetch, ny, DEPTH)
    cols = cols_ref[...]
    back_cols = back_cols_ref[...]
    back_rows = back_rows_ref[...]

    @pl.when(y == 0)
    def _():
        for copy in ends:
            copy.wait()
        lines = jnp.concatenate([own[last], other[last]], axis=0)
        edge = dot(jnp.concatenate([lines[:, :N], lines[:, N:]], axis=0), cols[:N])
        quarter = edge.reshape(4, last, 2 * N)
        low = times_conj(quarter[0], quarter[1], sign)
        high = times_conj(quarter[2], quarter[3], sign)
        back = dot(jnp.concatenate([low, high], axis=0), back_cols[:, :N])
        sides[...] = back.reshape(sides.shape)

    shift_rows = lax.broadcasted_iota(jnp.int32, (N, N), 0)
    offset_rows = (((shift_rows + HALF) % N) - HALF).astype(jnp.float32)
    offset_rows = jnp.concatenate([offset_rows, offset_rows], axis=1)
    step = 4
    for first in range(0, patches, step):
        here = pl.ds(y * patches + first, step)
        a = own[here].reshape(step * HALF, 2 * N).astype(jnp.float32)
        b = other[here].reshape(step * HALF, 2 * N).astype(jnp.float32)
        back = dot(times_conj(a, b, sign), back_cols)
        halves = []
        for i in range(step):
            p = first + i
            parts = []
            for side in range(2):
                part = back[i * HALF : (i + 1) * HALF, side * N : (side + 1) * N]
                top = jnp.where(first_row((16, N)), sides[side, y, p : p + 1, :], part[:16])
                parts += [top.astype(jnp.bfloat16), part[16:].astype(jnp.bfloat16)]
            halves.append(jnp.concatenate(parts, axis=0))
        for i in range(0, step, 2):
            corr = dot(back_rows, jnp.concatenate(halves[i : i + 2], axis=1))
            power = corr * corr
            total = power.sum(0, keepdims=True)
            moment = (power * offset_rows).sum(0, keepdims=True)
            for side in range(2):
                p = first + i + side
                sums[y, p : p + 1, :] = total[:, side * N : (side + 1) * N]
                moments[y, p : p + 1, :] = moment[:, side * N : (side + 1) * N]

    @pl.when(y == ny - 1)
    def _():
        lane = lax.broadcasted_iota(jnp.int32, (8, N), 1)
        row = lax.broadcasted_iota(jnp.int32, (8, N), 0)
        offset_cols = (((lane + HALF) % N) - HALF).astype(jnp.float32)
        reduce_by = jnp.where(row == 0, 1.0, jnp.where(row == 1, offset_cols, 0.0))
        over_lanes = lambda m: lax.dot_general(
            reduce_by, m.reshape(last, N), (((1,), (1,)), ((), ())),
            precision=lax.Precision.HIGHEST, preferred_element_type=jnp.float32,
        )
        by_sums = over_lanes(sums[...])
        by_moments = over_lanes(moments[...])
        total = by_sums[0:1] + EPS
        along_rows = by_moments[0:1] / total
        along_cols = by_sums[1:2] / total
        for row in range(ny):
            flow_ref[0, row : row + 1, :] = along_rows[:, row * patches : (row + 1) * patches]
            flow_ref[1, row : row + 1, :] = along_cols[:, row * patches : (row + 1) * patches]


def flow_of(own, other, sign, ny, nx, cols, back_cols, back_rows):
    whole = lambda shape: pl.BlockSpec(shape, lambda y: (0,) * len(shape))
    return pl.pallas_call(
        functools.partial(flow_kernel, sign),
        grid=(ny,),
        in_specs=[
            pl.BlockSpec(memory_space=pl.ANY),
            pl.BlockSpec(memory_space=pl.ANY),
            whole((2 * N, 2 * N)),
            whole((2 * N, 2 * N)),
            whole((N, N)),
        ],
        out_specs=whole((2, ny, nx)),
        out_shape=jax.ShapeDtypeStruct((2, ny, nx), jnp.float32),
        scratch_shapes=[
            pltpu.VMEM(own.shape, own.dtype),
            pltpu.VMEM(own.shape, own.dtype),
            pltpu.VMEM((2, ny, nx, N), jnp.float32),
            pltpu.VMEM((ny, nx, N), jnp.float32),
            pltpu.VMEM((ny, nx, N), jnp.float32),
            pltpu.SemaphoreType.DMA((ny + 1, 2)),
        ],
        compiler_params=pltpu.CompilerParams(vmem_limit_bytes=VMEM),
        cost_estimate=pl.CostEstimate(flops=2_000_000_000, bytes_accessed=4 * MIB, transcendentals=0),
        name="flow",
    )(own, other, *(t.astype(jnp.bfloat16) for t in (cols, back_cols, back_rows)))


def slots_kernel(tile_ref, rows_ref, shifts_ref, count_ref, weight_ref, target_ref, share_ref):
    ny, _, nx = rows_ref.shape[1:]
    tile, tiles = tile_ref[0], tile_ref[1]
    live = [k < count_ref[0] for k in range(K)]
    weights = [jnp.where(live[k], weight_ref[0, :, k, :], 0.0) for k in range(K)]
    total = weights[0] + weights[1] + weights[2] + weights[3]
    share = [(w / total).astype(jnp.bfloat16).astype(jnp.float32) for w in weights]
    columns = [lax.broadcasted_iota(jnp.int32, (ny, nx), 1) + shifts_ref[0, :, k, :] for k in range(K)]
    rows = [rows_ref[0, :, k, :] * ROW for k in range(K)]
    low = [c < 0 for c in columns]
    high = [c >= nx for c in columns]
    first, last = tile == 0, tile == tiles - 1
    inside = [jnp.where(l | h, 0.0, s) for l, h, s in zip(low, high, share, strict=True)]
    share_low = [jnp.where(first, 0.0, jnp.where(l, s, 0.0)) for l, s in zip(low, share, strict=True)]
    share_high = [jnp.where(last, 0.0, jnp.where(h, s, 0.0)) for h, s in zip(high, share, strict=True)]
    beyond = [l + h for l, h in zip(share_low, share_high, strict=True)]
    share_ref[...] = jnp.concatenate(inside + beyond, axis=1)
    target = [r + jnp.where(l | h, 0, c) for r, c, l, h in zip(rows, columns, low, high, strict=True)]
    away = [
        r + jnp.where(l, c + HB, jnp.where(h, c - nx + HB, 0))
        for r, c, l, h in zip(rows, columns, low, high, strict=True)
    ]
    target_ref[...] = jnp.concatenate(target + away, axis=1)


def slots_of(tile, box_row, box_shift, box_count, blend_weight):
    ny = box_row.shape[1]
    slots_first = lambda x: jnp.transpose(x, (0, 1, 3, 2))
    return pl.pallas_call(
        slots_kernel,
        in_specs=[pl.BlockSpec(memory_space=pltpu.SMEM)] + [pl.BlockSpec(memory_space=pltpu.VMEM)] * 4,
        out_shape=[
            jax.ShapeDtypeStruct((ny, N), jnp.int32),
            jax.ShapeDtypeStruct((ny, N), jnp.float32),
        ],
        compiler_params=pltpu.CompilerParams(vmem_limit_bytes=VMEM),
        name="slots",
    )(tile, slots_first(box_row), slots_first(box_shift), box_count, slots_first(blend_weight))


def blend_cell(y, first, nx, target_ref, share_ref, window):
    total = None
    for k in range(K):
        spot = target_ref[y, first + k * nx]
        piece = window[spot // ROW, spot % ROW].astype(jnp.float32) * share_ref[y, first + k * nx]
        total = piece if total is None else total + piece
    return total


def blend_kernel(target_ref, share_ref, x_hbm, out_hbm, window, staging, out, in_sems, out_sems):
    y = pl.program_id(0)
    ny, nx = staging.shape[:2]

    @pl.when(y == 0)
    def _():
        copies = [
            pltpu.make_async_copy(x_hbm.at[0, row], staging.at[row], in_sems.at[row]) for row in range(ny)
        ]
        for copy in copies:
            copy.start()
        for row, copy in enumerate(copies):
            copy.wait()
            for x in range(nx):
                window[row, x] = staging[row, x].astype(jnp.bfloat16)

    for x in range(nx):
        out[y, x] = blend_cell(y, x, nx, target_ref, share_ref, window)
    store = lambda row: pltpu.make_async_copy(out.at[row], out_hbm.at[row], out_sems.at[row])
    store(y).start()
    wait_all([store(row) for row in range(ny)])


def blend(target, share, sections):
    _, ny, nx, _, _ = sections.shape
    shape = sections.shape[1:]
    return pl.pallas_call(
        blend_kernel,
        grid=(ny,),
        in_specs=[pl.BlockSpec(memory_space=pltpu.SMEM)] * 2 + [pl.BlockSpec(memory_space=pl.ANY)],
        out_specs=pl.BlockSpec(memory_space=pl.ANY),
        out_shape=jax.ShapeDtypeStruct(shape, jnp.float32),
        scratch_shapes=[
            pltpu.VMEM(shape, jnp.bfloat16),
            pltpu.VMEM(shape, jnp.float32),
            pltpu.VMEM(shape, jnp.float32),
            pltpu.SemaphoreType.DMA((ny,)),
            pltpu.SemaphoreType.DMA((ny,)),
        ],
        compiler_params=pltpu.CompilerParams(vmem_limit_bytes=VMEM),
        cost_estimate=pl.CostEstimate(flops=20_000_000, bytes_accessed=16 * MIB, transcendentals=0),
        name="blend",
    )(target, share, sections)


def relax(low_ref, high_ref, mask_ref, left_ref, right_ref):
    ny, nx = mask_ref.shape[1:]
    rest = jnp.zeros((ny, N - nx - 2 * STEPS), jnp.float32)

    def across(left, own, right):
        return jnp.concatenate([left[:, nx - STEPS :], own, right[:, :STEPS], rest], axis=1)

    known = across(left_ref[2], mask_ref[0].astype(jnp.float32) + 1.0, right_ref[2])
    valid = jnp.where(known > 0.5, 1.0, 0.0)
    trust = jnp.where(known > 1.5, 1.0, 0.0)
    row = lax.broadcasted_iota(jnp.int32, trust.shape, 0)
    fields = []
    for component in range(2):
        own = jnp.concatenate([low_ref[component], high_ref[component]], axis=0)
        flow = across(left_ref[component], own, right_ref[component])
        field = trust * flow
        for _ in range(STEPS):
            below = jnp.where(row == 0, 0.0, pltpu.roll(field, 1, 0))
            above = jnp.where(row == ny - 1, 0.0, pltpu.roll(field, ny - 1, 0))
            beside = pltpu.roll(field, 1, 1) + pltpu.roll(field, N - 1, 1)
            lap = above + below + beside - 4.0 * field
            field = (field + SPRING * (lap + trust * (flow - field))) * valid
        fields.append(field)
    return fields


def warp_kernel(tile_ref, target_ref, share_ref, *refs):
    *flows, blended_hbm, on_hbm, off_hbm, out_hbm, field_ref, window, padded, out, wide, field, in_sems, out_sems = refs
    y = pl.program_id(0)
    ny, nx = out.shape[:2]
    even = tile_ref[0] % 2 == 0
    halos = {
        True: ((on_hbm, HB), (off_hbm.at[0], 0)),
        False: ((on_hbm, 0), (off_hbm.at[1], HB)),
    }
    halo_copies = {
        side: [
            pltpu.make_async_copy(ref, window.at[:, into : into + HB], in_sems.at[ny + i])
            for i, (ref, into) in enumerate(places)
        ]
        for side, places in halos.items()
    }
    fetch = lambda row: [
        pltpu.make_async_copy(blended_hbm.at[row], padded.at[row, :, PAD : PAD + N], in_sems.at[row])
    ]

    @pl.when((y == 0) & even)
    def _():
        for copy in halo_copies[True]:
            copy.start()

    @pl.when((y == 0) & jnp.logical_not(even))
    def _():
        for copy in halo_copies[False]:
            copy.start()

    padded[y, :, :PAD] = jnp.zeros((nx, PAD, N), jnp.float32)
    padded[y, :, PAD + N :] = jnp.zeros((nx, PAD, N), jnp.float32)

    @pl.when(y == 0)
    def _():
        for component, values in enumerate(relax(*flows)):
            wide[component] = values
            field_ref[0, component] = values[:, STEPS : STEPS + nx]
        scalars = pltpu.make_async_copy(wide, field, in_sems.at[ny + 2])
        scalars.start()
        scalars.wait()
        for copy in halo_copies[True]:
            copy.wait()

    ahead(fetch, ny, DEPTH)
    for x in (*range(HB), *range(nx - HB, nx)):
        more = blend_cell(y, K * nx + x, nx, target_ref, share_ref, window)
        padded[y, x, PAD : PAD + N] += more
    apart = lax.broadcasted_iota(jnp.int32, (N, N), 0) - lax.broadcasted_iota(jnp.int32, (N, N), 1)
    apart = apart.astype(jnp.float32)
    for x in range(nx):
        shift = field[0, y, STEPS + x]
        down = jnp.clip((shift + 256.0).astype(jnp.int32) - 256, 4 - PAD, PAD - 6)
        part = shift - down.astype(jnp.float32)
        upper = padded[y, x, pl.ds(PAD + down, N), :]
        lower = padded[y, x, pl.ds(PAD + 1 + down, N), :]
        image = upper + part * (lower - upper)
        hat = jnp.maximum(0.0, 1.0 - jnp.abs(apart - field[1, y, STEPS + x])).astype(jnp.bfloat16)
        warped = dot(jnp.concatenate(split(image), axis=1), jnp.concatenate([hat, hat], axis=0))
        out[y, x] = warped.astype(jnp.bfloat16)
    store = lambda row: pltpu.make_async_copy(out.at[row], out_hbm.at[0, row], out_sems.at[row])
    store(y).start()
    wait_all([store(row) for row in range(ny)])


def warp(tile, target, share, flows, blended, on, off):
    ny, nx = blended.shape[:2]
    whole = lambda shape: pl.BlockSpec(shape, lambda y: (0,) * len(shape))
    return pl.pallas_call(
        warp_kernel,
        grid=(ny,),
        in_specs=[pl.BlockSpec(memory_space=pltpu.SMEM)] * 3
        + [whole(x.shape) for x in flows]
        + [pl.BlockSpec(memory_space=pl.ANY)] * 3,
        out_specs=[pl.BlockSpec(memory_space=pl.ANY), whole((1, 2, ny, nx))],
        out_shape=[
            jax.ShapeDtypeStruct((1, ny, nx, N, N), jnp.bfloat16),
            jax.ShapeDtypeStruct((1, 2, ny, nx), jnp.float32),
        ],
        scratch_shapes=[
            pltpu.VMEM((ny, 2 * HB, N, N), jnp.bfloat16),
            pltpu.VMEM((ny, nx, 2 * PAD + N, N), jnp.float32),
            pltpu.VMEM((ny, nx, N, N), jnp.bfloat16),
            pltpu.VMEM((2, ny, N), jnp.float32),
            pltpu.SMEM((2, ny, N), jnp.float32),
            pltpu.SemaphoreType.DMA((ny + 3,)),
            pltpu.SemaphoreType.DMA((ny,)),
        ],
        compiler_params=pltpu.CompilerParams(vmem_limit_bytes=VMEM),
        cost_estimate=pl.CostEstimate(flops=20_000_000, bytes_accessed=12 * MIB, transcendentals=0),
        name="warp",
    )(tile, target, share, *flows, blended, on, off)


def from_behind(x, axis, by):
    length = lax.axis_size(axis)
    pairs = [(i, i + by) for i in range(length) if 0 <= i + by < length]
    return lax.ppermute(x, axis, pairs)


def swapped(x):
    pairs = [(i, i ^ 1) for i in range(lax.axis_size("tile"))]
    return lax.ppermute(x, "tile", pairs)


def gathered_across(x):
    tiles = lax.axis_size("tile")
    groups = [[i, (i + 1) % tiles] for i in range(1, tiles, 2)]
    return lax.all_gather(x, "tile", axis_index_groups=groups)


def per_device(sections, node_mask, box_row, box_shift, box_count, blend_weight):
    ny, nx = sections.shape[1:3]
    rows, cols, back_cols, back_rows = tables()
    half = ny // 2
    index = lax.axis_index("tile")
    odd = index % 2
    tile = jnp.stack([index, lax.axis_size("tile")]).astype(jnp.int32)

    def edge(high):
        strip = lax.dynamic_slice_in_dim(sections[0], high * (nx - HB), HB, axis=1)
        return strip.astype(jnp.bfloat16)

    edge_off, edge_on = edge(odd), edge(1 - odd)
    edge_off, edge_on, sections = lax.optimization_barrier((edge_off, edge_on, sections))
    off = gathered_across(edge_off)
    on = swapped(edge_on)

    spectra_low, spectra_high = forward(sections, rows, cols)
    from_last = from_behind(spectra_high, "sec", 1)
    from_next = from_behind(spectra_low, "sec", -1)
    target, share = slots_of(tile, box_row, box_shift, box_count, blend_weight)
    blended = blend(target, share, sections)
    from_last, blended = lax.optimization_barrier((from_last, blended))

    flow_high = flow_of(spectra_high, from_last, -1, half, nx, cols, back_cols, back_rows)
    flow_high = from_behind(flow_high, "sec", -1)
    flow_low = flow_of(spectra_low, from_next, 1, half, nx, cols, back_cols, back_rows)
    flow = jnp.concatenate([flow_low, flow_high], axis=1)
    flow = jnp.concatenate([flow, node_mask.astype(jnp.float32) + 1.0], axis=0)
    flow_left = from_behind(flow, "tile", 1)
    flow_right = from_behind(flow, "tile", -1)
    flows = (flow_low, flow_high, node_mask, flow_left, flow_right)
    return tuple(warp(tile, target, share, flows, blended, on, off))


def solution(mesh):
    return jax.shard_map(
        per_device,
        mesh=mesh,
        in_specs=(
            P("sec", None, "tile", None, None),
            P("sec", None, "tile"),
            P("sec", None, "tile", None),
            P("sec", None, "tile", None),
            P("sec", None, "tile"),
            P("sec", None, "tile", None),
        ),
        out_specs=(P("sec", None, "tile", None, None), P("sec", None, None, "tile")),
        check_vma=False,
    )
```

```python
import functools

import jax
import jax.numpy as jnp
import numpy as np
from jax import lax
from jax.experimental import pallas as pl
from jax.experimental.pallas import tpu as pltpu
from jax.sharding import PartitionSpec as P

K = 4
HB = 2
STEPS = 3
N = 128
HALF = N // 2
PAD = 72
ROW = 32
DEPTH = 3
SPRING = 0.2
EPS = 1e-06
MIB = 1024 * 1024


def split(x):
    high = x.astype(jnp.bfloat16)
    return high, (x - high.astype(jnp.float32)).astype(jnp.bfloat16)


def tables():
    grid = np.arange(N)[:, None] * np.arange(N)[None, :] % N
    cosine = np.cos(2.0 * np.pi * grid / N)
    sine = np.sin(2.0 * np.pi * grid / N)
    rows = np.concatenate([cosine[:HALF], sine[:HALF]])
    rows[HALF] = cosine[HALF]
    cols = np.block([[cosine, -sine], [-sine, -cosine]])
    back_cols = np.block([[cosine, sine], [-sine, cosine]]) / N
    weight = np.where(np.arange(HALF) == 0, 1.0, 2.0)
    back_rows = np.concatenate([cosine[:, :HALF] * weight, -2.0 * sine[:, :HALF]], axis=1) / N
    back_rows[:, HALF] = cosine[:, HALF] / N
    return [jnp.asarray(t, jnp.float32) for t in (rows, cols, back_cols, back_rows)]


def first_row(shape):
    return lax.broadcasted_iota(jnp.int32, shape, len(shape) - 2) == 0


def dot(a, b):
    return jnp.dot(a, b, preferred_element_type=jnp.float32)


def ahead(fetch, rows, depth):
    y = pl.program_id(0)

    @pl.when(y == 0)
    def _():
        for row in range(depth):
            for copy in fetch(row):
                copy.start()

    @pl.when(y + depth < rows)
    def _():
        for copy in fetch(y + depth):
            copy.start()

    for copy in fetch(y):
        copy.wait()


def in_hbm(x):
    return pltpu.with_memory_space_constraint(x, pltpu.HBM)


def in_vmem(x):
    return pltpu.with_memory_space_constraint(x, pltpu.VMEM)


def wait_all(copies):
    @pl.when(pl.program_id(0) == pl.num_programs(0) - 1)
    def _():
        for copy in copies:
            copy.wait()


def forward_kernel(tile_ref, x_hbm, rows_ref, cols_ref, low_ref, high_ref, on_ref, off_ref, x_ref, lines_ref, ends_ref, in_sems):
    y = pl.program_id(0)
    ny, patches = x_ref.shape[:2]
    half = ny // 2
    fetch = lambda row: [pltpu.make_async_copy(x_hbm.at[0, row], x_ref.at[row], in_sems.at[row])]
    ahead(fetch, ny, DEPTH)
    odd = tile_ref[0] % 2
    for i in range(HB):
        on_ref[y, i] = x_ref[y, (1 - odd) * (patches - HB) + i].astype(jnp.bfloat16)
        off_ref[y, i] = x_ref[y, odd * (patches - HB) + i].astype(jnp.bfloat16)

    rows2 = rows_ref[...]
    cols = cols_ref[...]
    cols2 = jnp.concatenate([cols, cols], axis=0)
    for pair in range(patches // 2):
        x = jnp.concatenate([x_ref[y, 2 * pair], x_ref[y, 2 * pair + 1]], axis=1)
        both = dot(rows2, jnp.concatenate(split(x), axis=0))
        for side in range(2):
            here = both[:, side * N : (side + 1) * N]
            p = 2 * pair + side
            ends_ref[p : p + 1, :N] = here[:1]
            ends_ref[p : p + 1, N:] = here[HALF : HALF + 1]
            lines = jnp.concatenate([here[:HALF], here[HALF:]], axis=1)
            high, low = split(lines)
            lines_ref[p * HALF : (p + 1) * HALF, : 2 * N] = high
            lines_ref[p * HALF : (p + 1) * HALF, 2 * N :] = low
    row = y % half
    last = half * patches
    ends = ends_ref[...].astype(jnp.bfloat16)
    step = 4

    def finish(spec_ref):
        for first in range(0, patches, step):
            lines = lines_ref[first * HALF : (first + step) * HALF, :]
            freq = dot(lines, cols2).reshape(step, HALF, 2 * N)
            spec_ref[pl.ds(row * patches + first, step)] = freq.astype(jnp.bfloat16)
        spec_ref[last, pl.ds(pl.multiple_of(row * patches, patches), patches), :] = ends

    pl.when(y < half)(lambda: finish(low_ref))
    pl.when(y >= half)(lambda: finish(high_ref))


def forward(tile, sections, rows, cols):
    _, ny, nx, _, _ = sections.shape
    half = ny // 2
    rows2 = jnp.concatenate([rows, rows], axis=1).astype(jnp.bfloat16)
    whole = lambda shape: pl.BlockSpec(shape, lambda y: (0,) * len(shape))
    spectra = (half * nx + 1, HALF, 2 * N)
    return pl.pallas_call(
        forward_kernel,
        grid=(ny,),
        in_specs=[
            pl.BlockSpec(memory_space=pltpu.SMEM),
            pl.BlockSpec(memory_space=pltpu.HBM),
            whole((N, 2 * N)),
            whole((2 * N, 2 * N)),
        ],
        out_specs=[pl.BlockSpec(memory_space=pltpu.VMEM)] * 4,
        out_shape=[pltpu.VMEM(spectra, jnp.bfloat16)] * 2 + [pltpu.VMEM((ny, HB, N, N), jnp.bfloat16)] * 2,
        scratch_shapes=[
            pltpu.VMEM(sections.shape[1:], jnp.float32),
            pltpu.VMEM((nx * HALF, 4 * N), jnp.bfloat16),
            pltpu.VMEM((nx, 2 * N), jnp.float32),
            pltpu.SemaphoreType.DMA((ny,)),
        ],
        compiler_params=pltpu.CompilerParams(vmem_limit_bytes=20 * MIB),
        cost_estimate=pl.CostEstimate(flops=4_000_000_000, bytes_accessed=12 * MIB, transcendentals=0),
        name="forward",
    )(tile, in_hbm(sections), rows2, cols.astype(jnp.bfloat16))


def times_conj(a, b, sign):
    ar, ai, br, bi = a[:, :N], a[:, N:], b[:, :N], b[:, N:]
    real = ar * br + ai * bi
    imag = ai * br - ar * bi if sign > 0 else ar * bi - ai * br
    return jnp.concatenate([real, imag], axis=1).astype(jnp.bfloat16)


def flow_kernel(sign, own, other, cols_ref, back_cols_ref, back_rows_ref, flow_ref, sides, sums, moments):
    y = pl.program_id(0)
    ny, patches = sums.shape[:2]
    last = ny * patches
    cols = cols_ref[...]
    back_cols = back_cols_ref[...]
    back_rows = back_rows_ref[...]

    @pl.when(y == 0)
    def _():
        lines = jnp.concatenate([own[last], other[last]], axis=0)
        edge = dot(jnp.concatenate([lines[:, :N], lines[:, N:]], axis=0), cols[:N])
        quarter = edge.reshape(4, last, 2 * N)
        low = times_conj(quarter[0], quarter[1], sign)
        high = times_conj(quarter[2], quarter[3], sign)
        back = dot(jnp.concatenate([low, high], axis=0), back_cols[:, :N])
        sides[...] = back.reshape(sides.shape)

    shift_rows = lax.broadcasted_iota(jnp.int32, (N, N), 0)
    offset_rows = (((shift_rows + HALF) % N) - HALF).astype(jnp.float32)
    offset_rows = jnp.concatenate([offset_rows, offset_rows], axis=1)
    step = 4
    for first in range(0, patches, step):
        here = pl.ds(y * patches + first, step)
        a = own[here].reshape(step * HALF, 2 * N).astype(jnp.float32)
        b = other[here].reshape(step * HALF, 2 * N).astype(jnp.float32)
        back = dot(times_conj(a, b, sign), back_cols)
        halves = []
        for i in range(step):
            p = first + i
            parts = []
            for side in range(2):
                part = back[i * HALF : (i + 1) * HALF, side * N : (side + 1) * N]
                top = jnp.where(first_row((16, N)), sides[side, y, p : p + 1, :], part[:16])
                parts += [top.astype(jnp.bfloat16), part[16:].astype(jnp.bfloat16)]
            halves.append(jnp.concatenate(parts, axis=0))
        for i in range(0, step, 2):
            corr = dot(back_rows, jnp.concatenate(halves[i : i + 2], axis=1))
            power = corr * corr
            total = power.sum(0, keepdims=True)
            moment = (power * offset_rows).sum(0, keepdims=True)
            for side in range(2):
                p = first + i + side
                sums[y, p : p + 1, :] = total[:, side * N : (side + 1) * N]
                moments[y, p : p + 1, :] = moment[:, side * N : (side + 1) * N]

    @pl.when(y == ny - 1)
    def _():
        lane = lax.broadcasted_iota(jnp.int32, (8, N), 1)
        row = lax.broadcasted_iota(jnp.int32, (8, N), 0)
        offset_cols = (((lane + HALF) % N) - HALF).astype(jnp.float32)
        reduce_by = jnp.where(row == 0, 1.0, jnp.where(row == 1, offset_cols, 0.0))
        over_lanes = lambda m: lax.dot_general(
            reduce_by, m.reshape(last, N), (((1,), (1,)), ((), ())),
            precision=lax.Precision.HIGHEST, preferred_element_type=jnp.float32,
        )
        by_sums = over_lanes(sums[...])
        by_moments = over_lanes(moments[...])
        total = by_sums[0:1] + EPS
        along_rows = by_moments[0:1] / total
        along_cols = by_sums[1:2] / total
        for row in range(ny):
            flow_ref[0, row : row + 1, :] = along_rows[:, row * patches : (row + 1) * patches]
            flow_ref[1, row : row + 1, :] = along_cols[:, row * patches : (row + 1) * patches]


def flow_of(own, other, sign, ny, nx, cols, back_cols, back_rows):
    whole = lambda shape: pl.BlockSpec(shape, lambda y: (0,) * len(shape))
    return pl.pallas_call(
        functools.partial(flow_kernel, sign),
        grid=(ny,),
        in_specs=[
            pl.BlockSpec(memory_space=pltpu.VMEM),
            pl.BlockSpec(memory_space=pltpu.VMEM),
            whole((2 * N, 2 * N)),
            whole((2 * N, 2 * N)),
            whole((N, N)),
        ],
        out_specs=whole((2, ny, nx)),
        out_shape=jax.ShapeDtypeStruct((2, ny, nx), jnp.float32),
        scratch_shapes=[
            pltpu.VMEM((2, ny, nx, N), jnp.float32),
            pltpu.VMEM((ny, nx, N), jnp.float32),
            pltpu.VMEM((ny, nx, N), jnp.float32),
        ],
        compiler_params=pltpu.CompilerParams(vmem_limit_bytes=8 * MIB),
        cost_estimate=pl.CostEstimate(flops=2_000_000_000, bytes_accessed=4 * MIB, transcendentals=0),
        name="flow",
    )(in_vmem(own), in_vmem(other), *(t.astype(jnp.bfloat16) for t in (cols, back_cols, back_rows)))


def slots_kernel(tile_ref, rows_ref, shifts_ref, count_ref, weight_ref, target_ref, share_ref):
    ny, _, nx = rows_ref.shape[1:]
    tile, tiles = tile_ref[0], tile_ref[1]
    live = [k < count_ref[0] for k in range(K)]
    weights = [jnp.where(live[k], weight_ref[0, :, k, :], 0.0) for k in range(K)]
    total = weights[0] + weights[1] + weights[2] + weights[3]
    share = [(w / total).astype(jnp.bfloat16).astype(jnp.float32) for w in weights]
    columns = [lax.broadcasted_iota(jnp.int32, (ny, nx), 1) + shifts_ref[0, :, k, :] for k in range(K)]
    rows = [rows_ref[0, :, k, :] * ROW for k in range(K)]
    low = [c < 0 for c in columns]
    high = [c >= nx for c in columns]
    first, last = tile == 0, tile == tiles - 1
    inside = [jnp.where(l | h, 0.0, s) for l, h, s in zip(low, high, share, strict=True)]
    share_low = [jnp.where(first, 0.0, jnp.where(l, s, 0.0)) for l, s in zip(low, share, strict=True)]
    share_high = [jnp.where(last, 0.0, jnp.where(h, s, 0.0)) for h, s in zip(high, share, strict=True)]
    beyond = [l + h for l, h in zip(share_low, share_high, strict=True)]
    share_ref[...] = jnp.concatenate(inside + beyond, axis=1)
    target = [r + jnp.where(l | h, 0, c) for r, c, l, h in zip(rows, columns, low, high, strict=True)]
    away = [
        r + jnp.where(l, c + HB, jnp.where(h, c - nx + HB, 0))
        for r, c, l, h in zip(rows, columns, low, high, strict=True)
    ]
    target_ref[...] = jnp.concatenate(target + away, axis=1)


def slots_of(tile, box_row, box_shift, box_count, blend_weight):
    ny = box_row.shape[1]
    slots_first = lambda x: jnp.transpose(x, (0, 1, 3, 2))
    return pl.pallas_call(
        slots_kernel,
        in_specs=[pl.BlockSpec(memory_space=pltpu.SMEM)] + [pl.BlockSpec(memory_space=pltpu.VMEM)] * 4,
        out_shape=[
            jax.ShapeDtypeStruct((ny, N), jnp.int32),
            jax.ShapeDtypeStruct((ny, N), jnp.float32),
        ],
        compiler_params=pltpu.CompilerParams(vmem_limit_bytes=4 * MIB),
        name="slots",
    )(tile, slots_first(box_row), slots_first(box_shift), box_count, slots_first(blend_weight))


def blend_cell(y, first, nx, target_ref, share_ref, window):
    total = None
    for k in range(K):
        spot = target_ref[y, first + k * nx]
        piece = window[spot // ROW, spot % ROW].astype(jnp.float32) * share_ref[y, first + k * nx]
        total = piece if total is None else total + piece
    return total


def blend_kernel(target_ref, share_ref, x_hbm, out_ref, window, staging, in_sems):
    y = pl.program_id(0)
    ny, nx = staging.shape[:2]
    border = jnp.zeros((nx, PAD, N), jnp.float32)
    out_ref[y, :, :PAD] = border
    out_ref[y, :, PAD + N :] = border

    @pl.when(y == 0)
    def _():
        copies = [
            pltpu.make_async_copy(x_hbm.at[0, row], staging.at[row], in_sems.at[row]) for row in range(ny)
        ]
        for copy in copies:
            copy.start()
        for row, copy in enumerate(copies):
            copy.wait()
            for x in range(nx):
                window[row, x] = staging[row, x].astype(jnp.bfloat16)

    for x in range(nx):
        out_ref[y, x, PAD : PAD + N] = blend_cell(y, x, nx, target_ref, share_ref, window)


def blend(target, share, sections):
    _, ny, nx, _, _ = sections.shape
    shape = sections.shape[1:]
    return pl.pallas_call(
        blend_kernel,
        grid=(ny,),
        in_specs=[pl.BlockSpec(memory_space=pltpu.SMEM)] * 2 + [pl.BlockSpec(memory_space=pltpu.HBM)],
        out_specs=pl.BlockSpec(memory_space=pltpu.VMEM),
        out_shape=pltpu.VMEM((ny, nx, N + 2 * PAD, N), jnp.float32),
        scratch_shapes=[
            pltpu.VMEM(shape, jnp.bfloat16),
            pltpu.VMEM(shape, jnp.float32),
            pltpu.SemaphoreType.DMA((ny,)),
        ],
        compiler_params=pltpu.CompilerParams(vmem_limit_bytes=16 * MIB),
        cost_estimate=pl.CostEstimate(flops=20_000_000, bytes_accessed=16 * MIB, transcendentals=0),
        name="blend",
    )(target, share, in_hbm(sections))


def relax(low_ref, high_ref, mask_ref, left_ref, right_ref):
    ny, nx = mask_ref.shape[1:]
    rest = jnp.zeros((ny, N - nx - 2 * STEPS), jnp.float32)

    def across(left, own, right):
        return jnp.concatenate([left[:, nx - STEPS :], own, right[:, :STEPS], rest], axis=1)

    known = across(left_ref[2], mask_ref[0].astype(jnp.float32) + 1.0, right_ref[2])
    valid = jnp.where(known > 0.5, 1.0, 0.0)
    trust = jnp.where(known > 1.5, 1.0, 0.0)
    row = lax.broadcasted_iota(jnp.int32, trust.shape, 0)
    fields = []
    for component in range(2):
        own = jnp.concatenate([low_ref[component], high_ref[component]], axis=0)
        flow = across(left_ref[component], own, right_ref[component])
        field = trust * flow
        for _ in range(STEPS):
            below = jnp.where(row == 0, 0.0, pltpu.roll(field, 1, 0))
            above = jnp.where(row == ny - 1, 0.0, pltpu.roll(field, ny - 1, 0))
            beside = pltpu.roll(field, 1, 1) + pltpu.roll(field, N - 1, 1)
            lap = above + below + beside - 4.0 * field
            field = (field + SPRING * (lap + trust * (flow - field))) * valid
        fields.append(field)
    return fields


def warp_kernel(tile_ref, target_ref, share_ref, *refs):
    *flows, padded, on_hbm, off_hbm, out_hbm, field_ref, window, edges, out, wide, field, in_sems, out_sems = refs
    y = pl.program_id(0)
    ny, nx = out.shape[:2]
    even = tile_ref[0] % 2 == 0
    halos = {True: ((on_hbm, HB), (off_hbm, 0)), False: ((on_hbm, 0), (off_hbm, HB))}
    halo_copies = {
        side: [
            pltpu.make_async_copy(ref, window.at[:, into : into + HB], in_sems.at[i])
            for i, (ref, into) in enumerate(places)
        ]
        for side, places in halos.items()
    }

    @pl.when((y == 0) & even)
    def _():
        for copy in halo_copies[True]:
            copy.start()

    @pl.when((y == 0) & jnp.logical_not(even))
    def _():
        for copy in halo_copies[False]:
            copy.start()

    @pl.when(y == 0)
    def _():
        for component, values in enumerate(relax(*flows)):
            wide[component] = values
            field_ref[0, component] = values[:, STEPS : STEPS + nx]
        scalars = pltpu.make_async_copy(wide, field, in_sems.at[2])
        scalars.start()
        edges[:, :PAD] = jnp.zeros((2 * HB, PAD, N), jnp.float32)
        edges[:, PAD + N :] = jnp.zeros((2 * HB, PAD, N), jnp.float32)
        scalars.wait()
        for copy in halo_copies[True]:
            copy.wait()

    borders = (*range(HB), *range(nx - HB, nx))
    for i, x in enumerate(borders):
        more = blend_cell(y, K * nx + x, nx, target_ref, share_ref, window)
        edges[i, PAD : PAD + N] = padded[y, x, PAD : PAD + N] + more
    apart = lax.broadcasted_iota(jnp.int32, (N, N), 0) - lax.broadcasted_iota(jnp.int32, (N, N), 1)
    apart = apart.astype(jnp.float32)
    for x in range(nx):
        cell = edges.at[borders.index(x)] if x in borders else padded.at[y, x]
        shift = field[0, y, STEPS + x]
        down = jnp.clip((shift + 256.0).astype(jnp.int32) - 256, 4 - PAD, PAD - 6)
        part = shift - down.astype(jnp.float32)
        upper = cell[pl.ds(PAD + down, N), :]
        lower = cell[pl.ds(PAD + 1 + down, N), :]
        image = upper + part * (lower - upper)
        hat = jnp.maximum(0.0, 1.0 - jnp.abs(apart - field[1, y, STEPS + x])).astype(jnp.bfloat16)
        warped = dot(jnp.concatenate(split(image), axis=1), jnp.concatenate([hat, hat], axis=0))
        out[y, x] = warped.astype(jnp.bfloat16)
    store = lambda row: pltpu.make_async_copy(out.at[row], out_hbm.at[0, row], out_sems.at[row])
    store(y).start()
    wait_all([store(row) for row in range(ny)])


def warp(tile, target, share, flows, blended, on, off):
    ny, nx = blended.shape[:2]
    whole = lambda shape: pl.BlockSpec(shape, lambda y: (0,) * len(shape))
    return pl.pallas_call(
        warp_kernel,
        grid=(ny,),
        in_specs=[pl.BlockSpec(memory_space=pltpu.SMEM)] * 3
        + [whole(x.shape) for x in flows]
        + [pl.BlockSpec(memory_space=pltpu.VMEM)]
        + [pl.BlockSpec(memory_space=pl.ANY)] * 2,
        out_specs=[pl.BlockSpec(memory_space=pl.ANY), whole((1, 2, ny, nx))],
        out_shape=[
            jax.ShapeDtypeStruct((1, ny, nx, N, N), jnp.bfloat16),
            jax.ShapeDtypeStruct((1, 2, ny, nx), jnp.float32),
        ],
        scratch_shapes=[
            pltpu.VMEM((ny, 2 * HB, N, N), jnp.bfloat16),
            pltpu.VMEM((2 * HB, 2 * PAD + N, N), jnp.float32),
            pltpu.VMEM((ny, nx, N, N), jnp.bfloat16),
            pltpu.VMEM((2, ny, N), jnp.float32),
            pltpu.SMEM((2, ny, N), jnp.float32),
            pltpu.SemaphoreType.DMA((3,)),
            pltpu.SemaphoreType.DMA((ny,)),
        ],
        compiler_params=pltpu.CompilerParams(vmem_limit_bytes=12 * MIB),
        cost_estimate=pl.CostEstimate(flops=20_000_000, bytes_accessed=12 * MIB, transcendentals=0),
        name="warp",
    )(tile, target, share, *flows, in_vmem(blended), on, off)


def from_behind(x, axis, by):
    length = lax.axis_size(axis)
    pairs = [(i, i + by) for i in range(length) if 0 <= i + by < length]
    return lax.ppermute(x, axis, pairs)


def hops(tiles, sections, across):
    pairs = ([], [])
    for section in range(sections):
        x_low, rest = divmod(section, sections // 2)
        way = 1 if rest < sections // 4 else -1
        for tile in range(tiles):
            z, x_high = divmod(tile, 2)
            ends = [section * tiles + tile]
            for hop in (1, 2):
                x = (2 * x_high + x_low + hop * way) % 4
                to_z = (z + 2 * x_high - 1) % (tiles // 2) if across and hop == 2 else z
                ends.append((x % 2 * (sections // 2) + rest) * tiles + 2 * to_z + x // 2)
            pairs[0].append((ends[0], ends[1]))
            pairs[1].append((ends[1], ends[2]))
    return pairs


def per_device(sections, node_mask, box_row, box_shift, box_count, blend_weight):
    ny, nx = sections.shape[1:3]
    rows, cols, back_cols, back_rows = tables()
    half = ny // 2
    tiles, count = lax.axis_size("tile"), lax.axis_size("sec")
    tile = jnp.stack([lax.axis_index("tile"), tiles]).astype(jnp.int32)
    on_hops, off_hops = hops(tiles, count, False), hops(tiles, count, True)
    hop = lambda x, pairs: lax.ppermute(x, ("sec", "tile"), pairs)

    spectra_low, spectra_high, on, off = forward(tile, sections, rows, cols)
    from_last = from_behind(spectra_high, "sec", 1)
    from_next = from_behind(spectra_low, "sec", -1)
    off = hop(off, off_hops[0])
    on = hop(on, on_hops[0])
    target, share = slots_of(tile, box_row, box_shift, box_count, blend_weight)
    blended = blend(target, share, sections)
    off, blended = lax.optimization_barrier((off, blended))
    off = hop(off, off_hops[1])
    from_last, blended = lax.optimization_barrier((from_last, blended))

    flow_high = flow_of(spectra_high, from_last, -1, half, nx, cols, back_cols, back_rows)
    on, flow_high = lax.optimization_barrier((on, flow_high))
    flow_high = from_behind(flow_high, "sec", -1)
    on = hop(on, on_hops[1])
    flow_low = flow_of(spectra_low, from_next, 1, half, nx, cols, back_cols, back_rows)
    flow = jnp.concatenate([flow_low, flow_high], axis=1)
    flow = jnp.concatenate([flow, node_mask.astype(jnp.float32) + 1.0], axis=0)
    flow_left = from_behind(flow, "tile", 1)
    flow_right = from_behind(flow, "tile", -1)
    flows = (flow_low, flow_high, node_mask, flow_left, flow_right)
    return tuple(warp(tile, target, share, flows, blended, on, off))


def solution(mesh):
    return jax.shard_map(
        per_device,
        mesh=mesh,
        in_specs=(
            P("sec", None, "tile", None, None),
            P("sec", None, "tile"),
            P("sec", None, "tile", None),
            P("sec", None, "tile", None),
            P("sec", None, "tile"),
            P("sec", None, "tile", None),
        ),
        out_specs=(P("sec", None, "tile", None, None), P("sec", None, None, "tile")),
        check_vma=False,
    )
```

```python
import functools

import jax
import jax.numpy as jnp
import numpy as np
from jax import lax
from jax.experimental import pallas as pl
from jax.experimental.pallas import tpu as pltpu
from jax.sharding import PartitionSpec as P

K = 4
HB = 2
STEPS = 3
N = 128
HALF = N // 2
PAD = 72
ROW = 32
DEPTH = 3
SPRING = 0.2
EPS = 1e-06
MIB = 1024 * 1024


def split(x):
    high = x.astype(jnp.bfloat16)
    return high, (x - high.astype(jnp.float32)).astype(jnp.bfloat16)


def tables():
    grid = np.arange(N)[:, None] * np.arange(N)[None, :] % N
    cosine = np.cos(2.0 * np.pi * grid / N)
    sine = np.sin(2.0 * np.pi * grid / N)
    rows = np.concatenate([cosine[:HALF], sine[:HALF]])
    rows[HALF] = cosine[HALF]
    cols = np.block([[cosine, -sine], [-sine, -cosine]])
    back_cols = np.block([[cosine, sine], [-sine, cosine]]) / N
    weight = np.where(np.arange(HALF) == 0, 1.0, 2.0)
    back_rows = np.concatenate([cosine[:, :HALF] * weight, -2.0 * sine[:, :HALF]], axis=1) / N
    back_rows[:, HALF] = cosine[:, HALF] / N
    return [jnp.asarray(t, jnp.float32) for t in (rows, cols, back_cols, back_rows)]


def first_row(shape):
    return lax.broadcasted_iota(jnp.int32, shape, len(shape) - 2) == 0


def dot(a, b):
    return jnp.dot(a, b, preferred_element_type=jnp.float32)


def ahead(fetch, rows, depth):
    y = pl.program_id(0)

    @pl.when(y == 0)
    def _():
        for row in range(depth):
            for copy in fetch(row):
                copy.start()

    @pl.when(y + depth < rows)
    def _():
        for copy in fetch(y + depth):
            copy.start()

    for copy in fetch(y):
        copy.wait()


def in_hbm(x):
    return pltpu.with_memory_space_constraint(x, pltpu.HBM)


def in_vmem(x):
    return pltpu.with_memory_space_constraint(x, pltpu.VMEM)


def wait_all(copies):
    @pl.when(pl.program_id(0) == pl.num_programs(0) - 1)
    def _():
        for copy in copies:
            copy.wait()


def forward_kernel(start, strips, tile_ref, x_hbm, rows_hbm, cols_hbm, *refs):
    spec_ref, refs = refs[0], refs[1:]
    if strips:
        on_ref, off_ref, on_x, off_x, strip_sems = refs[:2] + refs[-3:]
        refs = refs[2:-3]
    x_ref, lines_ref, ends_ref, rows_ref, cols_ref, in_sems, table_sems = refs
    y = pl.program_id(0)
    count, patches = x_ref.shape[:2]
    fetch = lambda row: [pltpu.make_async_copy(x_hbm.at[0, start + row], x_ref.at[row], in_sems.at[row])]
    tables_in = [
        pltpu.make_async_copy(rows_hbm, rows_ref, table_sems.at[0]),
        pltpu.make_async_copy(cols_hbm, cols_ref, table_sems.at[1]),
    ]

    @pl.when(y == 0)
    def _():
        for copy in tables_in:
            copy.start()

    ahead(fetch, count, min(DEPTH, count))

    @pl.when(y == 0)
    def _():
        for copy in tables_in:
            copy.wait()

    if strips:
        odd = tile_ref[0] % 2
        strip_copies = [
            pltpu.make_async_copy(x_hbm.at[0, :, pl.ds(column, HB)], target, strip_sems.at[i])
            for i, (column, target) in enumerate(
                (((1 - odd) * (patches - HB), on_x), (odd * (patches - HB), off_x))
            )
        ]

        @pl.when(y == 0)
        def _():
            for copy in strip_copies:
                copy.start()

        @pl.when(y == count - 1)
        def _():
            for copy in strip_copies:
                copy.wait()
            on_ref[...] = on_x[...].astype(jnp.bfloat16)
            off_ref[...] = off_x[...].astype(jnp.bfloat16)

    rows2 = rows_ref[...]
    cols = cols_ref[...]
    cols2 = jnp.concatenate([cols, cols], axis=0)
    for pair in range(patches // 2):
        x = jnp.concatenate([x_ref[y, 2 * pair], x_ref[y, 2 * pair + 1]], axis=1)
        both = dot(rows2, jnp.concatenate(split(x), axis=0))
        for side in range(2):
            here = both[:, side * N : (side + 1) * N]
            p = 2 * pair + side
            ends_ref[p : p + 1, :N] = here[:1]
            ends_ref[p : p + 1, N:] = here[HALF : HALF + 1]
            lines = jnp.concatenate([here[:HALF], here[HALF:]], axis=1)
            high, low = split(lines)
            lines_ref[p * HALF : (p + 1) * HALF, : 2 * N] = high
            lines_ref[p * HALF : (p + 1) * HALF, 2 * N :] = low
    step = 4
    for first in range(0, patches, step):
        lines = lines_ref[first * HALF : (first + step) * HALF, :]
        freq = dot(lines, cols2).reshape(step, HALF, 2 * N)
        spec_ref[pl.ds(y * patches + first, step)] = freq.astype(jnp.bfloat16)
    ends = ends_ref[...].astype(jnp.bfloat16)
    spec_ref[count * patches, pl.ds(pl.multiple_of(y * patches, patches), patches), :] = ends


def forward(tile, sections, start, count, strips, rows, cols):
    _, ny, nx, _, _ = sections.shape
    rows2 = jnp.concatenate([rows, rows], axis=1).astype(jnp.bfloat16)
    spectra = (count * nx + 1, HALF, 2 * N)
    strip = (ny, HB, N, N)
    extra = [pltpu.VMEM(strip, jnp.float32)] * 2 + [pltpu.SemaphoreType.DMA((2,))]
    return pl.pallas_call(
        functools.partial(forward_kernel, start, strips),
        grid=(count,),
        in_specs=[pl.BlockSpec(memory_space=pltpu.SMEM)] + [pl.BlockSpec(memory_space=pltpu.HBM)] * 3,
        out_specs=[pl.BlockSpec(memory_space=pltpu.VMEM)] * (3 if strips else 1),
        out_shape=[pltpu.VMEM(spectra, jnp.bfloat16)] + [pltpu.VMEM(strip, jnp.bfloat16)] * (2 if strips else 0),
        scratch_shapes=[
            pltpu.VMEM((count, nx, N, N), jnp.float32),
            pltpu.VMEM((nx * HALF, 4 * N), jnp.bfloat16),
            pltpu.VMEM((nx, 2 * N), jnp.float32),
            pltpu.VMEM((N, 2 * N), jnp.bfloat16),
            pltpu.VMEM((2 * N, 2 * N), jnp.bfloat16),
            pltpu.SemaphoreType.DMA((count,)),
            pltpu.SemaphoreType.DMA((2,)),
        ]
        + (extra if strips else []),
        compiler_params=pltpu.CompilerParams(vmem_limit_bytes=16 * MIB),
        cost_estimate=pl.CostEstimate(flops=2_000_000_000, bytes_accessed=6 * MIB, transcendentals=0),
        name="forward",
    )(tile, in_hbm(sections), in_hbm(rows2), in_hbm(cols.astype(jnp.bfloat16)))


def times_conj(a, b, sign):
    ar, ai, br, bi = a[:, :N], a[:, N:], b[:, :N], b[:, N:]
    real = ar * br + ai * bi
    imag = ai * br - ar * bi if sign > 0 else ar * bi - ai * br
    return jnp.concatenate([real, imag], axis=1).astype(jnp.bfloat16)


def flow_kernel(sign, own, other, cols_ref, back_cols_ref, back_rows_ref, flow_ref, sides, sums, moments):
    y = pl.program_id(0)
    ny, patches = sums.shape[:2]
    last = ny * patches
    cols = cols_ref[...]
    back_cols = back_cols_ref[...]
    back_rows = back_rows_ref[...]

    @pl.when(y == 0)
    def _():
        lines = jnp.concatenate([own[last], other[last]], axis=0)
        edge = dot(jnp.concatenate([lines[:, :N], lines[:, N:]], axis=0), cols[:N])
        quarter = edge.reshape(4, last, 2 * N)
        low = times_conj(quarter[0], quarter[1], sign)
        high = times_conj(quarter[2], quarter[3], sign)
        back = dot(jnp.concatenate([low, high], axis=0), back_cols[:, :N])
        sides[...] = back.reshape(sides.shape)

    shift_rows = lax.broadcasted_iota(jnp.int32, (N, N), 0)
    offset_rows = (((shift_rows + HALF) % N) - HALF).astype(jnp.float32)
    offset_rows = jnp.concatenate([offset_rows, offset_rows], axis=1)
    step = 4
    for first in range(0, patches, step):
        here = pl.ds(y * patches + first, step)
        a = own[here].reshape(step * HALF, 2 * N).astype(jnp.float32)
        b = other[here].reshape(step * HALF, 2 * N).astype(jnp.float32)
        back = dot(times_conj(a, b, sign), back_cols)
        halves = []
        for i in range(step):
            p = first + i
            parts = []
            for side in range(2):
                part = back[i * HALF : (i + 1) * HALF, side * N : (side + 1) * N]
                top = jnp.where(first_row((16, N)), sides[side, y, p : p + 1, :], part[:16])
                parts += [top.astype(jnp.bfloat16), part[16:].astype(jnp.bfloat16)]
            halves.append(jnp.concatenate(parts, axis=0))
        for i in range(0, step, 2):
            corr = dot(back_rows, jnp.concatenate(halves[i : i + 2], axis=1))
            power = corr * corr
            total = power.sum(0, keepdims=True)
            moment = (power * offset_rows).sum(0, keepdims=True)
            for side in range(2):
                p = first + i + side
                sums[y, p : p + 1, :] = total[:, side * N : (side + 1) * N]
                moments[y, p : p + 1, :] = moment[:, side * N : (side + 1) * N]

    @pl.when(y == ny - 1)
    def _():
        lane = lax.broadcasted_iota(jnp.int32, (8, N), 1)
        row = lax.broadcasted_iota(jnp.int32, (8, N), 0)
        offset_cols = (((lane + HALF) % N) - HALF).astype(jnp.float32)
        reduce_by = jnp.where(row == 0, 1.0, jnp.where(row == 1, offset_cols, 0.0))
        over_lanes = lambda m: lax.dot_general(
            reduce_by, m.reshape(last, N), (((1,), (1,)), ((), ())),
            precision=lax.Precision.HIGHEST, preferred_element_type=jnp.float32,
        )
        by_sums = over_lanes(sums[...])
        by_moments = over_lanes(moments[...])
        total = by_sums[0:1] + EPS
        along_rows = by_moments[0:1] / total
        along_cols = by_sums[1:2] / total
        for row in range(ny):
            flow_ref[0, row : row + 1, :] = along_rows[:, row * patches : (row + 1) * patches]
            flow_ref[1, row : row + 1, :] = along_cols[:, row * patches : (row + 1) * patches]


def flow_of(own, other, sign, ny, nx, cols, back_cols, back_rows):
    whole = lambda shape: pl.BlockSpec(shape, lambda y: (0,) * len(shape))
    return pl.pallas_call(
        functools.partial(flow_kernel, sign),
        grid=(ny,),
        in_specs=[
            pl.BlockSpec(memory_space=pltpu.VMEM),
            pl.BlockSpec(memory_space=pltpu.VMEM),
            whole((2 * N, 2 * N)),
            whole((2 * N, 2 * N)),
            whole((N, N)),
        ],
        out_specs=whole((2, ny, nx)),
        out_shape=jax.ShapeDtypeStruct((2, ny, nx), jnp.float32),
        scratch_shapes=[
            pltpu.VMEM((2, ny, nx, N), jnp.float32),
            pltpu.VMEM((ny, nx, N), jnp.float32),
            pltpu.VMEM((ny, nx, N), jnp.float32),
        ],
        compiler_params=pltpu.CompilerParams(vmem_limit_bytes=8 * MIB),
        cost_estimate=pl.CostEstimate(flops=2_000_000_000, bytes_accessed=4 * MIB, transcendentals=0),
        name="flow",
    )(in_vmem(own), in_vmem(other), *(t.astype(jnp.bfloat16) for t in (cols, back_cols, back_rows)))


def slots_kernel(tile_ref, rows_ref, shifts_ref, count_ref, weight_ref, target_ref, share_ref):
    ny, _, nx = rows_ref.shape[1:]
    tile, tiles = tile_ref[0], tile_ref[1]
    live = [k < count_ref[0] for k in range(K)]
    weights = [jnp.where(live[k], weight_ref[0, :, k, :], 0.0) for k in range(K)]
    total = weights[0] + weights[1] + weights[2] + weights[3]
    share = [(w / total).astype(jnp.bfloat16).astype(jnp.float32) for w in weights]
    columns = [lax.broadcasted_iota(jnp.int32, (ny, nx), 1) + shifts_ref[0, :, k, :] for k in range(K)]
    rows = [rows_ref[0, :, k, :] * ROW for k in range(K)]
    low = [c < 0 for c in columns]
    high = [c >= nx for c in columns]
    first, last = tile == 0, tile == tiles - 1
    inside = [jnp.where(l | h, 0.0, s) for l, h, s in zip(low, high, share, strict=True)]
    share_low = [jnp.where(first, 0.0, jnp.where(l, s, 0.0)) for l, s in zip(low, share, strict=True)]
    share_high = [jnp.where(last, 0.0, jnp.where(h, s, 0.0)) for h, s in zip(high, share, strict=True)]
    beyond = [l + h for l, h in zip(share_low, share_high, strict=True)]
    share_ref[...] = jnp.concatenate(inside + beyond, axis=1)
    target = [r + jnp.where(l | h, 0, c) for r, c, l, h in zip(rows, columns, low, high, strict=True)]
    away = [
        r + jnp.where(l, c + HB, jnp.where(h, c - nx + HB, 0))
        for r, c, l, h in zip(rows, columns, low, high, strict=True)
    ]
    target_ref[...] = jnp.concatenate(target + away, axis=1)


def slots_of(tile, box_row, box_shift, box_count, blend_weight):
    ny = box_row.shape[1]
    slots_first = lambda x: jnp.transpose(x, (0, 1, 3, 2))
    return pl.pallas_call(
        slots_kernel,
        in_specs=[pl.BlockSpec(memory_space=pltpu.SMEM)] + [pl.BlockSpec(memory_space=pltpu.VMEM)] * 4,
        out_shape=[
            jax.ShapeDtypeStruct((ny, N), jnp.int32),
            jax.ShapeDtypeStruct((ny, N), jnp.float32),
        ],
        compiler_params=pltpu.CompilerParams(vmem_limit_bytes=4 * MIB),
        name="slots",
    )(tile, slots_first(box_row), slots_first(box_shift), box_count, slots_first(blend_weight))


def blend_cell(y, first, nx, target_ref, share_ref, window):
    total = None
    for k in range(K):
        spot = target_ref[y, first + k * nx]
        piece = window[spot // ROW, spot % ROW].astype(jnp.float32) * share_ref[y, first + k * nx]
        total = piece if total is None else total + piece
    return total


def blend_kernel(target_ref, share_ref, x_hbm, out_ref, window, staging, in_sems):
    y = pl.program_id(0)
    ny, nx = staging.shape[:2]
    border = jnp.zeros((nx, PAD, N), jnp.float32)
    out_ref[y, :, :PAD] = border
    out_ref[y, :, PAD + N :] = border

    @pl.when(y == 0)
    def _():
        copies = [
            pltpu.make_async_copy(x_hbm.at[0, row], staging.at[row], in_sems.at[row]) for row in range(ny)
        ]
        for copy in copies:
            copy.start()
        for row, copy in enumerate(copies):
            copy.wait()
            for x in range(nx):
                window[row, x] = staging[row, x].astype(jnp.bfloat16)

    for x in range(nx):
        out_ref[y, x, PAD : PAD + N] = blend_cell(y, x, nx, target_ref, share_ref, window)


def blend(target, share, sections):
    _, ny, nx, _, _ = sections.shape
    shape = sections.shape[1:]
    return pl.pallas_call(
        blend_kernel,
        grid=(ny,),
        in_specs=[pl.BlockSpec(memory_space=pltpu.SMEM)] * 2 + [pl.BlockSpec(memory_space=pltpu.HBM)],
        out_specs=pl.BlockSpec(memory_space=pltpu.VMEM),
        out_shape=pltpu.VMEM((ny, nx, N + 2 * PAD, N), jnp.float32),
        scratch_shapes=[
            pltpu.VMEM(shape, jnp.bfloat16),
            pltpu.VMEM(shape, jnp.float32),
            pltpu.SemaphoreType.DMA((ny,)),
        ],
        compiler_params=pltpu.CompilerParams(vmem_limit_bytes=16 * MIB),
        cost_estimate=pl.CostEstimate(flops=20_000_000, bytes_accessed=16 * MIB, transcendentals=0),
        name="blend",
    )(target, share, in_hbm(sections))


def relax(low_ref, high_ref, mask_ref, left_ref, right_ref):
    ny, nx = mask_ref.shape[1:]
    rest = jnp.zeros((ny, N - nx - 2 * STEPS), jnp.float32)

    def across(left, own, right):
        return jnp.concatenate([left[:, nx - STEPS :], own, right[:, :STEPS], rest], axis=1)

    known = across(left_ref[2], mask_ref[0].astype(jnp.float32) + 1.0, right_ref[2])
    valid = jnp.where(known > 0.5, 1.0, 0.0)
    trust = jnp.where(known > 1.5, 1.0, 0.0)
    row = lax.broadcasted_iota(jnp.int32, trust.shape, 0)
    fields = []
    for component in range(2):
        own = jnp.concatenate([low_ref[component], high_ref[component]], axis=0)
        flow = across(left_ref[component], own, right_ref[component])
        field = trust * flow
        for _ in range(STEPS):
            below = jnp.where(row == 0, 0.0, pltpu.roll(field, 1, 0))
            above = jnp.where(row == ny - 1, 0.0, pltpu.roll(field, ny - 1, 0))
            beside = pltpu.roll(field, 1, 1) + pltpu.roll(field, N - 1, 1)
            lap = above + below + beside - 4.0 * field
            field = (field + SPRING * (lap + trust * (flow - field))) * valid
        fields.append(field)
    return fields


def edge_kernel(tile_ref, target_ref, share_ref, on_ref, off_ref, padded, out_ref, window, sems):
    y = pl.program_id(0)
    ny, nx = padded.shape[:2]
    even = tile_ref[0] % 2 == 0
    halos = {True: ((on_ref, HB), (off_ref, 0)), False: ((on_ref, 0), (off_ref, HB))}
    copies = {
        side: [
            pltpu.make_async_copy(ref, window.at[:, into : into + HB], sems.at[i])
            for i, (ref, into) in enumerate(places)
        ]
        for side, places in halos.items()
    }

    @pl.when((y == 0) & even)
    def _():
        for copy in copies[True]:
            copy.start()

    @pl.when((y == 0) & jnp.logical_not(even))
    def _():
        for copy in copies[False]:
            copy.start()

    border = jnp.zeros((2 * HB, PAD, N), jnp.float32)
    out_ref[y, :, :PAD] = border
    out_ref[y, :, PAD + N :] = border

    @pl.when(y == 0)
    def _():
        for copy in copies[True]:
            copy.wait()

    for i, x in enumerate((*range(HB), *range(nx - HB, nx))):
        more = blend_cell(y, K * nx + x, nx, target_ref, share_ref, window)
        out_ref[y, i, PAD : PAD + N] = padded[y, x, PAD : PAD + N] + more


def edges_of(tile, target, share, on, off, blended):
    ny, _, tall, _ = blended.shape
    vmem = pl.BlockSpec(memory_space=pltpu.VMEM)
    return pl.pallas_call(
        edge_kernel,
        grid=(ny,),
        in_specs=[pl.BlockSpec(memory_space=pltpu.SMEM)] * 3 + [vmem] * 3,
        out_specs=vmem,
        out_shape=pltpu.VMEM((ny, 2 * HB, tall, N), jnp.float32),
        scratch_shapes=[pltpu.VMEM((ny, 2 * HB, N, N), jnp.bfloat16), pltpu.SemaphoreType.DMA((2,))],
        compiler_params=pltpu.CompilerParams(vmem_limit_bytes=4 * MIB),
        cost_estimate=pl.CostEstimate(flops=5_000_000, bytes_accessed=4 * MIB, transcendentals=0),
        name="edges",
    )(tile, target, share, in_vmem(on), in_vmem(off), in_vmem(blended))


def warp_kernel(*refs):
    *flows, padded, edges, out_hbm, field_ref, out, wide, field, sem, out_sems = refs
    y = pl.program_id(0)
    ny, nx = out.shape[:2]

    @pl.when(y == 0)
    def _():
        for component, values in enumerate(relax(*flows)):
            wide[component] = values
            field_ref[0, component] = values[:, STEPS : STEPS + nx]
        scalars = pltpu.make_async_copy(wide, field, sem)
        scalars.start()
        scalars.wait()

    borders = (*range(HB), *range(nx - HB, nx))
    apart = lax.broadcasted_iota(jnp.int32, (N, N), 0) - lax.broadcasted_iota(jnp.int32, (N, N), 1)
    apart = apart.astype(jnp.float32)
    for x in range(nx):
        cell = edges.at[y, borders.index(x)] if x in borders else padded.at[y, x]
        shift = field[0, y, STEPS + x]
        down = jnp.clip((shift + 256.0).astype(jnp.int32) - 256, 4 - PAD, PAD - 6)
        part = shift - down.astype(jnp.float32)
        upper = cell[pl.ds(PAD + down, N), :]
        lower = cell[pl.ds(PAD + 1 + down, N), :]
        image = upper + part * (lower - upper)
        hat = jnp.maximum(0.0, 1.0 - jnp.abs(apart - field[1, y, STEPS + x])).astype(jnp.bfloat16)
        warped = dot(jnp.concatenate(split(image), axis=1), jnp.concatenate([hat, hat], axis=0))
        out[y, x] = warped.astype(jnp.bfloat16)
    store = lambda row: pltpu.make_async_copy(out.at[row], out_hbm.at[0, row], out_sems.at[row])
    store(y).start()
    wait_all([store(row) for row in range(ny)])


def warp(flows, blended, edges):
    ny, nx = blended.shape[:2]
    whole = lambda shape: pl.BlockSpec(shape, lambda y: (0,) * len(shape))
    return pl.pallas_call(
        warp_kernel,
        grid=(ny,),
        in_specs=[whole(x.shape) for x in flows] + [pl.BlockSpec(memory_space=pltpu.VMEM)] * 2,
        out_specs=[pl.BlockSpec(memory_space=pl.ANY), whole((1, 2, ny, nx))],
        out_shape=[
            jax.ShapeDtypeStruct((1, ny, nx, N, N), jnp.bfloat16),
            jax.ShapeDtypeStruct((1, 2, ny, nx), jnp.float32),
        ],
        scratch_shapes=[
            pltpu.VMEM((ny, nx, N, N), jnp.bfloat16),
            pltpu.VMEM((2, ny, N), jnp.float32),
            pltpu.SMEM((2, ny, N), jnp.float32),
            pltpu.SemaphoreType.DMA,
            pltpu.SemaphoreType.DMA((ny,)),
        ],
        compiler_params=pltpu.CompilerParams(vmem_limit_bytes=8 * MIB),
        cost_estimate=pl.CostEstimate(flops=20_000_000, bytes_accessed=12 * MIB, transcendentals=0),
        name="warp",
    )(*flows, in_vmem(blended), in_vmem(edges))


def from_behind(x, axis, by):
    length = lax.axis_size(axis)
    pairs = [(i, i + by) for i in range(length) if 0 <= i + by < length]
    return lax.ppermute(x, axis, pairs)


def swapped(x):
    return lax.ppermute(x, "tile", [(i, i ^ 1) for i in range(lax.axis_size("tile"))])


def hops(tiles, sections):
    pairs = ([], [])
    for section in range(sections):
        x_low, rest = divmod(section, sections // 2)
        way = 1 if rest < sections // 4 else -1
        for tile in range(tiles):
            z, x_high = divmod(tile, 2)
            ends = [section * tiles + tile]
            for hop in (1, 2):
                x = (2 * x_high + x_low + hop * way) % 4
                to_z = (z + 2 * x_high - 1) % (tiles // 2) if hop == 2 else z
                ends.append((x % 2 * (sections // 2) + rest) * tiles + 2 * to_z + x // 2)
            pairs[0].append((ends[0], ends[1]))
            pairs[1].append((ends[1], ends[2]))
    return pairs


def per_device(sections, node_mask, box_row, box_shift, box_count, blend_weight):
    ny, nx = sections.shape[1:3]
    rows, cols, back_cols, back_rows = tables()
    half = ny // 2
    tiles, count = lax.axis_size("tile"), lax.axis_size("sec")
    tile = jnp.stack([lax.axis_index("tile"), tiles]).astype(jnp.int32)
    off_hops = hops(tiles, count)
    hop = lambda x, pairs: lax.ppermute(x, ("sec", "tile"), pairs)

    spectra_high, = forward(tile, sections, half, half, False, rows, cols)
    from_last = from_behind(spectra_high, "sec", 1)
    spectra_low, on, off = forward(tile, sections, 0, half, True, rows, cols)
    from_next = from_behind(spectra_low, "sec", -1)
    off = hop(off, off_hops[0])
    target, share = slots_of(tile, box_row, box_shift, box_count, blend_weight)
    blended = blend(target, share, sections)
    off, blended = lax.optimization_barrier((off, blended))
    off = hop(off, off_hops[1])
    from_last, blended = lax.optimization_barrier((from_last, blended))

    flow_high = flow_of(spectra_high, from_last, -1, half, nx, cols, back_cols, back_rows)
    on, flow_high = lax.optimization_barrier((on, flow_high))
    flow_high = from_behind(flow_high, "sec", -1)
    on = swapped(on)
    flow_low = flow_of(spectra_low, from_next, 1, half, nx, cols, back_cols, back_rows)
    flow = jnp.concatenate([flow_low, flow_high], axis=1)
    flow = jnp.concatenate([flow, node_mask.astype(jnp.float32) + 1.0], axis=0)
    flow_left = from_behind(flow, "tile", 1)
    flow_right = from_behind(flow, "tile", -1)
    flows = (flow_low, flow_high, node_mask, flow_left, flow_right)
    edges = edges_of(tile, target, share, on, off, blended)
    return tuple(warp(flows, blended, edges))


def solution(mesh):
    return jax.shard_map(
        per_device,
        mesh=mesh,
        in_specs=(
            P("sec", None, "tile", None, None),
            P("sec", None, "tile"),
            P("sec", None, "tile", None),
            P("sec", None, "tile", None),
            P("sec", None, "tile"),
            P("sec", None, "tile", None),
        ),
        out_specs=(P("sec", None, "tile", None, None), P("sec", None, None, "tile")),
        check_vma=False,
    )
```

```python
import functools

import jax
import jax.numpy as jnp
import numpy as np
from jax import lax
from jax.experimental import pallas as pl
from jax.experimental.pallas import tpu as pltpu
from jax.sharding import PartitionSpec as P

K = 4
HB = 2
STEPS = 3
N = 128
HALF = N // 2
PAD = 72
ROW = 32
DEPTH = 3
SPRING = 0.2
EPS = 1e-06
MIB = 1024 * 1024


def split(x):
    high = x.astype(jnp.bfloat16)
    return high, (x - high.astype(jnp.float32)).astype(jnp.bfloat16)


def tables():
    grid = np.arange(N)[:, None] * np.arange(N)[None, :] % N
    cosine = np.cos(2.0 * np.pi * grid / N)
    sine = np.sin(2.0 * np.pi * grid / N)
    rows = np.concatenate([cosine[:HALF], sine[:HALF]])
    rows[HALF] = cosine[HALF]
    cols = np.block([[cosine, -sine], [-sine, -cosine]])
    back_cols = np.block([[cosine, sine], [-sine, cosine]]) / N
    weight = np.where(np.arange(HALF) == 0, 1.0, 2.0)
    back_rows = np.concatenate([cosine[:, :HALF] * weight, -2.0 * sine[:, :HALF]], axis=1) / N
    back_rows[:, HALF] = cosine[:, HALF] / N
    return [jnp.asarray(t, jnp.float32) for t in (rows, cols, back_cols, back_rows)]


def first_row(shape):
    return lax.broadcasted_iota(jnp.int32, shape, len(shape) - 2) == 0


def dot(a, b):
    return jnp.dot(a, b, preferred_element_type=jnp.float32)


def ahead(fetch, rows, depth):
    y = pl.program_id(0)

    @pl.when(y == 0)
    def _():
        for row in range(depth):
            for copy in fetch(row):
                copy.start()

    @pl.when(y + depth < rows)
    def _():
        for copy in fetch(y + depth):
            copy.start()

    for copy in fetch(y):
        copy.wait()


def in_hbm(x):
    return pltpu.with_memory_space_constraint(x, pltpu.HBM)


def in_vmem(x):
    return pltpu.with_memory_space_constraint(x, pltpu.VMEM)


def wait_all(copies):
    @pl.when(pl.program_id(0) == pl.num_programs(0) - 1)
    def _():
        for copy in copies:
            copy.wait()


def forward_kernel(start, toward_pair, tile_ref, x_hbm, rows_hbm, cols_hbm, *refs):
    *_, spec_ref, src_ref, strip_ref, x_ref, rest_ref, lines_ref, ends_ref, rows_ref, cols_ref, in_sems, more_sems = refs
    y = pl.program_id(0)
    count, patches = x_ref.shape[:2]
    ny = strip_ref.shape[0]
    odd = tile_ref[0] % 2
    column = ((1 - odd) if toward_pair else odd) * (patches - HB)
    rest = (start + count) % ny
    fetch = lambda row: [pltpu.make_async_copy(x_hbm.at[0, start + row], x_ref.at[row], in_sems.at[row])]
    more = [
        pltpu.make_async_copy(rows_hbm, rows_ref, more_sems.at[0]),
        pltpu.make_async_copy(cols_hbm, cols_ref, more_sems.at[1]),
        pltpu.make_async_copy(
            x_hbm.at[0, pl.ds(rest, ny - count), pl.ds(column, HB)], rest_ref, more_sems.at[2]
        ),
    ]

    @pl.when(y == 0)
    def _():
        for copy in more[:2]:
            copy.start()

    ahead(fetch, count, min(DEPTH, count))

    @pl.when(y == 0)
    def _():
        for copy in more[:2]:
            copy.wait()
        more[2].start()

    @pl.when(y == count - 1)
    def _():
        more[2].wait()
        strip_ref[rest : rest + ny - count] = rest_ref[...].astype(jnp.bfloat16)

    for i in range(HB):
        strip_ref[start + y, i] = x_ref[y, column + i].astype(jnp.bfloat16)
    rows2 = rows_ref[...]
    cols = cols_ref[...]
    for pair in range(patches // 2):
        x = jnp.concatenate([x_ref[y, 2 * pair], x_ref[y, 2 * pair + 1]], axis=1)
        high, low = split(x)
        src_ref[start + y, 2 * pair] = high[:, :N]
        src_ref[start + y, 2 * pair + 1] = high[:, N:]
        both = dot(rows2, jnp.concatenate([high, low], axis=0))
        for side in range(2):
            here = both[:, side * N : (side + 1) * N]
            p = 2 * pair + side
            ends_ref[p : p + 1, :N] = here[:1]
            ends_ref[p : p + 1, N:] = here[HALF : HALF + 1]
            lines_ref[p * HALF : (p + 1) * HALF, :N] = here[:HALF].astype(jnp.bfloat16)
            lines_ref[p * HALF : (p + 1) * HALF, N:] = here[HALF:].astype(jnp.bfloat16)
    step = 4
    for first in range(0, patches, step):
        lines = lines_ref[first * HALF : (first + step) * HALF, :]
        freq = dot(lines, cols).reshape(step, HALF, 2 * N)
        spec_ref[pl.ds(y * patches + first, step)] = freq.astype(jnp.bfloat16)
    ends = ends_ref[...].astype(jnp.bfloat16)
    spec_ref[count * patches, pl.ds(pl.multiple_of(y * patches, patches), patches), :] = ends


def forward(tile, sections, start, count, toward_pair, source, rows, cols):
    _, ny, nx, _, _ = sections.shape
    rows2 = jnp.concatenate([rows, rows], axis=1).astype(jnp.bfloat16)
    spectra = (count * nx + 1, HALF, 2 * N)
    before = () if source is None else (in_vmem(source),)
    return pl.pallas_call(
        functools.partial(forward_kernel, start, toward_pair),
        grid=(count,),
        in_specs=[pl.BlockSpec(memory_space=pltpu.SMEM)]
        + [pl.BlockSpec(memory_space=pltpu.HBM)] * 3
        + [pl.BlockSpec(memory_space=pltpu.VMEM)] * len(before),
        out_specs=[pl.BlockSpec(memory_space=pltpu.VMEM)] * 3,
        out_shape=[
            pltpu.VMEM(spectra, jnp.bfloat16),
            pltpu.VMEM((ny, nx, N, N), jnp.bfloat16),
            pltpu.VMEM((ny, HB, N, N), jnp.bfloat16),
        ],
        scratch_shapes=[
            pltpu.VMEM((count, nx, N, N), jnp.float32),
            pltpu.VMEM((ny - count, HB, N, N), jnp.float32),
            pltpu.VMEM((nx * HALF, 2 * N), jnp.bfloat16),
            pltpu.VMEM((nx, 2 * N), jnp.float32),
            pltpu.VMEM((N, 2 * N), jnp.bfloat16),
            pltpu.VMEM((2 * N, 2 * N), jnp.bfloat16),
            pltpu.SemaphoreType.DMA((count,)),
            pltpu.SemaphoreType.DMA((3,)),
        ],
        input_output_aliases={4: 1} if before else {},
        compiler_params=pltpu.CompilerParams(vmem_limit_bytes=12 * MIB),
        cost_estimate=pl.CostEstimate(flops=2_000_000_000, bytes_accessed=6 * MIB, transcendentals=0),
        name="forward",
    )(tile, in_hbm(sections), in_hbm(rows2), in_hbm(cols.astype(jnp.bfloat16)), *before)


def times_conj(a, b, sign):
    ar, ai, br, bi = a[:, :N], a[:, N:], b[:, :N], b[:, N:]
    real = ar * br + ai * bi
    imag = ai * br - ar * bi if sign > 0 else ar * bi - ai * br
    return jnp.concatenate([real, imag], axis=1).astype(jnp.bfloat16)


def flow_kernel(sign, own, other, cols_ref, back_cols_ref, back_rows_ref, flow_ref, sides, sums, moments):
    y = pl.program_id(0)
    ny, patches = sums.shape[:2]
    last = ny * patches
    cols = cols_ref[...]
    back_cols = back_cols_ref[...]
    back_rows = back_rows_ref[...]

    @pl.when(y == 0)
    def _():
        lines = jnp.concatenate([own[last], other[last]], axis=0)
        edge = dot(jnp.concatenate([lines[:, :N], lines[:, N:]], axis=0), cols[:N])
        quarter = edge.reshape(4, last, 2 * N)
        low = times_conj(quarter[0], quarter[1], sign)
        high = times_conj(quarter[2], quarter[3], sign)
        back = dot(jnp.concatenate([low, high], axis=0), back_cols[:, :N])
        sides[...] = back.reshape(sides.shape)

    shift_rows = lax.broadcasted_iota(jnp.int32, (N, N), 0)
    offset_rows = (((shift_rows + HALF) % N) - HALF).astype(jnp.float32)
    offset_rows = jnp.concatenate([offset_rows, offset_rows], axis=1)
    step = 4
    for first in range(0, patches, step):
        here = pl.ds(y * patches + first, step)
        a = own[here].reshape(step * HALF, 2 * N).astype(jnp.float32)
        b = other[here].reshape(step * HALF, 2 * N).astype(jnp.float32)
        back = dot(times_conj(a, b, sign), back_cols)
        halves = []
        for i in range(step):
            p = first + i
            parts = []
            for side in range(2):
                part = back[i * HALF : (i + 1) * HALF, side * N : (side + 1) * N]
                top = jnp.where(first_row((16, N)), sides[side, y, p : p + 1, :], part[:16])
                parts += [top.astype(jnp.bfloat16), part[16:].astype(jnp.bfloat16)]
            halves.append(jnp.concatenate(parts, axis=0))
        for i in range(0, step, 2):
            corr = dot(back_rows, jnp.concatenate(halves[i : i + 2], axis=1))
            power = corr * corr
            total = power.sum(0, keepdims=True)
            moment = (power * offset_rows).sum(0, keepdims=True)
            for side in range(2):
                p = first + i + side
                sums[y, p : p + 1, :] = total[:, side * N : (side + 1) * N]
                moments[y, p : p + 1, :] = moment[:, side * N : (side + 1) * N]

    @pl.when(y == ny - 1)
    def _():
        lane = lax.broadcasted_iota(jnp.int32, (8, N), 1)
        row = lax.broadcasted_iota(jnp.int32, (8, N), 0)
        offset_cols = (((lane + HALF) % N) - HALF).astype(jnp.float32)
        reduce_by = jnp.where(row == 0, 1.0, jnp.where(row == 1, offset_cols, 0.0))
        over_lanes = lambda m: lax.dot_general(
            reduce_by, m.reshape(last, N), (((1,), (1,)), ((), ())),
            precision=lax.Precision.HIGHEST, preferred_element_type=jnp.float32,
        )
        by_sums = over_lanes(sums[...])
        by_moments = over_lanes(moments[...])
        total = by_sums[0:1] + EPS
        along_rows = by_moments[0:1] / total
        along_cols = by_sums[1:2] / total
        for row in range(ny):
            flow_ref[0, row : row + 1, :] = along_rows[:, row * patches : (row + 1) * patches]
            flow_ref[1, row : row + 1, :] = along_cols[:, row * patches : (row + 1) * patches]


def flow_of(own, other, sign, ny, nx, cols, back_cols, back_rows):
    whole = lambda shape: pl.BlockSpec(shape, lambda y: (0,) * len(shape))
    return pl.pallas_call(
        functools.partial(flow_kernel, sign),
        grid=(ny,),
        in_specs=[
            pl.BlockSpec(memory_space=pltpu.VMEM),
            pl.BlockSpec(memory_space=pltpu.VMEM),
            whole((2 * N, 2 * N)),
            whole((2 * N, 2 * N)),
            whole((N, N)),
        ],
        out_specs=whole((2, ny, nx)),
        out_shape=jax.ShapeDtypeStruct((2, ny, nx), jnp.float32),
        scratch_shapes=[
            pltpu.VMEM((2, ny, nx, N), jnp.float32),
            pltpu.VMEM((ny, nx, N), jnp.float32),
            pltpu.VMEM((ny, nx, N), jnp.float32),
        ],
        compiler_params=pltpu.CompilerParams(vmem_limit_bytes=8 * MIB),
        cost_estimate=pl.CostEstimate(flops=50_000_000_000, bytes_accessed=4 * MIB, transcendentals=0),
        name="flow",
    )(in_vmem(own), in_vmem(other), *(t.astype(jnp.bfloat16) for t in (cols, back_cols, back_rows)))


def slots_kernel(tile_ref, rows_ref, shifts_ref, count_ref, weight_ref, target_ref, share_ref):
    ny, _, nx = rows_ref.shape[1:]
    tile, tiles = tile_ref[0], tile_ref[1]
    live = [k < count_ref[0] for k in range(K)]
    weights = [jnp.where(live[k], weight_ref[0, :, k, :], 0.0) for k in range(K)]
    total = weights[0] + weights[1] + weights[2] + weights[3]
    share = [(w / total).astype(jnp.bfloat16).astype(jnp.float32) for w in weights]
    columns = [lax.broadcasted_iota(jnp.int32, (ny, nx), 1) + shifts_ref[0, :, k, :] for k in range(K)]
    rows = [rows_ref[0, :, k, :] * ROW for k in range(K)]
    low = [c < 0 for c in columns]
    high = [c >= nx for c in columns]
    first, last = tile == 0, tile == tiles - 1
    inside = [jnp.where(l | h, 0.0, s) for l, h, s in zip(low, high, share, strict=True)]
    share_low = [jnp.where(first, 0.0, jnp.where(l, s, 0.0)) for l, s in zip(low, share, strict=True)]
    share_high = [jnp.where(last, 0.0, jnp.where(h, s, 0.0)) for h, s in zip(high, share, strict=True)]
    beyond = [l + h for l, h in zip(share_low, share_high, strict=True)]
    share_ref[...] = jnp.concatenate(inside + beyond, axis=1)
    target = [r + jnp.where(l | h, 0, c) for r, c, l, h in zip(rows, columns, low, high, strict=True)]
    away = [
        r + jnp.where(l, c + HB, jnp.where(h, c - nx + HB, 0))
        for r, c, l, h in zip(rows, columns, low, high, strict=True)
    ]
    target_ref[...] = jnp.concatenate(target + away, axis=1)


def slots_of(tile, box_row, box_shift, box_count, blend_weight):
    ny = box_row.shape[1]
    slots_first = lambda x: jnp.transpose(x, (0, 1, 3, 2))
    return pl.pallas_call(
        slots_kernel,
        in_specs=[pl.BlockSpec(memory_space=pltpu.SMEM)] + [pl.BlockSpec(memory_space=pltpu.VMEM)] * 4,
        out_shape=[
            jax.ShapeDtypeStruct((ny, N), jnp.int32),
            jax.ShapeDtypeStruct((ny, N), jnp.float32),
        ],
        compiler_params=pltpu.CompilerParams(vmem_limit_bytes=4 * MIB),
        cost_estimate=pl.CostEstimate(flops=0, bytes_accessed=0, transcendentals=0),
        name="slots",
    )(tile, slots_first(box_row), slots_first(box_shift), box_count, slots_first(blend_weight))


def blend_cell(y, first, nx, target_ref, share_ref, window):
    total = None
    for k in range(K):
        spot = target_ref[y, first + k * nx]
        piece = window[spot // ROW, spot % ROW].astype(jnp.float32) * share_ref[y, first + k * nx]
        total = piece if total is None else total + piece
    return total


def blend_kernel(target_ref, share_ref, source, out_ref):
    y = pl.program_id(0)
    nx = source.shape[1]
    border = jnp.zeros((nx, PAD, N), jnp.float32)
    out_ref[y, :, :PAD] = border
    out_ref[y, :, PAD + N :] = border
    for x in range(nx):
        out_ref[y, x, PAD : PAD + N] = blend_cell(y, x, nx, target_ref, share_ref, source)


def blend(target, share, source):
    ny, nx = source.shape[:2]
    return pl.pallas_call(
        blend_kernel,
        grid=(ny,),
        in_specs=[pl.BlockSpec(memory_space=pltpu.SMEM)] * 2 + [pl.BlockSpec(memory_space=pltpu.VMEM)],
        out_specs=pl.BlockSpec(memory_space=pltpu.VMEM),
        out_shape=pltpu.VMEM((ny, nx, N + 2 * PAD, N), jnp.float32),
        compiler_params=pltpu.CompilerParams(vmem_limit_bytes=4 * MIB),
        cost_estimate=pl.CostEstimate(flops=20_000_000, bytes_accessed=4 * MIB, transcendentals=0),
        name="blend",
    )(target, share, in_vmem(source))


def relax(tile_ref, low_ref, high_ref, mask_ref, on_ref, off_ref):
    ny, nx = mask_ref.shape[1:]
    even = tile_ref[0] % 2 == 0
    left_ref = [jnp.where(even, off_ref[i], on_ref[i]) for i in range(3)]
    right_ref = [jnp.where(even, on_ref[i], off_ref[i]) for i in range(3)]
    rest = jnp.zeros((ny, N - nx - 2 * STEPS), jnp.float32)

    def across(left, own, right):
        return jnp.concatenate([left[:, nx - STEPS :], own, right[:, :STEPS], rest], axis=1)

    known = across(left_ref[2], mask_ref[0].astype(jnp.float32) + 1.0, right_ref[2])
    valid = jnp.where(known > 0.5, 1.0, 0.0)
    trust = jnp.where(known > 1.5, 1.0, 0.0)
    row = lax.broadcasted_iota(jnp.int32, trust.shape, 0)
    fields = []
    for component in range(2):
        own = jnp.concatenate([low_ref[component], high_ref[component]], axis=0)
        flow = across(left_ref[component], own, right_ref[component])
        field = trust * flow
        for _ in range(STEPS):
            below = jnp.where(row == 0, 0.0, pltpu.roll(field, 1, 0))
            above = jnp.where(row == ny - 1, 0.0, pltpu.roll(field, ny - 1, 0))
            beside = pltpu.roll(field, 1, 1) + pltpu.roll(field, N - 1, 1)
            lap = above + below + beside - 4.0 * field
            field = (field + SPRING * (lap + trust * (flow - field))) * valid
        fields.append(field)
    return fields


def edge_kernel(tile_ref, target_ref, share_ref, on_ref, off_ref, padded, out_ref, window, sems):
    y = pl.program_id(0)
    ny, nx = padded.shape[:2]
    even = tile_ref[0] % 2 == 0
    halos = {True: ((on_ref, HB), (off_ref, 0)), False: ((on_ref, 0), (off_ref, HB))}
    copies = {
        side: [
            pltpu.make_async_copy(ref, window.at[:, into : into + HB], sems.at[i])
            for i, (ref, into) in enumerate(places)
        ]
        for side, places in halos.items()
    }

    @pl.when((y == 0) & even)
    def _():
        for copy in copies[True]:
            copy.start()

    @pl.when((y == 0) & jnp.logical_not(even))
    def _():
        for copy in copies[False]:
            copy.start()

    border = jnp.zeros((2 * HB, PAD, N), jnp.float32)
    out_ref[y, :, :PAD] = border
    out_ref[y, :, PAD + N :] = border

    @pl.when(y == 0)
    def _():
        for copy in copies[True]:
            copy.wait()

    for i, x in enumerate((*range(HB), *range(nx - HB, nx))):
        more = blend_cell(y, K * nx + x, nx, target_ref, share_ref, window)
        out_ref[y, i, PAD : PAD + N] = padded[y, x, PAD : PAD + N] + more


def edges_of(tile, target, share, on, off, blended):
    ny, _, tall, _ = blended.shape
    vmem = pl.BlockSpec(memory_space=pltpu.VMEM)
    return pl.pallas_call(
        edge_kernel,
        grid=(ny,),
        in_specs=[pl.BlockSpec(memory_space=pltpu.SMEM)] * 3 + [vmem] * 3,
        out_specs=vmem,
        out_shape=pltpu.VMEM((ny, 2 * HB, tall, N), jnp.float32),
        scratch_shapes=[pltpu.VMEM((ny, 2 * HB, N, N), jnp.bfloat16), pltpu.SemaphoreType.DMA((2,))],
        compiler_params=pltpu.CompilerParams(vmem_limit_bytes=4 * MIB),
        cost_estimate=pl.CostEstimate(flops=5_000_000, bytes_accessed=4 * MIB, transcendentals=0),
        name="edges",
    )(tile, target, share, in_vmem(on), in_vmem(off), in_vmem(blended))


def warp_kernel(tile_ref, *refs):
    *flows, padded, edges, out_hbm, field_ref, out, wide, field, sem, out_sems = refs
    y = pl.program_id(0)
    ny, nx = out.shape[:2]

    @pl.when(y == 0)
    def _():
        for component, values in enumerate(relax(tile_ref, *flows)):
            wide[component] = values
            field_ref[0, component] = values[:, STEPS : STEPS + nx]
        scalars = pltpu.make_async_copy(wide, field, sem)
        scalars.start()
        scalars.wait()

    borders = (*range(HB), *range(nx - HB, nx))
    apart = lax.broadcasted_iota(jnp.int32, (N, N), 0) - lax.broadcasted_iota(jnp.int32, (N, N), 1)
    apart = apart.astype(jnp.float32)
    for x in range(nx):
        cell = edges.at[y, borders.index(x)] if x in borders else padded.at[y, x]
        shift = field[0, y, STEPS + x]
        down = jnp.clip((shift + 256.0).astype(jnp.int32) - 256, 4 - PAD, PAD - 6)
        part = shift - down.astype(jnp.float32)
        upper = cell[pl.ds(PAD + down, N), :]
        lower = cell[pl.ds(PAD + 1 + down, N), :]
        image = upper + part * (lower - upper)
        hat = jnp.maximum(0.0, 1.0 - jnp.abs(apart - field[1, y, STEPS + x])).astype(jnp.bfloat16)
        warped = dot(jnp.concatenate(split(image), axis=1), jnp.concatenate([hat, hat], axis=0))
        out[y, x] = warped.astype(jnp.bfloat16)
    store = lambda row: pltpu.make_async_copy(out.at[row], out_hbm.at[0, row], out_sems.at[row])
    store(y).start()
    wait_all([store(row) for row in range(ny)])


def warp(tile, flows, blended, edges):
    ny, nx = blended.shape[:2]
    whole = lambda shape: pl.BlockSpec(shape, lambda y: (0,) * len(shape))
    return pl.pallas_call(
        warp_kernel,
        grid=(ny,),
        in_specs=[pl.BlockSpec(memory_space=pltpu.SMEM)]
        + [whole(x.shape) for x in flows]
        + [pl.BlockSpec(memory_space=pltpu.VMEM)] * 2,
        out_specs=[pl.BlockSpec(memory_space=pl.ANY), whole((1, 2, ny, nx))],
        out_shape=[
            jax.ShapeDtypeStruct((1, ny, nx, N, N), jnp.bfloat16),
            jax.ShapeDtypeStruct((1, 2, ny, nx), jnp.float32),
        ],
        scratch_shapes=[
            pltpu.VMEM((ny, nx, N, N), jnp.bfloat16),
            pltpu.VMEM((2, ny, N), jnp.float32),
            pltpu.SMEM((2, ny, N), jnp.float32),
            pltpu.SemaphoreType.DMA,
            pltpu.SemaphoreType.DMA((ny,)),
        ],
        compiler_params=pltpu.CompilerParams(vmem_limit_bytes=8 * MIB),
        cost_estimate=pl.CostEstimate(flops=20_000_000, bytes_accessed=12 * MIB, transcendentals=0),
        name="warp",
    )(tile, *flows, in_vmem(blended), in_vmem(edges))


def from_behind(x, axis, by):
    length = lax.axis_size(axis)
    pairs = [(i, i + by) for i in range(length) if 0 <= i + by < length]
    return lax.ppermute(x, axis, pairs)


def swapped(x):
    return lax.ppermute(x, "tile", [(i, i ^ 1) for i in range(lax.axis_size("tile"))])


def hops(tiles, sections, beyond):
    pairs = ([], [])
    for section in range(sections):
        x_low, rest = divmod(section, sections // 2)
        way = 1 if rest < sections // 4 else -1
        for tile in range(tiles):
            z, x_high = divmod(tile, 2)
            ends = [section * tiles + tile]
            for hop in (1, 2):
                x = (2 * x_high + x_low + hop * way) % 4
                to_z = (z + 2 * x_high - 1) % (tiles // 2) if beyond and hop == 2 else z
                ends.append((x % 2 * (sections // 2) + rest) * tiles + 2 * to_z + x // 2)
            pairs[0].append((ends[0], ends[1]))
            pairs[1].append((ends[1], ends[2]))
    return pairs


def per_device(sections, node_mask, box_row, box_shift, box_count, blend_weight):
    ny, nx = sections.shape[1:3]
    rows, cols, back_cols, back_rows = tables()
    half = ny // 2
    tiles, count = lax.axis_size("tile"), lax.axis_size("sec")
    tile = jnp.stack([lax.axis_index("tile"), tiles]).astype(jnp.int32)
    on_hops, off_hops = hops(tiles, count, False), hops(tiles, count, True)
    hop = lambda x, pairs: lax.ppermute(x, ("sec", "tile"), pairs)

    spectra_high, source, on = forward(tile, sections, half, half, True, None, rows, cols)
    from_last = from_behind(spectra_high, "sec", 1)
    on = hop(on, on_hops[0])
    spectra_low, source, off = forward(tile, sections, 0, half, False, source, rows, cols)
    from_next = from_behind(spectra_low, "sec", -1)
    off = hop(off, off_hops[0])
    target, share = slots_of(tile, box_row, box_shift, box_count, blend_weight)
    on, source = lax.optimization_barrier((on, source))
    on = hop(on, on_hops[1])
    blended = blend(target, share, source)
    from_last, blended = lax.optimization_barrier((from_last, blended))

    flow_high = flow_of(spectra_high, from_last, -1, half, nx, cols, back_cols, back_rows)
    off, flow_high = lax.optimization_barrier((off, flow_high))
    flow_high = from_behind(flow_high, "sec", -1)
    off = hop(off, off_hops[1])
    flow_low = flow_of(spectra_low, from_next, 1, half, nx, cols, back_cols, back_rows)
    flow = jnp.concatenate([flow_low, flow_high], axis=1)
    flow = jnp.concatenate([flow, node_mask.astype(jnp.float32) + 1.0], axis=0)
    beyond = [(i, i + 1) for i in range(1, tiles - 1, 2)]
    flow_off = lax.ppermute(flow, "tile", beyond + [(j, i) for i, j in beyond])
    flow_on = swapped(flow)
    flows = (flow_low, flow_high, node_mask, flow_on, flow_off)
    edges = edges_of(tile, target, share, on, off, blended)
    return tuple(warp(tile, flows, blended, edges))


def solution(mesh):
    return jax.shard_map(
        per_device,
        mesh=mesh,
        in_specs=(
            P("sec", None, "tile", None, None),
            P("sec", None, "tile"),
            P("sec", None, "tile", None),
            P("sec", None, "tile", None),
            P("sec", None, "tile"),
            P("sec", None, "tile", None),
        ),
        out_specs=(P("sec", None, "tile", None, None), P("sec", None, None, "tile")),
        check_vma=False,
    )
```

```python
import functools

import jax
import jax.numpy as jnp
import numpy as np
from jax import lax
from jax.experimental import pallas as pl
from jax.experimental.pallas import tpu as pltpu
from jax.sharding import PartitionSpec as P

K = 4
HB = 2
STEPS = 3
N = 128
HALF = N // 2
PAD = 72
ROW = 32
DEPTH = 2
SPRING = 0.2
EPS = 1e-06
MIB = 1024 * 1024


def split(x):
    high = x.astype(jnp.bfloat16)
    return high, (x - high.astype(jnp.float32)).astype(jnp.bfloat16)


def tables():
    grid = np.arange(N)[:, None] * np.arange(N)[None, :] % N
    cosine = np.cos(2.0 * np.pi * grid / N)
    sine = np.sin(2.0 * np.pi * grid / N)
    rows = np.concatenate([cosine[:HALF], sine[:HALF]])
    rows[HALF] = cosine[HALF]
    cols = np.block([[cosine, -sine], [-sine, -cosine]])
    back_cols = np.block([[cosine, sine], [-sine, cosine]]) / N
    weight = np.where(np.arange(HALF) == 0, 1.0, 2.0)
    back_rows = np.concatenate([cosine[:, :HALF] * weight, -2.0 * sine[:, :HALF]], axis=1) / N
    back_rows[:, HALF] = cosine[:, HALF] / N
    return [jnp.asarray(t, jnp.float32) for t in (rows, cols, back_cols, back_rows)]


def first_row(shape):
    return lax.broadcasted_iota(jnp.int32, shape, len(shape) - 2) == 0


def dot(a, b):
    return jnp.dot(a, b, preferred_element_type=jnp.float32)


def ahead(fetch, rows, depth):
    y = pl.program_id(0)

    @pl.when(y == 0)
    def _():
        for row in range(depth):
            for copy in fetch(row):
                copy.start()

    @pl.when(y + depth < rows)
    def _():
        for copy in fetch(y + depth):
            copy.start()

    for copy in fetch(y):
        copy.wait()


def in_hbm(x):
    return pltpu.with_memory_space_constraint(x, pltpu.HBM)


def in_vmem(x):
    return pltpu.with_memory_space_constraint(x, pltpu.VMEM)


def wait_all(copies):
    @pl.when(pl.program_id(0) == pl.num_programs(0) - 1)
    def _():
        for copy in copies:
            copy.wait()


def forward_kernel(start, toward_pair, tile_ref, x_hbm, rows_hbm, cols_hbm, *refs):
    *_, spec_ref, src_ref, strip_ref, x_ref, rest_ref, lines_ref, ends_ref, rows_ref, cols_ref, in_sems, more_sems = refs
    y = pl.program_id(0)
    count, patches = x_ref.shape[:2]
    ny = strip_ref.shape[0]
    odd = tile_ref[0] % 2
    column = ((1 - odd) if toward_pair else odd) * (patches - HB)
    rest = (start + count) % ny
    fetch = lambda row: [pltpu.make_async_copy(x_hbm.at[0, start + row], x_ref.at[row], in_sems.at[row])]
    more = [
        pltpu.make_async_copy(rows_hbm, rows_ref, more_sems.at[0]),
        pltpu.make_async_copy(cols_hbm, cols_ref, more_sems.at[1]),
        pltpu.make_async_copy(
            x_hbm.at[0, pl.ds(rest, ny - count), pl.ds(column, HB)], rest_ref, more_sems.at[2]
        ),
    ]

    @pl.when(y == 0)
    def _():
        for copy in more[:2]:
            copy.start()

    ahead(fetch, count, min(DEPTH, count))

    @pl.when(y == 0)
    def _():
        for copy in more[:2]:
            copy.wait()
        more[2].start()

    @pl.when(y == count - 1)
    def _():
        more[2].wait()
        strip_ref[rest : rest + ny - count] = rest_ref[...].astype(jnp.bfloat16)

    for i in range(HB):
        strip_ref[start + y, i] = x_ref[y, column + i].astype(jnp.bfloat16)
    rows2 = rows_ref[...]
    cols = cols_ref[...]
    for pair in range(patches // 2):
        x = jnp.concatenate([x_ref[y, 2 * pair], x_ref[y, 2 * pair + 1]], axis=1)
        high, low = split(x)
        src_ref[start + y, 2 * pair] = high[:, :N]
        src_ref[start + y, 2 * pair + 1] = high[:, N:]
        both = dot(rows2, jnp.concatenate([high, low], axis=0))
        for side in range(2):
            here = both[:, side * N : (side + 1) * N]
            p = 2 * pair + side
            ends_ref[p : p + 1, :N] = here[:1]
            ends_ref[p : p + 1, N:] = here[HALF : HALF + 1]
            lines_ref[p * HALF : (p + 1) * HALF, :N] = here[:HALF].astype(jnp.bfloat16)
            lines_ref[p * HALF : (p + 1) * HALF, N:] = here[HALF:].astype(jnp.bfloat16)
    step = 4
    for first in range(0, patches, step):
        lines = lines_ref[first * HALF : (first + step) * HALF, :]
        freq = dot(lines, cols).reshape(step, HALF, 2 * N)
        spec_ref[pl.ds(y * patches + first, step)] = freq.astype(jnp.bfloat16)
    ends = ends_ref[...].astype(jnp.bfloat16)
    spec_ref[count * patches, pl.ds(pl.multiple_of(y * patches, patches), patches), :] = ends


def forward(tile, sections, start, count, toward_pair, source, rows, cols):
    _, ny, nx, _, _ = sections.shape
    rows2 = jnp.concatenate([rows, rows], axis=1).astype(jnp.bfloat16)
    spectra = (count * nx + 1, HALF, 2 * N)
    before = () if source is None else (in_vmem(source),)
    return pl.pallas_call(
        functools.partial(forward_kernel, start, toward_pair),
        grid=(count,),
        in_specs=[pl.BlockSpec(memory_space=pltpu.SMEM)]
        + [pl.BlockSpec(memory_space=pltpu.HBM)] * 3
        + [pl.BlockSpec(memory_space=pltpu.VMEM)] * len(before),
        out_specs=[pl.BlockSpec(memory_space=pltpu.VMEM)] * 3,
        out_shape=[
            pltpu.VMEM(spectra, jnp.bfloat16),
            pltpu.VMEM((ny, nx, N, N), jnp.bfloat16),
            pltpu.VMEM((ny, HB, N, N), jnp.bfloat16),
        ],
        scratch_shapes=[
            pltpu.VMEM((count, nx, N, N), jnp.float32),
            pltpu.VMEM((ny - count, HB, N, N), jnp.float32),
            pltpu.VMEM((nx * HALF, 2 * N), jnp.bfloat16),
            pltpu.VMEM((nx, 2 * N), jnp.float32),
            pltpu.VMEM((N, 2 * N), jnp.bfloat16),
            pltpu.VMEM((2 * N, 2 * N), jnp.bfloat16),
            pltpu.SemaphoreType.DMA((count,)),
            pltpu.SemaphoreType.DMA((3,)),
        ],
        input_output_aliases={4: 1} if before else {},
        compiler_params=pltpu.CompilerParams(vmem_limit_bytes=12 * MIB),
        cost_estimate=pl.CostEstimate(flops=2_000_000_000, bytes_accessed=6 * MIB, transcendentals=0),
        name="forward",
    )(tile, in_hbm(sections), in_hbm(rows2), in_hbm(cols.astype(jnp.bfloat16)), *before)


def times_conj(a, b, sign):
    ar, ai, br, bi = a[:, :N], a[:, N:], b[:, :N], b[:, N:]
    real = ar * br + ai * bi
    imag = ai * br - ar * bi if sign > 0 else ar * bi - ai * br
    return jnp.concatenate([real, imag], axis=1).astype(jnp.bfloat16)


def flow_kernel(sign, own, other, cols_ref, back_cols_ref, back_rows_ref, flow_ref, sides, sums, moments):
    y = pl.program_id(0)
    ny, patches = sums.shape[:2]
    last = ny * patches
    cols = cols_ref[...]
    back_cols = back_cols_ref[...]
    back_rows = back_rows_ref[...]

    @pl.when(y == 0)
    def _():
        lines = jnp.concatenate([own[last], other[last]], axis=0)
        edge = dot(jnp.concatenate([lines[:, :N], lines[:, N:]], axis=0), cols[:N])
        quarter = edge.reshape(4, last, 2 * N)
        low = times_conj(quarter[0], quarter[1], sign)
        high = times_conj(quarter[2], quarter[3], sign)
        back = dot(jnp.concatenate([low, high], axis=0), back_cols[:, :N])
        sides[...] = back.reshape(sides.shape)

    shift_rows = lax.broadcasted_iota(jnp.int32, (N, N), 0)
    offset_rows = (((shift_rows + HALF) % N) - HALF).astype(jnp.float32)
    offset_rows = jnp.concatenate([offset_rows, offset_rows], axis=1)
    step = 4
    for first in range(0, patches, step):
        here = pl.ds(y * patches + first, step)
        a = own[here].reshape(step * HALF, 2 * N).astype(jnp.float32)
        b = other[here].reshape(step * HALF, 2 * N).astype(jnp.float32)
        back = dot(times_conj(a, b, sign), back_cols)
        halves = []
        for i in range(step):
            p = first + i
            parts = []
            for side in range(2):
                part = back[i * HALF : (i + 1) * HALF, side * N : (side + 1) * N]
                top = jnp.where(first_row((16, N)), sides[side, y, p : p + 1, :], part[:16])
                parts += [top.astype(jnp.bfloat16), part[16:].astype(jnp.bfloat16)]
            halves.append(jnp.concatenate(parts, axis=0))
        for i in range(0, step, 2):
            corr = dot(back_rows, jnp.concatenate(halves[i : i + 2], axis=1))
            power = corr * corr
            total = power.sum(0, keepdims=True)
            moment = (power * offset_rows).sum(0, keepdims=True)
            for side in range(2):
                p = first + i + side
                sums[y, p : p + 1, :] = total[:, side * N : (side + 1) * N]
                moments[y, p : p + 1, :] = moment[:, side * N : (side + 1) * N]

    @pl.when(y == ny - 1)
    def _():
        lane = lax.broadcasted_iota(jnp.int32, (8, N), 1)
        row = lax.broadcasted_iota(jnp.int32, (8, N), 0)
        offset_cols = (((lane + HALF) % N) - HALF).astype(jnp.float32)
        reduce_by = jnp.where(row == 0, 1.0, jnp.where(row == 1, offset_cols, 0.0))
        over_lanes = lambda m: lax.dot_general(
            reduce_by, m.reshape(last, N), (((1,), (1,)), ((), ())),
            precision=lax.Precision.HIGHEST, preferred_element_type=jnp.float32,
        )
        by_sums = over_lanes(sums[...])
        by_moments = over_lanes(moments[...])
        total = by_sums[0:1] + EPS
        along_rows = by_moments[0:1] / total
        along_cols = by_sums[1:2] / total
        for row in range(ny):
            flow_ref[0, row : row + 1, :] = along_rows[:, row * patches : (row + 1) * patches]
            flow_ref[1, row : row + 1, :] = along_cols[:, row * patches : (row + 1) * patches]


def flow_of(own, other, sign, ny, nx, cols, back_cols, back_rows):
    whole = lambda shape: pl.BlockSpec(shape, lambda y: (0,) * len(shape))
    return pl.pallas_call(
        functools.partial(flow_kernel, sign),
        grid=(ny,),
        in_specs=[
            pl.BlockSpec(memory_space=pltpu.VMEM),
            pl.BlockSpec(memory_space=pltpu.VMEM),
            whole((2 * N, 2 * N)),
            whole((2 * N, 2 * N)),
            whole((N, N)),
        ],
        out_specs=whole((2, ny, nx)),
        out_shape=jax.ShapeDtypeStruct((2, ny, nx), jnp.float32),
        scratch_shapes=[
            pltpu.VMEM((2, ny, nx, N), jnp.float32),
            pltpu.VMEM((ny, nx, N), jnp.float32),
            pltpu.VMEM((ny, nx, N), jnp.float32),
        ],
        compiler_params=pltpu.CompilerParams(vmem_limit_bytes=8 * MIB),
        cost_estimate=pl.CostEstimate(flops=50_000_000_000, bytes_accessed=4 * MIB, transcendentals=0),
        name="flow",
    )(in_vmem(own), in_vmem(other), *(t.astype(jnp.bfloat16) for t in (cols, back_cols, back_rows)))


def slots_kernel(tile_ref, rows_ref, shifts_ref, count_ref, weight_ref, target_ref, share_ref):
    ny, _, nx = rows_ref.shape[1:]
    tile, tiles = tile_ref[0], tile_ref[1]
    live = [k < count_ref[0] for k in range(K)]
    weights = [jnp.where(live[k], weight_ref[0, :, k, :], 0.0) for k in range(K)]
    total = weights[0] + weights[1] + weights[2] + weights[3]
    share = [(w / total).astype(jnp.bfloat16).astype(jnp.float32) for w in weights]
    columns = [lax.broadcasted_iota(jnp.int32, (ny, nx), 1) + shifts_ref[0, :, k, :] for k in range(K)]
    rows = [rows_ref[0, :, k, :] * ROW for k in range(K)]
    low = [c < 0 for c in columns]
    high = [c >= nx for c in columns]
    first, last = tile == 0, tile == tiles - 1
    inside = [jnp.where(l | h, 0.0, s) for l, h, s in zip(low, high, share, strict=True)]
    share_low = [jnp.where(first, 0.0, jnp.where(l, s, 0.0)) for l, s in zip(low, share, strict=True)]
    share_high = [jnp.where(last, 0.0, jnp.where(h, s, 0.0)) for h, s in zip(high, share, strict=True)]
    beyond = [l + h for l, h in zip(share_low, share_high, strict=True)]
    share_ref[...] = jnp.concatenate(inside + beyond, axis=1)
    target = [r + jnp.where(l | h, 0, c) for r, c, l, h in zip(rows, columns, low, high, strict=True)]
    away = [
        r + jnp.where(l, c + HB, jnp.where(h, c - nx + HB, 0))
        for r, c, l, h in zip(rows, columns, low, high, strict=True)
    ]
    target_ref[...] = jnp.concatenate(target + away, axis=1)


def slots_of(tile, box_row, box_shift, box_count, blend_weight):
    ny = box_row.shape[1]
    slots_first = lambda x: jnp.transpose(x, (0, 1, 3, 2))
    return pl.pallas_call(
        slots_kernel,
        in_specs=[pl.BlockSpec(memory_space=pltpu.SMEM)] + [pl.BlockSpec(memory_space=pltpu.VMEM)] * 4,
        out_shape=[
            jax.ShapeDtypeStruct((ny, N), jnp.int32),
            jax.ShapeDtypeStruct((ny, N), jnp.float32),
        ],
        compiler_params=pltpu.CompilerParams(vmem_limit_bytes=4 * MIB),
        cost_estimate=pl.CostEstimate(flops=0, bytes_accessed=0, transcendentals=0),
        name="slots",
    )(tile, slots_first(box_row), slots_first(box_shift), box_count, slots_first(blend_weight))


def blend_cell(y, first, nx, target_ref, share_ref, window):
    total = None
    for k in range(K):
        spot = target_ref[y, first + k * nx]
        piece = window[spot // ROW, spot % ROW].astype(jnp.float32) * share_ref[y, first + k * nx]
        total = piece if total is None else total + piece
    return total


def blend_kernel(target_ref, share_ref, source, out_ref):
    y = pl.program_id(0)
    nx = source.shape[1]
    border = jnp.zeros((nx, PAD, N), jnp.float32)
    out_ref[y, :, :PAD] = border
    out_ref[y, :, PAD + N :] = border
    for x in range(nx):
        out_ref[y, x, PAD : PAD + N] = blend_cell(y, x, nx, target_ref, share_ref, source)


def blend(target, share, source):
    ny, nx = source.shape[:2]
    return pl.pallas_call(
        blend_kernel,
        grid=(ny,),
        in_specs=[pl.BlockSpec(memory_space=pltpu.SMEM)] * 2 + [pl.BlockSpec(memory_space=pltpu.VMEM)],
        out_specs=pl.BlockSpec(memory_space=pltpu.VMEM),
        out_shape=pltpu.VMEM((ny, nx, N + 2 * PAD, N), jnp.float32),
        compiler_params=pltpu.CompilerParams(vmem_limit_bytes=4 * MIB),
        cost_estimate=pl.CostEstimate(flops=20_000_000, bytes_accessed=4 * MIB, transcendentals=0),
        name="blend",
    )(target, share, in_vmem(source))


def relax(tile_ref, low_ref, high_ref, mask_ref, on_ref, off_ref):
    ny, nx = mask_ref.shape[1:]
    even = tile_ref[0] % 2 == 0
    left_ref = [jnp.where(even, off_ref[i], on_ref[i]) for i in range(3)]
    right_ref = [jnp.where(even, on_ref[i], off_ref[i]) for i in range(3)]
    rest = jnp.zeros((ny, N - nx - 2 * STEPS), jnp.float32)

    def across(left, own, right):
        return jnp.concatenate([left[:, nx - STEPS :], own, right[:, :STEPS], rest], axis=1)

    known = across(left_ref[2], mask_ref[0].astype(jnp.float32) + 1.0, right_ref[2])
    valid = jnp.where(known > 0.5, 1.0, 0.0)
    trust = jnp.where(known > 1.5, 1.0, 0.0)
    row = lax.broadcasted_iota(jnp.int32, trust.shape, 0)
    fields = []
    for component in range(2):
        own = jnp.concatenate([low_ref[component], high_ref[component]], axis=0)
        flow = across(left_ref[component], own, right_ref[component])
        field = trust * flow
        for _ in range(STEPS):
            below = jnp.where(row == 0, 0.0, pltpu.roll(field, 1, 0))
            above = jnp.where(row == ny - 1, 0.0, pltpu.roll(field, ny - 1, 0))
            beside = pltpu.roll(field, 1, 1) + pltpu.roll(field, N - 1, 1)
            lap = above + below + beside - 4.0 * field
            field = (field + SPRING * (lap + trust * (flow - field))) * valid
        fields.append(field)
    return fields


def edge_kernel(tile_ref, target_ref, share_ref, on_ref, off_ref, padded, out_ref, window, sems):
    y = pl.program_id(0)
    ny, nx = padded.shape[:2]
    even = tile_ref[0] % 2 == 0
    halos = {True: ((on_ref, HB), (off_ref, 0)), False: ((on_ref, 0), (off_ref, HB))}
    copies = {
        side: [
            pltpu.make_async_copy(ref, window.at[:, into : into + HB], sems.at[i])
            for i, (ref, into) in enumerate(places)
        ]
        for side, places in halos.items()
    }

    @pl.when((y == 0) & even)
    def _():
        for copy in copies[True]:
            copy.start()

    @pl.when((y == 0) & jnp.logical_not(even))
    def _():
        for copy in copies[False]:
            copy.start()

    border = jnp.zeros((2 * HB, PAD, N), jnp.float32)
    out_ref[y, :, :PAD] = border
    out_ref[y, :, PAD + N :] = border

    @pl.when(y == 0)
    def _():
        for copy in copies[True]:
            copy.wait()

    for i, x in enumerate((*range(HB), *range(nx - HB, nx))):
        more = blend_cell(y, K * nx + x, nx, target_ref, share_ref, window)
        out_ref[y, i, PAD : PAD + N] = padded[y, x, PAD : PAD + N] + more


def edges_of(tile, target, share, on, off, blended):
    ny, _, tall, _ = blended.shape
    vmem = pl.BlockSpec(memory_space=pltpu.VMEM)
    return pl.pallas_call(
        edge_kernel,
        grid=(ny,),
        in_specs=[pl.BlockSpec(memory_space=pltpu.SMEM)] * 3 + [vmem] * 3,
        out_specs=vmem,
        out_shape=pltpu.VMEM((ny, 2 * HB, tall, N), jnp.float32),
        scratch_shapes=[pltpu.VMEM((ny, 2 * HB, N, N), jnp.bfloat16), pltpu.SemaphoreType.DMA((2,))],
        compiler_params=pltpu.CompilerParams(vmem_limit_bytes=4 * MIB),
        cost_estimate=pl.CostEstimate(flops=5_000_000, bytes_accessed=4 * MIB, transcendentals=0),
        name="edges",
    )(tile, target, share, in_vmem(on), in_vmem(off), in_vmem(blended))


def warped(cell, down_shift, right_shift):
    whole_of = lambda shift: (shift + 256.0).astype(jnp.int32) - 256
    line = lambda value: jnp.full((1, N), value, jnp.float32).astype(jnp.bfloat16)
    down = jnp.clip(whole_of(down_shift), 4 - PAD, PAD - 6)
    part = down_shift - down.astype(jnp.float32)
    upper = cell[pl.ds(PAD + down, N), :]
    lower = cell[pl.ds(PAD + 1 + down, N), :]
    image = upper + part * (lower - upper)
    right = whole_of(right_shift).astype(jnp.float32)
    apart = lax.broadcasted_iota(jnp.int32, (N, N), 0) - lax.broadcasted_iota(jnp.int32, (N, N), 1)
    apart = apart.astype(jnp.bfloat16) - line(right)
    one = jnp.bfloat16(1.0)
    hat = jnp.maximum(jnp.bfloat16(0.0), one - jnp.abs(apart - line(right_shift - right)))
    return dot(image.astype(jnp.bfloat16), hat).astype(jnp.bfloat16)


def warp_kernel(tile_ref, *refs):
    *flows, padded, edges, out_hbm, field_ref, out, wide, field, sem, out_sems = refs
    y = pl.program_id(0)
    ny, nx = out.shape[:2]

    @pl.when(y == 0)
    def _():
        for component, values in enumerate(relax(tile_ref, *flows)):
            wide[component] = values
            field_ref[0, component] = values[:, STEPS : STEPS + nx]
        scalars = pltpu.make_async_copy(wide, field, sem)
        scalars.start()
        scalars.wait()

    borders = (*range(HB), *range(nx - HB, nx))
    for x in range(nx):
        cell = edges.at[y, borders.index(x)] if x in borders else padded.at[y, x]
        out[y, x] = warped(cell, field[0, y, STEPS + x], field[1, y, STEPS + x])
    store = lambda row: pltpu.make_async_copy(out.at[row], out_hbm.at[0, row], out_sems.at[row])
    store(y).start()
    wait_all([store(row) for row in range(ny)])


def warp(tile, flows, blended, edges):
    ny, nx = blended.shape[:2]
    whole = lambda shape: pl.BlockSpec(shape, lambda y: (0,) * len(shape))
    return pl.pallas_call(
        warp_kernel,
        grid=(ny,),
        in_specs=[pl.BlockSpec(memory_space=pltpu.SMEM)]
        + [whole(x.shape) for x in flows]
        + [pl.BlockSpec(memory_space=pltpu.VMEM)] * 2,
        out_specs=[pl.BlockSpec(memory_space=pl.ANY), whole((1, 2, ny, nx))],
        out_shape=[
            jax.ShapeDtypeStruct((1, ny, nx, N, N), jnp.bfloat16),
            jax.ShapeDtypeStruct((1, 2, ny, nx), jnp.float32),
        ],
        scratch_shapes=[
            pltpu.VMEM((ny, nx, N, N), jnp.bfloat16),
            pltpu.VMEM((2, ny, N), jnp.float32),
            pltpu.SMEM((2, ny, N), jnp.float32),
            pltpu.SemaphoreType.DMA,
            pltpu.SemaphoreType.DMA((ny,)),
        ],
        compiler_params=pltpu.CompilerParams(vmem_limit_bytes=8 * MIB),
        cost_estimate=pl.CostEstimate(flops=20_000_000, bytes_accessed=12 * MIB, transcendentals=0),
        name="warp",
    )(tile, *flows, in_vmem(blended), in_vmem(edges))


def from_behind(x, axis, by):
    length = lax.axis_size(axis)
    pairs = [(i, i + by) for i in range(length) if 0 <= i + by < length]
    return lax.ppermute(x, axis, pairs)


def swapped(x):
    return lax.ppermute(x, "tile", [(i, i ^ 1) for i in range(lax.axis_size("tile"))])


def hops(tiles, sections):
    pairs = ([], [])
    for section in range(sections):
        x_low, rest = divmod(section, sections // 2)
        way = 1 if rest < sections // 4 else -1
        for tile in range(tiles):
            z, x_high = divmod(tile, 2)
            ends = [section * tiles + tile]
            for hop in (1, 2):
                x = (2 * x_high + x_low + hop * way) % 4
                ends.append((x % 2 * (sections // 2) + rest) * tiles + 2 * z + x // 2)
            pairs[0].append((ends[0], ends[1]))
            pairs[1].append((ends[1], ends[2]))
    return pairs


def beyond(x):
    tiles = lax.axis_size("tile")
    pairs = [(i, i + 1) for i in range(1, tiles - 1, 2)]
    return lax.ppermute(x, "tile", pairs + [(j, i) for i, j in pairs])


def per_device(sections, node_mask, box_row, box_shift, box_count, blend_weight):
    ny, nx = sections.shape[1:3]
    rows, cols, back_cols, back_rows = tables()
    half = ny // 2
    tiles, count = lax.axis_size("tile"), lax.axis_size("sec")
    tile = jnp.stack([lax.axis_index("tile"), tiles]).astype(jnp.int32)
    on_hops = hops(tiles, count)
    hop = lambda x, pairs: lax.ppermute(x, ("sec", "tile"), pairs)

    spectra_high, source, on = forward(tile, sections, half, half, True, None, rows, cols)
    from_last = from_behind(spectra_high, "sec", 1)
    on = hop(on, on_hops[0])
    spectra_low, source, off = forward(tile, sections, 0, half, False, source, rows, cols)
    from_next = from_behind(spectra_low, "sec", -1)
    target, share = slots_of(tile, box_row, box_shift, box_count, blend_weight)
    on, source = lax.optimization_barrier((on, source))
    on = hop(on, on_hops[1])
    blended = blend(target, share, source)
    from_last, blended = lax.optimization_barrier((from_last, blended))

    flow_high = flow_of(spectra_high, from_last, -1, half, nx, cols, back_cols, back_rows)
    off, flow_high = lax.optimization_barrier((off, flow_high))
    flow_high = from_behind(flow_high, "sec", -1)
    off = beyond(off)
    flow_low = flow_of(spectra_low, from_next, 1, half, nx, cols, back_cols, back_rows)
    flow = jnp.concatenate([flow_low, flow_high], axis=1)
    flow = jnp.concatenate([flow, node_mask.astype(jnp.float32) + 1.0], axis=0)
    flow_off = beyond(flow)
    flow_on = swapped(flow)
    flows = (flow_low, flow_high, node_mask, flow_on, flow_off)
    edges = edges_of(tile, target, share, on, off, blended)
    return tuple(warp(tile, flows, blended, edges))


def solution(mesh):
    return jax.shard_map(
        per_device,
        mesh=mesh,
        in_specs=(
            P("sec", None, "tile", None, None),
            P("sec", None, "tile"),
            P("sec", None, "tile", None),
            P("sec", None, "tile", None),
            P("sec", None, "tile"),
            P("sec", None, "tile", None),
        ),
        out_specs=(P("sec", None, "tile", None, None), P("sec", None, None, "tile")),
        check_vma=False,
    )
```

```python
import functools

import jax
import jax.numpy as jnp
import numpy as np
from jax import lax
from jax.experimental import pallas as pl
from jax.experimental.pallas import tpu as pltpu
from jax.sharding import PartitionSpec as P

K = 4
HB = 2
STEPS = 3
N = 128
HALF = N // 2
PAD = 72
ROW = 32
DEPTH = 2
SPRING = 0.2
EPS = 1e-06
MIB = 1024 * 1024


def split(x):
    high = x.astype(jnp.bfloat16)
    return high, (x - high.astype(jnp.float32)).astype(jnp.bfloat16)


def tables():
    grid = np.arange(N)[:, None] * np.arange(N)[None, :] % N
    cosine = np.cos(2.0 * np.pi * grid / N)
    sine = np.sin(2.0 * np.pi * grid / N)
    rows = np.concatenate([cosine[:HALF], sine[:HALF]])
    rows[HALF] = cosine[HALF]
    cols = np.block([[cosine, -sine], [-sine, -cosine]])
    back_cols = np.block([[cosine, sine], [-sine, cosine]]) / N
    weight = np.where(np.arange(HALF) == 0, 1.0, 2.0)
    back_rows = np.concatenate([cosine[:, :HALF] * weight, -2.0 * sine[:, :HALF]], axis=1) / N
    back_rows[:, HALF] = cosine[:, HALF] / N
    return [jnp.asarray(t, jnp.float32) for t in (rows, cols, back_cols, back_rows)]


def first_row(shape):
    return lax.broadcasted_iota(jnp.int32, shape, len(shape) - 2) == 0


def dot(a, b):
    return jnp.dot(a, b, preferred_element_type=jnp.float32)


def ahead(fetch, rows, depth):
    y = pl.program_id(0)

    @pl.when(y == 0)
    def _():
        for row in range(depth):
            for copy in fetch(row):
                copy.start()

    @pl.when(y + depth < rows)
    def _():
        for copy in fetch(y + depth):
            copy.start()

    for copy in fetch(y):
        copy.wait()


def in_hbm(x):
    return pltpu.with_memory_space_constraint(x, pltpu.HBM)


def in_vmem(x):
    return pltpu.with_memory_space_constraint(x, pltpu.VMEM)


def wait_all(copies):
    @pl.when(pl.program_id(0) == pl.num_programs(0) - 1)
    def _():
        for copy in copies:
            copy.wait()


def forward_kernel(start, toward_pair, tile_ref, x_hbm, rows_hbm, cols_hbm, *refs):
    *_, spec_ref, src_ref, strip_ref, x_ref, rest_ref, lines_ref, ends_ref, rows_ref, cols_ref, in_sems, more_sems = refs
    y = pl.program_id(0)
    count, patches = x_ref.shape[:2]
    ny = strip_ref.shape[0]
    odd = tile_ref[0] % 2
    column = ((1 - odd) if toward_pair else odd) * (patches - HB)
    rest = (start + count) % ny
    fetch = lambda row: [pltpu.make_async_copy(x_hbm.at[0, start + row], x_ref.at[row], in_sems.at[row])]
    more = [
        pltpu.make_async_copy(rows_hbm, rows_ref, more_sems.at[0]),
        pltpu.make_async_copy(cols_hbm, cols_ref, more_sems.at[1]),
        pltpu.make_async_copy(
            x_hbm.at[0, pl.ds(rest, ny - count), pl.ds(column, HB)], rest_ref, more_sems.at[2]
        ),
    ]

    @pl.when(y == 0)
    def _():
        for copy in more[:2]:
            copy.start()

    ahead(fetch, count, min(DEPTH, count))

    @pl.when(y == 0)
    def _():
        for copy in more[:2]:
            copy.wait()
        more[2].start()

    @pl.when(y == count - 1)
    def _():
        more[2].wait()
        strip_ref[rest : rest + ny - count] = rest_ref[...].astype(jnp.bfloat16)

    for i in range(HB):
        strip_ref[start + y, i] = x_ref[y, column + i].astype(jnp.bfloat16)
    rows2 = rows_ref[...]
    cols = cols_ref[...]
    for pair in range(patches // 2):
        x = jnp.concatenate([x_ref[y, 2 * pair], x_ref[y, 2 * pair + 1]], axis=1)
        high, low = split(x)
        src_ref[start + y, 2 * pair] = high[:, :N]
        src_ref[start + y, 2 * pair + 1] = high[:, N:]
        both = dot(rows2, jnp.concatenate([high, low], axis=0))
        for side in range(2):
            here = both[:, side * N : (side + 1) * N]
            p = 2 * pair + side
            ends_ref[p : p + 1, :N] = here[:1]
            ends_ref[p : p + 1, N:] = here[HALF : HALF + 1]
            lines_ref[p * HALF : (p + 1) * HALF, :N] = here[:HALF].astype(jnp.bfloat16)
            lines_ref[p * HALF : (p + 1) * HALF, N:] = here[HALF:].astype(jnp.bfloat16)
    step = 4
    for first in range(0, patches, step):
        lines = lines_ref[first * HALF : (first + step) * HALF, :]
        freq = dot(lines, cols).reshape(step, HALF, 2 * N)
        spec_ref[pl.ds(y * patches + first, step)] = freq.astype(jnp.bfloat16)
    ends = ends_ref[...].astype(jnp.bfloat16)
    spec_ref[count * patches, pl.ds(pl.multiple_of(y * patches, patches), patches), :] = ends


def forward(tile, sections, start, count, toward_pair, source, rows, cols):
    _, ny, nx, _, _ = sections.shape
    rows2 = jnp.concatenate([rows, rows], axis=1).astype(jnp.bfloat16)
    spectra = (count * nx + 1, HALF, 2 * N)
    before = () if source is None else (in_vmem(source),)
    return pl.pallas_call(
        functools.partial(forward_kernel, start, toward_pair),
        grid=(count,),
        in_specs=[pl.BlockSpec(memory_space=pltpu.SMEM)]
        + [pl.BlockSpec(memory_space=pltpu.HBM)] * 3
        + [pl.BlockSpec(memory_space=pltpu.VMEM)] * len(before),
        out_specs=[pl.BlockSpec(memory_space=pltpu.VMEM)] * 3,
        out_shape=[
            pltpu.VMEM(spectra, jnp.bfloat16),
            pltpu.VMEM((ny, nx, N, N), jnp.bfloat16),
            pltpu.VMEM((ny, HB, N, N), jnp.bfloat16),
        ],
        scratch_shapes=[
            pltpu.VMEM((count, nx, N, N), jnp.float32),
            pltpu.VMEM((ny - count, HB, N, N), jnp.float32),
            pltpu.VMEM((nx * HALF, 2 * N), jnp.bfloat16),
            pltpu.VMEM((nx, 2 * N), jnp.float32),
            pltpu.VMEM((N, 2 * N), jnp.bfloat16),
            pltpu.VMEM((2 * N, 2 * N), jnp.bfloat16),
            pltpu.SemaphoreType.DMA((count,)),
            pltpu.SemaphoreType.DMA((3,)),
        ],
        input_output_aliases={4: 1} if before else {},
        compiler_params=pltpu.CompilerParams(vmem_limit_bytes=12 * MIB),
        cost_estimate=pl.CostEstimate(flops=2_000_000_000, bytes_accessed=6 * MIB, transcendentals=0),
        name="forward",
    )(tile, in_hbm(sections), in_hbm(rows2), in_hbm(cols.astype(jnp.bfloat16)), *before)


def times_conj(a, b, sign):
    ar, ai, br, bi = a[:, :N], a[:, N:], b[:, :N], b[:, N:]
    real = ar * br + ai * bi
    imag = ai * br - ar * bi if sign > 0 else ar * bi - ai * br
    return jnp.concatenate([real, imag], axis=1).astype(jnp.bfloat16)


def flow_kernel(sign, own, other, cols_ref, back_cols_ref, back_rows_ref, flow_ref, sides, sums, moments):
    y = pl.program_id(0)
    ny, patches = sums.shape[:2]
    last = ny * patches
    cols = cols_ref[...]
    back_cols = back_cols_ref[...]
    back_rows = back_rows_ref[...]

    @pl.when(y == 0)
    def _():
        lines = jnp.concatenate([own[last], other[last]], axis=0)
        edge = dot(jnp.concatenate([lines[:, :N], lines[:, N:]], axis=0), cols[:N])
        quarter = edge.reshape(4, last, 2 * N)
        low = times_conj(quarter[0], quarter[1], sign)
        high = times_conj(quarter[2], quarter[3], sign)
        back = dot(jnp.concatenate([low, high], axis=0), back_cols[:, :N])
        sides[...] = back.reshape(sides.shape)

    shift_rows = lax.broadcasted_iota(jnp.int32, (N, N), 0)
    offset_rows = (((shift_rows + HALF) % N) - HALF).astype(jnp.float32)
    offset_rows = jnp.concatenate([offset_rows, offset_rows], axis=1)
    step = 4
    for first in range(0, patches, step):
        here = pl.ds(y * patches + first, step)
        a = own[here].reshape(step * HALF, 2 * N).astype(jnp.float32)
        b = other[here].reshape(step * HALF, 2 * N).astype(jnp.float32)
        back = dot(times_conj(a, b, sign), back_cols)
        halves = []
        for i in range(step):
            p = first + i
            parts = []
            for side in range(2):
                part = back[i * HALF : (i + 1) * HALF, side * N : (side + 1) * N]
                top = jnp.where(first_row((16, N)), sides[side, y, p : p + 1, :], part[:16])
                parts += [top.astype(jnp.bfloat16), part[16:].astype(jnp.bfloat16)]
            halves.append(jnp.concatenate(parts, axis=0))
        for i in range(0, step, 2):
            corr = dot(back_rows, jnp.concatenate(halves[i : i + 2], axis=1))
            power = corr * corr
            total = power.sum(0, keepdims=True)
            moment = (power * offset_rows).sum(0, keepdims=True)
            for side in range(2):
                p = first + i + side
                sums[y, p : p + 1, :] = total[:, side * N : (side + 1) * N]
                moments[y, p : p + 1, :] = moment[:, side * N : (side + 1) * N]

    @pl.when(y == ny - 1)
    def _():
        lane = lax.broadcasted_iota(jnp.int32, (8, N), 1)
        row = lax.broadcasted_iota(jnp.int32, (8, N), 0)
        offset_cols = (((lane + HALF) % N) - HALF).astype(jnp.float32)
        reduce_by = jnp.where(row == 0, 1.0, jnp.where(row == 1, offset_cols, 0.0))
        over_lanes = lambda m: lax.dot_general(
            reduce_by, m.reshape(last, N), (((1,), (1,)), ((), ())),
            precision=lax.Precision.HIGHEST, preferred_element_type=jnp.float32,
        )
        by_sums = over_lanes(sums[...])
        by_moments = over_lanes(moments[...])
        total = by_sums[0:1] + EPS
        along_rows = by_moments[0:1] / total
        along_cols = by_sums[1:2] / total
        for row in range(ny):
            flow_ref[0, row : row + 1, :] = along_rows[:, row * patches : (row + 1) * patches]
            flow_ref[1, row : row + 1, :] = along_cols[:, row * patches : (row + 1) * patches]


def flow_of(own, other, sign, ny, nx, cols, back_cols, back_rows):
    whole = lambda shape: pl.BlockSpec(shape, lambda y: (0,) * len(shape))
    return pl.pallas_call(
        functools.partial(flow_kernel, sign),
        grid=(ny,),
        in_specs=[
            pl.BlockSpec(memory_space=pltpu.VMEM),
            pl.BlockSpec(memory_space=pltpu.VMEM),
            whole((2 * N, 2 * N)),
            whole((2 * N, 2 * N)),
            whole((N, N)),
        ],
        out_specs=whole((2, ny, nx)),
        out_shape=jax.ShapeDtypeStruct((2, ny, nx), jnp.float32),
        scratch_shapes=[
            pltpu.VMEM((2, ny, nx, N), jnp.float32),
            pltpu.VMEM((ny, nx, N), jnp.float32),
            pltpu.VMEM((ny, nx, N), jnp.float32),
        ],
        compiler_params=pltpu.CompilerParams(vmem_limit_bytes=8 * MIB),
        cost_estimate=pl.CostEstimate(flops=0 if sign < 0 else 50_000_000_000, bytes_accessed=0, transcendentals=0),
        name="flow",
    )(in_vmem(own), in_vmem(other), *(t.astype(jnp.bfloat16) for t in (cols, back_cols, back_rows)))


def slots_kernel(tile_ref, rows_ref, shifts_ref, count_ref, weight_ref, target_ref, share_ref):
    ny, _, nx = rows_ref.shape[1:]
    tile, tiles = tile_ref[0], tile_ref[1]
    live = [k < count_ref[0] for k in range(K)]
    weights = [jnp.where(live[k], weight_ref[0, :, k, :], 0.0) for k in range(K)]
    total = weights[0] + weights[1] + weights[2] + weights[3]
    share = [(w / total).astype(jnp.bfloat16).astype(jnp.float32) for w in weights]
    columns = [lax.broadcasted_iota(jnp.int32, (ny, nx), 1) + shifts_ref[0, :, k, :] for k in range(K)]
    rows = [rows_ref[0, :, k, :] * ROW for k in range(K)]
    low = [c < 0 for c in columns]
    high = [c >= nx for c in columns]
    first, last = tile == 0, tile == tiles - 1
    inside = [jnp.where(l | h, 0.0, s) for l, h, s in zip(low, high, share, strict=True)]
    share_low = [jnp.where(first, 0.0, jnp.where(l, s, 0.0)) for l, s in zip(low, share, strict=True)]
    share_high = [jnp.where(last, 0.0, jnp.where(h, s, 0.0)) for h, s in zip(high, share, strict=True)]
    beyond = [l + h for l, h in zip(share_low, share_high, strict=True)]
    share_ref[...] = jnp.concatenate(inside + beyond, axis=1)
    target = [r + jnp.where(l | h, 0, c) for r, c, l, h in zip(rows, columns, low, high, strict=True)]
    away = [
        r + jnp.where(l, c + HB, jnp.where(h, c - nx + HB, 0))
        for r, c, l, h in zip(rows, columns, low, high, strict=True)
    ]
    target_ref[...] = jnp.concatenate(target + away, axis=1)


def slots_of(tile, box_row, box_shift, box_count, blend_weight):
    ny = box_row.shape[1]
    slots_first = lambda x: jnp.transpose(x, (0, 1, 3, 2))
    return pl.pallas_call(
        slots_kernel,
        in_specs=[pl.BlockSpec(memory_space=pltpu.SMEM)] + [pl.BlockSpec(memory_space=pltpu.VMEM)] * 4,
        out_shape=[
            jax.ShapeDtypeStruct((ny, N), jnp.int32),
            jax.ShapeDtypeStruct((ny, N), jnp.float32),
        ],
        compiler_params=pltpu.CompilerParams(vmem_limit_bytes=4 * MIB),
        cost_estimate=pl.CostEstimate(flops=0, bytes_accessed=0, transcendentals=0),
        name="slots",
    )(tile, slots_first(box_row), slots_first(box_shift), box_count, slots_first(blend_weight))


def blend_cell(y, first, nx, target_ref, share_ref, window):
    total = None
    for k in range(K):
        spot = target_ref[y, first + k * nx]
        piece = window[spot // ROW, spot % ROW].astype(jnp.float32) * share_ref[y, first + k * nx]
        total = piece if total is None else total + piece
    return total


def blend_kernel(target_ref, share_ref, source, out_ref):
    y = pl.program_id(0)
    nx = source.shape[1]
    border = jnp.zeros((nx, PAD, N), jnp.float32)
    out_ref[y, :, :PAD] = border
    out_ref[y, :, PAD + N :] = border
    for x in range(nx):
        out_ref[y, x, PAD : PAD + N] = blend_cell(y, x, nx, target_ref, share_ref, source)


def blend(target, share, source):
    ny, nx = source.shape[:2]
    return pl.pallas_call(
        blend_kernel,
        grid=(ny,),
        in_specs=[pl.BlockSpec(memory_space=pltpu.SMEM)] * 2 + [pl.BlockSpec(memory_space=pltpu.VMEM)],
        out_specs=pl.BlockSpec(memory_space=pltpu.VMEM),
        out_shape=pltpu.VMEM((ny, nx, N + 2 * PAD, N), jnp.float32),
        compiler_params=pltpu.CompilerParams(vmem_limit_bytes=4 * MIB),
        cost_estimate=pl.CostEstimate(flops=20_000_000_000, bytes_accessed=4 * MIB, transcendentals=0),
        name="blend",
    )(target, share, in_vmem(source))


def relax(tile_ref, low_ref, high_ref, mask_ref, on_ref, off_ref):
    ny, nx = mask_ref.shape[1:]
    even = tile_ref[0] % 2 == 0
    left_ref = [jnp.where(even, off_ref[i], on_ref[i]) for i in range(3)]
    right_ref = [jnp.where(even, on_ref[i], off_ref[i]) for i in range(3)]
    rest = jnp.zeros((ny, N - nx - 2 * STEPS), jnp.float32)

    def across(left, own, right):
        return jnp.concatenate([left[:, nx - STEPS :], own, right[:, :STEPS], rest], axis=1)

    known = across(left_ref[2], mask_ref[0].astype(jnp.float32) + 1.0, right_ref[2])
    valid = jnp.where(known > 0.5, 1.0, 0.0)
    trust = jnp.where(known > 1.5, 1.0, 0.0)
    row = lax.broadcasted_iota(jnp.int32, trust.shape, 0)
    fields = []
    for component in range(2):
        own = jnp.concatenate([low_ref[component], high_ref[component]], axis=0)
        flow = across(left_ref[component], own, right_ref[component])
        field = trust * flow
        for _ in range(STEPS):
            below = jnp.where(row == 0, 0.0, pltpu.roll(field, 1, 0))
            above = jnp.where(row == ny - 1, 0.0, pltpu.roll(field, ny - 1, 0))
            beside = pltpu.roll(field, 1, 1) + pltpu.roll(field, N - 1, 1)
            lap = above + below + beside - 4.0 * field
            field = (field + SPRING * (lap + trust * (flow - field))) * valid
        fields.append(field)
    return fields


def edge_kernel(tile_ref, target_ref, share_ref, on_ref, off_ref, padded, out_ref, window, sems):
    y = pl.program_id(0)
    ny, nx = padded.shape[:2]
    even = tile_ref[0] % 2 == 0
    halos = {True: ((on_ref, HB), (off_ref, 0)), False: ((on_ref, 0), (off_ref, HB))}
    copies = {
        side: [
            pltpu.make_async_copy(ref, window.at[:, into : into + HB], sems.at[i])
            for i, (ref, into) in enumerate(places)
        ]
        for side, places in halos.items()
    }

    @pl.when((y == 0) & even)
    def _():
        for copy in copies[True]:
            copy.start()

    @pl.when((y == 0) & jnp.logical_not(even))
    def _():
        for copy in copies[False]:
            copy.start()

    border = jnp.zeros((2 * HB, PAD, N), jnp.float32)
    out_ref[y, :, :PAD] = border
    out_ref[y, :, PAD + N :] = border

    @pl.when(y == 0)
    def _():
        for copy in copies[True]:
            copy.wait()

    for i, x in enumerate((*range(HB), *range(nx - HB, nx))):
        more = blend_cell(y, K * nx + x, nx, target_ref, share_ref, window)
        out_ref[y, i, PAD : PAD + N] = padded[y, x, PAD : PAD + N] + more


def edges_of(tile, target, share, on, off, blended):
    ny, _, tall, _ = blended.shape
    vmem = pl.BlockSpec(memory_space=pltpu.VMEM)
    return pl.pallas_call(
        edge_kernel,
        grid=(ny,),
        in_specs=[pl.BlockSpec(memory_space=pltpu.SMEM)] * 3 + [vmem] * 3,
        out_specs=vmem,
        out_shape=pltpu.VMEM((ny, 2 * HB, tall, N), jnp.float32),
        scratch_shapes=[pltpu.VMEM((ny, 2 * HB, N, N), jnp.bfloat16), pltpu.SemaphoreType.DMA((2,))],
        compiler_params=pltpu.CompilerParams(vmem_limit_bytes=4 * MIB),
        cost_estimate=pl.CostEstimate(flops=5_000_000, bytes_accessed=4 * MIB, transcendentals=0),
        name="edges",
    )(tile, target, share, in_vmem(on), in_vmem(off), in_vmem(blended))


def warped(cell, down_shift, right_shift):
    whole_of = lambda shift: (shift + 256.0).astype(jnp.int32) - 256
    line = lambda value: jnp.full((1, N), value, jnp.float32).astype(jnp.bfloat16)
    down = jnp.clip(whole_of(down_shift), 4 - PAD, PAD - 6)
    part = down_shift - down.astype(jnp.float32)
    upper = cell[pl.ds(PAD + down, N), :]
    lower = cell[pl.ds(PAD + 1 + down, N), :]
    image = upper + part * (lower - upper)
    right = whole_of(right_shift).astype(jnp.float32)
    apart = lax.broadcasted_iota(jnp.int32, (N, N), 0) - lax.broadcasted_iota(jnp.int32, (N, N), 1)
    apart = apart.astype(jnp.bfloat16) - line(right)
    one = jnp.bfloat16(1.0)
    hat = jnp.maximum(jnp.bfloat16(0.0), one - jnp.abs(apart - line(right_shift - right)))
    return dot(image.astype(jnp.bfloat16), hat).astype(jnp.bfloat16)


def warp_kernel(tile_ref, *refs):
    *flows, padded, edges, out_hbm, field_ref, out, wide, field, sem, out_sems = refs
    y = pl.program_id(0)
    ny, nx = out.shape[:2]

    @pl.when(y == 0)
    def _():
        for component, values in enumerate(relax(tile_ref, *flows)):
            wide[component] = values
            field_ref[0, component] = values[:, STEPS : STEPS + nx]
        scalars = pltpu.make_async_copy(wide, field, sem)
        scalars.start()
        scalars.wait()

    borders = (*range(HB), *range(nx - HB, nx))
    for x in range(nx):
        cell = edges.at[y, borders.index(x)] if x in borders else padded.at[y, x]
        out[y, x] = warped(cell, field[0, y, STEPS + x], field[1, y, STEPS + x])
    store = lambda row: pltpu.make_async_copy(out.at[row], out_hbm.at[0, row], out_sems.at[row])
    store(y).start()
    wait_all([store(row) for row in range(ny)])


def warp(tile, flows, blended, edges):
    ny, nx = blended.shape[:2]
    whole = lambda shape: pl.BlockSpec(shape, lambda y: (0,) * len(shape))
    return pl.pallas_call(
        warp_kernel,
        grid=(ny,),
        in_specs=[pl.BlockSpec(memory_space=pltpu.SMEM)]
        + [whole(x.shape) for x in flows]
        + [pl.BlockSpec(memory_space=pltpu.VMEM)] * 2,
        out_specs=[pl.BlockSpec(memory_space=pl.ANY), whole((1, 2, ny, nx))],
        out_shape=[
            jax.ShapeDtypeStruct((1, ny, nx, N, N), jnp.bfloat16),
            jax.ShapeDtypeStruct((1, 2, ny, nx), jnp.float32),
        ],
        scratch_shapes=[
            pltpu.VMEM((ny, nx, N, N), jnp.bfloat16),
            pltpu.VMEM((2, ny, N), jnp.float32),
            pltpu.SMEM((2, ny, N), jnp.float32),
            pltpu.SemaphoreType.DMA,
            pltpu.SemaphoreType.DMA((ny,)),
        ],
        compiler_params=pltpu.CompilerParams(vmem_limit_bytes=8 * MIB),
        cost_estimate=pl.CostEstimate(flops=20_000_000, bytes_accessed=12 * MIB, transcendentals=0),
        name="warp",
    )(tile, *flows, in_vmem(blended), in_vmem(edges))


def from_behind(x, axis, by):
    length = lax.axis_size(axis)
    pairs = [(i, i + by) for i in range(length) if 0 <= i + by < length]
    return lax.ppermute(x, axis, pairs)


def swapped(x):
    return lax.ppermute(x, "tile", [(i, i ^ 1) for i in range(lax.axis_size("tile"))])


def hops(tiles, sections):
    pairs = ([], [])
    for section in range(sections):
        x_low, rest = divmod(section, sections // 2)
        way = 1 if rest < sections // 4 else -1
        for tile in range(tiles):
            z, x_high = divmod(tile, 2)
            ends = [section * tiles + tile]
            for hop in (1, 2):
                x = (2 * x_high + x_low + hop * way) % 4
                to_z = (z + 2 * x_high - 1) % (tiles // 2) if hop == 2 else z
                ends.append((x % 2 * (sections // 2) + rest) * tiles + 2 * to_z + x // 2)
            pairs[0].append((ends[0], ends[1]))
            pairs[1].append((ends[1], ends[2]))
    return pairs


def beyond(x):
    tiles = lax.axis_size("tile")
    pairs = [(i, i + 1) for i in range(1, tiles - 1, 2)]
    return lax.ppermute(x, "tile", pairs + [(j, i) for i, j in pairs])


def per_device(sections, node_mask, box_row, box_shift, box_count, blend_weight):
    ny, nx = sections.shape[1:3]
    rows, cols, back_cols, back_rows = tables()
    half = ny // 2
    tiles, count = lax.axis_size("tile"), lax.axis_size("sec")
    tile = jnp.stack([lax.axis_index("tile"), tiles]).astype(jnp.int32)
    off_hops = hops(tiles, count)
    hop = lambda x, pairs: lax.ppermute(x, ("sec", "tile"), pairs)

    spectra_high, source, off = forward(tile, sections, half, half, False, None, rows, cols)
    from_last = from_behind(spectra_high, "sec", 1)
    off = hop(off, off_hops[0])
    spectra_low, source, on = forward(tile, sections, 0, half, True, source, rows, cols)
    from_next = from_behind(spectra_low, "sec", -1)
    target, share = slots_of(tile, box_row, box_shift, box_count, blend_weight)
    off, source = lax.optimization_barrier((off, source))
    off = hop(off, off_hops[1])
    blended = blend(target, share, source)
    from_last, blended = lax.optimization_barrier((from_last, blended))

    flow_high = flow_of(spectra_high, from_last, -1, half, nx, cols, back_cols, back_rows)
    on, off, flow_high = lax.optimization_barrier((on, off, flow_high))
    flow_high = from_behind(flow_high, "sec", -1)
    from_next, flow_high = lax.optimization_barrier((from_next, flow_high))
    flow_low = flow_of(spectra_low, from_next, 1, half, nx, cols, back_cols, back_rows)
    on = swapped(on)
    flow = jnp.concatenate([flow_low, flow_high], axis=1)
    flow = jnp.concatenate([flow, node_mask.astype(jnp.float32) + 1.0], axis=0)
    flow_off = beyond(flow)
    flow_on = swapped(flow)
    flows = (flow_low, flow_high, node_mask, flow_on, flow_off)
    edges = edges_of(tile, target, share, on, off, blended)
    return tuple(warp(tile, flows, blended, edges))


def solution(mesh):
    return jax.shard_map(
        per_device,
        mesh=mesh,
        in_specs=(
            P("sec", None, "tile", None, None),
            P("sec", None, "tile"),
            P("sec", None, "tile", None),
            P("sec", None, "tile", None),
            P("sec", None, "tile"),
            P("sec", None, "tile", None),
        ),
        out_specs=(P("sec", None, "tile", None, None), P("sec", None, None, "tile")),
        check_vma=False,
    )
```

```python
import functools

import jax
import jax.numpy as jnp
import numpy as np
from jax import lax
from jax.experimental import pallas as pl
from jax.experimental.pallas import tpu as pltpu
from jax.sharding import PartitionSpec as P

K = 4
HB = 2
STEPS = 3
N = 128
HALF = N // 2
PAD = 72
ROW = 32
DEPTH = 2
SPRING = 0.2
EPS = 1e-06
MIB = 1024 * 1024


def split(x):
    high = x.astype(jnp.bfloat16)
    return high, (x - high.astype(jnp.float32)).astype(jnp.bfloat16)


def tables():
    grid = np.arange(N)[:, None] * np.arange(N)[None, :] % N
    cosine = np.cos(2.0 * np.pi * grid / N)
    sine = np.sin(2.0 * np.pi * grid / N)
    rows = np.concatenate([cosine[:HALF], sine[:HALF]])
    rows[HALF] = cosine[HALF]
    cols = np.block([[cosine, -sine], [-sine, -cosine]])
    back_cols = np.block([[cosine, sine], [-sine, cosine]]) / N
    weight = np.where(np.arange(HALF) == 0, 1.0, 2.0)
    back_rows = np.concatenate([cosine[:, :HALF] * weight, -2.0 * sine[:, :HALF]], axis=1) / N
    back_rows[:, HALF] = cosine[:, HALF] / N
    return [jnp.asarray(t, jnp.float32) for t in (rows, cols, back_cols, back_rows)]


def first_row(shape):
    return lax.broadcasted_iota(jnp.int32, shape, len(shape) - 2) == 0


def dot(a, b):
    return jnp.dot(a, b, preferred_element_type=jnp.float32)


def ahead(fetch, rows, depth):
    y = pl.program_id(0)

    @pl.when(y == 0)
    def _():
        for row in range(depth):
            for copy in fetch(row):
                copy.start()

    @pl.when(y + depth < rows)
    def _():
        for copy in fetch(y + depth):
            copy.start()

    for copy in fetch(y):
        copy.wait()


def in_hbm(x):
    return pltpu.with_memory_space_constraint(x, pltpu.HBM)


def in_vmem(x):
    return pltpu.with_memory_space_constraint(x, pltpu.VMEM)


def wait_all(copies):
    @pl.when(pl.program_id(0) == pl.num_programs(0) - 1)
    def _():
        for copy in copies:
            copy.wait()


def forward_kernel(start, toward_pair, tile_ref, x_hbm, rows_hbm, cols_hbm, *refs):
    *refs, x_ref, rest_ref, lines_ref, ends_ref, rows_ref, cols_ref, in_sems, more_sems = refs
    spec_ref, src_ref, *strip_refs = refs[-2 - (HB if toward_pair else 1) :]
    y = pl.program_id(0)
    count, patches = x_ref.shape[:2]
    ny = src_ref.shape[0]
    odd = tile_ref[0] % 2
    column = ((1 - odd) if toward_pair else odd) * (patches - HB)
    rest = (start + count) % ny
    fetch = lambda row: [pltpu.make_async_copy(x_hbm.at[0, start + row], x_ref.at[row], in_sems.at[row])]
    to_strip = lambda i: strip_refs[i].at[:, 0] if toward_pair else strip_refs[0].at[:, i]
    more = [
        pltpu.make_async_copy(rows_hbm, rows_ref, more_sems.at[0]),
        pltpu.make_async_copy(cols_hbm, cols_ref, more_sems.at[1]),
        pltpu.make_async_copy(
            x_hbm.at[0, pl.ds(rest, ny - count), pl.ds(column, HB)], rest_ref, more_sems.at[2]
        ),
    ]

    @pl.when(y == 0)
    def _():
        for copy in more[:2]:
            copy.start()

    ahead(fetch, count, min(DEPTH, count))

    @pl.when(y == 0)
    def _():
        for copy in more[:2]:
            copy.wait()
        more[2].start()

    @pl.when(y == count - 1)
    def _():
        more[2].wait()
        for i in range(HB):
            to_strip(i)[rest : rest + ny - count] = rest_ref[:, i].astype(jnp.bfloat16)

    for i in range(HB):
        to_strip(i)[start + y] = x_ref[y, column + i].astype(jnp.bfloat16)
    rows2 = rows_ref[...]
    cols = cols_ref[...]
    for pair in range(patches // 2):
        x = jnp.concatenate([x_ref[y, 2 * pair], x_ref[y, 2 * pair + 1]], axis=1)
        high, low = split(x)
        src_ref[start + y, 2 * pair] = high[:, :N]
        src_ref[start + y, 2 * pair + 1] = high[:, N:]
        both = dot(rows2, jnp.concatenate([high, low], axis=0))
        for side in range(2):
            here = both[:, side * N : (side + 1) * N]
            p = 2 * pair + side
            ends_ref[p : p + 1, :N] = here[:1]
            ends_ref[p : p + 1, N:] = here[HALF : HALF + 1]
            lines_ref[p * HALF : (p + 1) * HALF, :N] = here[:HALF].astype(jnp.bfloat16)
            lines_ref[p * HALF : (p + 1) * HALF, N:] = here[HALF:].astype(jnp.bfloat16)
    step = 4
    for first in range(0, patches, step):
        lines = lines_ref[first * HALF : (first + step) * HALF, :]
        freq = dot(lines, cols).reshape(step, HALF, 2 * N)
        spec_ref[pl.ds(y * patches + first, step)] = freq.astype(jnp.bfloat16)
    ends = ends_ref[...].astype(jnp.bfloat16)
    spec_ref[count * patches, pl.ds(pl.multiple_of(y * patches, patches), patches), :] = ends


def forward(tile, sections, start, count, toward_pair, source, rows, cols):
    _, ny, nx, _, _ = sections.shape
    rows2 = jnp.concatenate([rows, rows], axis=1).astype(jnp.bfloat16)
    spectra = (count * nx + 1, HALF, 2 * N)
    before = () if source is None else (in_vmem(source),)
    strips = (1,) * HB if toward_pair else (HB,)
    return pl.pallas_call(
        functools.partial(forward_kernel, start, toward_pair),
        grid=(count,),
        in_specs=[pl.BlockSpec(memory_space=pltpu.SMEM)]
        + [pl.BlockSpec(memory_space=pltpu.HBM)] * 3
        + [pl.BlockSpec(memory_space=pltpu.VMEM)] * len(before),
        out_specs=[pl.BlockSpec(memory_space=pltpu.VMEM)] * (2 + len(strips)),
        out_shape=[
            pltpu.VMEM(spectra, jnp.bfloat16),
            pltpu.VMEM((ny, nx, N, N), jnp.bfloat16),
            *(pltpu.VMEM((ny, wide, N, N), jnp.bfloat16) for wide in strips),
        ],
        scratch_shapes=[
            pltpu.VMEM((count, nx, N, N), jnp.float32),
            pltpu.VMEM((ny - count, HB, N, N), jnp.float32),
            pltpu.VMEM((nx * HALF, 2 * N), jnp.bfloat16),
            pltpu.VMEM((nx, 2 * N), jnp.float32),
            pltpu.VMEM((N, 2 * N), jnp.bfloat16),
            pltpu.VMEM((2 * N, 2 * N), jnp.bfloat16),
            pltpu.SemaphoreType.DMA((count,)),
            pltpu.SemaphoreType.DMA((3,)),
        ],
        input_output_aliases={4: 1} if before else {},
        compiler_params=pltpu.CompilerParams(vmem_limit_bytes=12 * MIB),
        cost_estimate=pl.CostEstimate(flops=2_000_000_000, bytes_accessed=6 * MIB, transcendentals=0),
        name="forward",
    )(tile, in_hbm(sections), in_hbm(rows2), in_hbm(cols.astype(jnp.bfloat16)), *before)


def times_conj(a, b, sign):
    ar, ai, br, bi = a[:, :N], a[:, N:], b[:, :N], b[:, N:]
    real = ar * br + ai * bi
    imag = ai * br - ar * bi if sign > 0 else ar * bi - ai * br
    return jnp.concatenate([real, imag], axis=1).astype(jnp.bfloat16)


def flow_kernel(sign, own, other, cols_ref, back_cols_ref, back_rows_ref, flow_ref, sides, sums, moments):
    y = pl.program_id(0)
    ny, patches = sums.shape[:2]
    last = ny * patches
    cols = cols_ref[...]
    back_cols = back_cols_ref[...]
    back_rows = back_rows_ref[...]

    @pl.when(y == 0)
    def _():
        lines = jnp.concatenate([own[last], other[last]], axis=0)
        edge = dot(jnp.concatenate([lines[:, :N], lines[:, N:]], axis=0), cols[:N])
        quarter = edge.reshape(4, last, 2 * N)
        low = times_conj(quarter[0], quarter[1], sign)
        high = times_conj(quarter[2], quarter[3], sign)
        back = dot(jnp.concatenate([low, high], axis=0), back_cols[:, :N])
        sides[...] = back.reshape(sides.shape)

    shift_rows = lax.broadcasted_iota(jnp.int32, (N, N), 0)
    offset_rows = (((shift_rows + HALF) % N) - HALF).astype(jnp.float32)
    offset_rows = jnp.concatenate([offset_rows, offset_rows], axis=1)
    step = 4
    for first in range(0, patches, step):
        here = pl.ds(y * patches + first, step)
        a = own[here].reshape(step * HALF, 2 * N).astype(jnp.float32)
        b = other[here].reshape(step * HALF, 2 * N).astype(jnp.float32)
        back = dot(times_conj(a, b, sign), back_cols)
        halves = []
        for i in range(step):
            p = first + i
            parts = []
            for side in range(2):
                part = back[i * HALF : (i + 1) * HALF, side * N : (side + 1) * N]
                top = jnp.where(first_row((16, N)), sides[side, y, p : p + 1, :], part[:16])
                parts += [top.astype(jnp.bfloat16), part[16:].astype(jnp.bfloat16)]
            halves.append(jnp.concatenate(parts, axis=0))
        for i in range(0, step, 2):
            corr = dot(back_rows, jnp.concatenate(halves[i : i + 2], axis=1))
            power = corr * corr
            total = power.sum(0, keepdims=True)
            moment = (power * offset_rows).sum(0, keepdims=True)
            for side in range(2):
                p = first + i + side
                sums[y, p : p + 1, :] = total[:, side * N : (side + 1) * N]
                moments[y, p : p + 1, :] = moment[:, side * N : (side + 1) * N]

    @pl.when(y == ny - 1)
    def _():
        lane = lax.broadcasted_iota(jnp.int32, (8, N), 1)
        row = lax.broadcasted_iota(jnp.int32, (8, N), 0)
        offset_cols = (((lane + HALF) % N) - HALF).astype(jnp.float32)
        reduce_by = jnp.where(row == 0, 1.0, jnp.where(row == 1, offset_cols, 0.0))
        over_lanes = lambda m: lax.dot_general(
            reduce_by, m.reshape(last, N), (((1,), (1,)), ((), ())),
            precision=lax.Precision.HIGHEST, preferred_element_type=jnp.float32,
        )
        by_sums = over_lanes(sums[...])
        by_moments = over_lanes(moments[...])
        total = by_sums[0:1] + EPS
        along_rows = by_moments[0:1] / total
        along_cols = by_sums[1:2] / total
        for row in range(ny):
            flow_ref[0, row : row + 1, :] = along_rows[:, row * patches : (row + 1) * patches]
            flow_ref[1, row : row + 1, :] = along_cols[:, row * patches : (row + 1) * patches]


def flow_of(own, other, sign, ny, nx, cols, back_cols, back_rows):
    whole = lambda shape: pl.BlockSpec(shape, lambda y: (0,) * len(shape))
    return pl.pallas_call(
        functools.partial(flow_kernel, sign),
        grid=(ny,),
        in_specs=[
            pl.BlockSpec(memory_space=pltpu.VMEM),
            pl.BlockSpec(memory_space=pltpu.VMEM),
            whole((2 * N, 2 * N)),
            whole((2 * N, 2 * N)),
            whole((N, N)),
        ],
        out_specs=whole((2, ny, nx)),
        out_shape=jax.ShapeDtypeStruct((2, ny, nx), jnp.float32),
        scratch_shapes=[
            pltpu.VMEM((2, ny, nx, N), jnp.float32),
            pltpu.VMEM((ny, nx, N), jnp.float32),
            pltpu.VMEM((ny, nx, N), jnp.float32),
        ],
        compiler_params=pltpu.CompilerParams(vmem_limit_bytes=8 * MIB),
        cost_estimate=pl.CostEstimate(flops=0 if sign < 0 else 50_000_000_000, bytes_accessed=0, transcendentals=0),
        name="flow",
    )(in_vmem(own), in_vmem(other), *(t.astype(jnp.bfloat16) for t in (cols, back_cols, back_rows)))


def slots_kernel(tile_ref, rows_ref, shifts_ref, count_ref, weight_ref, target_ref, share_ref):
    ny, _, nx = rows_ref.shape[1:]
    tile, tiles = tile_ref[0], tile_ref[1]
    live = [k < count_ref[0] for k in range(K)]
    weights = [jnp.where(live[k], weight_ref[0, :, k, :], 0.0) for k in range(K)]
    total = weights[0] + weights[1] + weights[2] + weights[3]
    share = [(w / total).astype(jnp.bfloat16).astype(jnp.float32) for w in weights]
    columns = [lax.broadcasted_iota(jnp.int32, (ny, nx), 1) + shifts_ref[0, :, k, :] for k in range(K)]
    rows = [rows_ref[0, :, k, :] * ROW for k in range(K)]
    low = [c < 0 for c in columns]
    high = [c >= nx for c in columns]
    first, last = tile == 0, tile == tiles - 1
    inside = [jnp.where(l | h, 0.0, s) for l, h, s in zip(low, high, share, strict=True)]
    share_low = [jnp.where(first, 0.0, jnp.where(l, s, 0.0)) for l, s in zip(low, share, strict=True)]
    share_high = [jnp.where(last, 0.0, jnp.where(h, s, 0.0)) for h, s in zip(high, share, strict=True)]
    beyond = [l + h for l, h in zip(share_low, share_high, strict=True)]
    share_ref[...] = jnp.concatenate(inside + beyond, axis=1)
    target = [r + jnp.where(l | h, 0, c) for r, c, l, h in zip(rows, columns, low, high, strict=True)]
    away = [
        r + jnp.where(l, c + HB, jnp.where(h, c - nx + HB, 0))
        for r, c, l, h in zip(rows, columns, low, high, strict=True)
    ]
    target_ref[...] = jnp.concatenate(target + away, axis=1)


def slots_of(tile, box_row, box_shift, box_count, blend_weight):
    ny = box_row.shape[1]
    slots_first = lambda x: jnp.transpose(x, (0, 1, 3, 2))
    return pl.pallas_call(
        slots_kernel,
        in_specs=[pl.BlockSpec(memory_space=pltpu.SMEM)] + [pl.BlockSpec(memory_space=pltpu.VMEM)] * 4,
        out_shape=[
            jax.ShapeDtypeStruct((ny, N), jnp.int32),
            jax.ShapeDtypeStruct((ny, N), jnp.float32),
        ],
        compiler_params=pltpu.CompilerParams(vmem_limit_bytes=4 * MIB),
        cost_estimate=pl.CostEstimate(flops=0, bytes_accessed=0, transcendentals=0),
        name="slots",
    )(tile, slots_first(box_row), slots_first(box_shift), box_count, slots_first(blend_weight))


def blend_cell(y, first, nx, target_ref, share_ref, window):
    total = None
    for k in range(K):
        spot = target_ref[y, first + k * nx]
        piece = window[spot // ROW, spot % ROW].astype(jnp.float32) * share_ref[y, first + k * nx]
        total = piece if total is None else total + piece
    return total


def blend_kernel(target_ref, share_ref, source, out_ref):
    y = pl.program_id(0)
    nx = source.shape[1]
    border = jnp.zeros((nx, PAD, N), jnp.float32)
    out_ref[y, :, :PAD] = border
    out_ref[y, :, PAD + N :] = border
    for x in range(nx):
        out_ref[y, x, PAD : PAD + N] = blend_cell(y, x, nx, target_ref, share_ref, source)


def blend(target, share, source):
    ny, nx = source.shape[:2]
    return pl.pallas_call(
        blend_kernel,
        grid=(ny,),
        in_specs=[pl.BlockSpec(memory_space=pltpu.SMEM)] * 2 + [pl.BlockSpec(memory_space=pltpu.VMEM)],
        out_specs=pl.BlockSpec(memory_space=pltpu.VMEM),
        out_shape=pltpu.VMEM((ny, nx, N + 2 * PAD, N), jnp.float32),
        compiler_params=pltpu.CompilerParams(vmem_limit_bytes=4 * MIB),
        cost_estimate=pl.CostEstimate(flops=16_000_000_000, bytes_accessed=4 * MIB, transcendentals=0),
        name="blend",
    )(target, share, in_vmem(source))


def relax(tile_ref, low_ref, high_ref, mask_ref, on_ref, off_ref):
    ny, nx = mask_ref.shape[1:]
    even = tile_ref[0] % 2 == 0
    left_ref = [jnp.where(even, off_ref[i], on_ref[i]) for i in range(3)]
    right_ref = [jnp.where(even, on_ref[i], off_ref[i]) for i in range(3)]
    rest = jnp.zeros((ny, N - nx - 2 * STEPS), jnp.float32)

    def across(left, own, right):
        return jnp.concatenate([left[:, nx - STEPS :], own, right[:, :STEPS], rest], axis=1)

    known = across(left_ref[2], mask_ref[0].astype(jnp.float32) + 1.0, right_ref[2])
    valid = jnp.where(known > 0.5, 1.0, 0.0)
    trust = jnp.where(known > 1.5, 1.0, 0.0)
    row = lax.broadcasted_iota(jnp.int32, trust.shape, 0)
    fields = []
    for component in range(2):
        own = jnp.concatenate([low_ref[component], high_ref[component]], axis=0)
        flow = across(left_ref[component], own, right_ref[component])
        field = trust * flow
        for _ in range(STEPS):
            below = jnp.where(row == 0, 0.0, pltpu.roll(field, 1, 0))
            above = jnp.where(row == ny - 1, 0.0, pltpu.roll(field, ny - 1, 0))
            beside = pltpu.roll(field, 1, 1) + pltpu.roll(field, N - 1, 1)
            lap = above + below + beside - 4.0 * field
            field = (field + SPRING * (lap + trust * (flow - field))) * valid
        fields.append(field)
    return fields


def edge_kernel(tile_ref, target_ref, share_ref, first_ref, second_ref, off_ref, padded, out_ref, window, sems):
    y = pl.program_id(0)
    ny, nx = padded.shape[:2]
    even = tile_ref[0] % 2 == 0
    halos = {
        side: ((first_ref, on_at), (second_ref, on_at + 1), (off_ref, HB - on_at))
        for side, on_at in ((True, HB), (False, 0))
    }
    copies = {
        side: [
            pltpu.make_async_copy(ref, window.at[:, into : into + ref.shape[1]], sems.at[i])
            for i, (ref, into) in enumerate(places)
        ]
        for side, places in halos.items()
    }

    @pl.when((y == 0) & even)
    def _():
        for copy in copies[True]:
            copy.start()

    @pl.when((y == 0) & jnp.logical_not(even))
    def _():
        for copy in copies[False]:
            copy.start()

    border = jnp.zeros((2 * HB, PAD, N), jnp.float32)
    out_ref[y, :, :PAD] = border
    out_ref[y, :, PAD + N :] = border

    @pl.when(y == 0)
    def _():
        for copy in copies[True]:
            copy.wait()

    for i, x in enumerate((*range(HB), *range(nx - HB, nx))):
        more = blend_cell(y, K * nx + x, nx, target_ref, share_ref, window)
        out_ref[y, i, PAD : PAD + N] = padded[y, x, PAD : PAD + N] + more


def edges_of(tile, target, share, first, second, off, blended):
    ny, _, tall, _ = blended.shape
    vmem = pl.BlockSpec(memory_space=pltpu.VMEM)
    return pl.pallas_call(
        edge_kernel,
        grid=(ny,),
        in_specs=[pl.BlockSpec(memory_space=pltpu.SMEM)] * 3 + [vmem] * 4,
        out_specs=vmem,
        out_shape=pltpu.VMEM((ny, 2 * HB, tall, N), jnp.float32),
        scratch_shapes=[pltpu.VMEM((ny, 2 * HB, N, N), jnp.bfloat16), pltpu.SemaphoreType.DMA((3,))],
        compiler_params=pltpu.CompilerParams(vmem_limit_bytes=4 * MIB),
        cost_estimate=pl.CostEstimate(flops=5_000_000, bytes_accessed=4 * MIB, transcendentals=0),
        name="edges",
    )(tile, target, share, in_vmem(first), in_vmem(second), in_vmem(off), in_vmem(blended))


def warped(cell, down_shift, right_shift):
    whole_of = lambda shift: (shift + 256.0).astype(jnp.int32) - 256
    line = lambda value: jnp.full((1, N), value, jnp.float32).astype(jnp.bfloat16)
    down = jnp.clip(whole_of(down_shift), 4 - PAD, PAD - 6)
    part = down_shift - down.astype(jnp.float32)
    upper = cell[pl.ds(PAD + down, N), :]
    lower = cell[pl.ds(PAD + 1 + down, N), :]
    image = upper + part * (lower - upper)
    right = whole_of(right_shift).astype(jnp.float32)
    apart = lax.broadcasted_iota(jnp.int32, (N, N), 0) - lax.broadcasted_iota(jnp.int32, (N, N), 1)
    apart = apart.astype(jnp.bfloat16) - line(right)
    one = jnp.bfloat16(1.0)
    hat = jnp.maximum(jnp.bfloat16(0.0), one - jnp.abs(apart - line(right_shift - right)))
    return dot(image.astype(jnp.bfloat16), hat).astype(jnp.bfloat16)


def warp_kernel(tile_ref, *refs):
    *flows, padded, edges, out_hbm, field_ref, out, wide, field, sem, out_sems = refs
    y = pl.program_id(0)
    ny, nx = out.shape[:2]

    @pl.when(y == 0)
    def _():
        for component, values in enumerate(relax(tile_ref, *flows)):
            wide[component] = values
            field_ref[0, component] = values[:, STEPS : STEPS + nx]
        scalars = pltpu.make_async_copy(wide, field, sem)
        scalars.start()
        scalars.wait()

    borders = (*range(HB), *range(nx - HB, nx))
    for x in range(nx):
        cell = edges.at[y, borders.index(x)] if x in borders else padded.at[y, x]
        out[y, x] = warped(cell, field[0, y, STEPS + x], field[1, y, STEPS + x])
    store = lambda row: pltpu.make_async_copy(out.at[row], out_hbm.at[0, row], out_sems.at[row])
    store(y).start()
    wait_all([store(row) for row in range(ny)])


def warp(tile, flows, blended, edges):
    ny, nx = blended.shape[:2]
    whole = lambda shape: pl.BlockSpec(shape, lambda y: (0,) * len(shape))
    return pl.pallas_call(
        warp_kernel,
        grid=(ny,),
        in_specs=[pl.BlockSpec(memory_space=pltpu.SMEM)]
        + [whole(x.shape) for x in flows]
        + [pl.BlockSpec(memory_space=pltpu.VMEM)] * 2,
        out_specs=[pl.BlockSpec(memory_space=pl.ANY), whole((1, 2, ny, nx))],
        out_shape=[
            jax.ShapeDtypeStruct((1, ny, nx, N, N), jnp.bfloat16),
            jax.ShapeDtypeStruct((1, 2, ny, nx), jnp.float32),
        ],
        scratch_shapes=[
            pltpu.VMEM((ny, nx, N, N), jnp.bfloat16),
            pltpu.VMEM((2, ny, N), jnp.float32),
            pltpu.SMEM((2, ny, N), jnp.float32),
            pltpu.SemaphoreType.DMA,
            pltpu.SemaphoreType.DMA((ny,)),
        ],
        compiler_params=pltpu.CompilerParams(vmem_limit_bytes=8 * MIB),
        cost_estimate=pl.CostEstimate(flops=20_000_000, bytes_accessed=12 * MIB, transcendentals=0),
        name="warp",
    )(tile, *flows, in_vmem(blended), in_vmem(edges))


def from_behind(x, axis, by):
    length = lax.axis_size(axis)
    pairs = [(i, i + by) for i in range(length) if 0 <= i + by < length]
    return lax.ppermute(x, axis, pairs)


def swapped(x):
    return lax.ppermute(x, "tile", [(i, i ^ 1) for i in range(lax.axis_size("tile"))])


def hops(tiles, sections, far):
    pairs = ([], [])
    for section in range(sections):
        x_low, rest = divmod(section, sections // 2)
        way = 1 if rest < sections // 4 else -1
        for tile in range(tiles):
            z, x_high = divmod(tile, 2)
            ends = [section * tiles + tile]
            for hop in (1, 2):
                x = (2 * x_high + x_low + hop * way) % 4
                to_z = (z + 2 * x_high - 1) % (tiles // 2) if far and hop == 2 else z
                ends.append((x % 2 * (sections // 2) + rest) * tiles + 2 * to_z + x // 2)
            pairs[0].append((ends[0], ends[1]))
            pairs[1].append((ends[1], ends[2]))
    return pairs


def beyond(x):
    tiles = lax.axis_size("tile")
    pairs = [(i, i + 1) for i in range(1, tiles - 1, 2)]
    return lax.ppermute(x, "tile", pairs + [(j, i) for i, j in pairs])


def per_device(sections, node_mask, box_row, box_shift, box_count, blend_weight):
    ny, nx = sections.shape[1:3]
    rows, cols, back_cols, back_rows = tables()
    half = ny // 2
    tiles, count = lax.axis_size("tile"), lax.axis_size("sec")
    tile = jnp.stack([lax.axis_index("tile"), tiles]).astype(jnp.int32)
    on_hops, off_hops = hops(tiles, count, False), hops(tiles, count, True)
    hop = lambda x, pairs: lax.ppermute(x, ("sec", "tile"), pairs)

    spectra_high, source, off = forward(tile, sections, half, half, False, None, rows, cols)
    from_last = from_behind(spectra_high, "sec", 1)
    off = hop(off, off_hops[0])
    spectra_low, source, first, second = forward(tile, sections, 0, half, True, source, rows, cols)
    from_next = from_behind(spectra_low, "sec", -1)
    first = hop(first, on_hops[0])
    target, share = slots_of(tile, box_row, box_shift, box_count, blend_weight)
    off, first, source = lax.optimization_barrier((off, first, source))
    off = hop(off, off_hops[1])
    first = hop(first, on_hops[1])
    blended = blend(target, share, source)
    from_last, blended = lax.optimization_barrier((from_last, blended))

    flow_high = flow_of(spectra_high, from_last, -1, half, nx, cols, back_cols, back_rows)
    second, off, flow_high = lax.optimization_barrier((second, off, flow_high))
    flow_high = from_behind(flow_high, "sec", -1)
    second = swapped(second)
    from_next, flow_high, first = lax.optimization_barrier((from_next, flow_high, first))
    flow_low = flow_of(spectra_low, from_next, 1, half, nx, cols, back_cols, back_rows)
    flow = jnp.concatenate([flow_low, flow_high], axis=1)
    flow = jnp.concatenate([flow, node_mask.astype(jnp.float32) + 1.0], axis=0)
    flow_off = beyond(flow)
    flow_on = swapped(flow)
    flows = (flow_low, flow_high, node_mask, flow_on, flow_off)
    edges = edges_of(tile, target, share, first, second, off, blended)
    return tuple(warp(tile, flows, blended, edges))


def solution(mesh):
    return jax.shard_map(
        per_device,
        mesh=mesh,
        in_specs=(
            P("sec", None, "tile", None, None),
            P("sec", None, "tile"),
            P("sec", None, "tile", None),
            P("sec", None, "tile", None),
            P("sec", None, "tile"),
            P("sec", None, "tile", None),
        ),
        out_specs=(P("sec", None, "tile", None, None), P("sec", None, None, "tile")),
        check_vma=False,
    )
```

```python
import functools

import jax
import jax.numpy as jnp
import numpy as np
from jax import lax
from jax.experimental import pallas as pl
from jax.experimental.pallas import tpu as pltpu
from jax.sharding import PartitionSpec as P

K = 4
HB = 2
STEPS = 3
N = 128
HALF = N // 2
PAD = 72
ROW = 32
DEPTH = 2
SPRING = 0.2
EPS = 1e-06
MIB = 1024 * 1024


def split(x):
    high = x.astype(jnp.bfloat16)
    return high, (x - high.astype(jnp.float32)).astype(jnp.bfloat16)


def tables():
    grid = np.arange(N)[:, None] * np.arange(N)[None, :] % N
    cosine = np.cos(2.0 * np.pi * grid / N)
    sine = np.sin(2.0 * np.pi * grid / N)
    rows = np.concatenate([cosine[:HALF], sine[:HALF]])
    rows[HALF] = cosine[HALF]
    cols = np.block([[cosine, -sine], [-sine, -cosine]])
    back_cols = np.block([[cosine, sine], [-sine, cosine]]) / N
    weight = np.where(np.arange(HALF) == 0, 1.0, 2.0)
    back_rows = np.concatenate([cosine[:, :HALF] * weight, -2.0 * sine[:, :HALF]], axis=1) / N
    back_rows[:, HALF] = cosine[:, HALF] / N
    return [jnp.asarray(t, jnp.float32) for t in (rows, cols, back_cols, back_rows)]


def first_row(shape):
    return lax.broadcasted_iota(jnp.int32, shape, len(shape) - 2) == 0


def dot(a, b):
    return jnp.dot(a, b, preferred_element_type=jnp.float32)


def ahead(fetch, rows, depth):
    y = pl.program_id(0)

    @pl.when(y == 0)
    def _():
        for row in range(depth):
            for copy in fetch(row):
                copy.start()

    @pl.when(y + depth < rows)
    def _():
        for copy in fetch(y + depth):
            copy.start()

    for copy in fetch(y):
        copy.wait()


def in_hbm(x):
    return pltpu.with_memory_space_constraint(x, pltpu.HBM)


def in_vmem(x):
    return pltpu.with_memory_space_constraint(x, pltpu.VMEM)


def wait_all(copies):
    @pl.when(pl.program_id(0) == pl.num_programs(0) - 1)
    def _():
        for copy in copies:
            copy.wait()


def forward_kernel(start, toward_pair, tile_ref, x_hbm, rows_hbm, cols_hbm, *refs):
    *_, spec_ref, src_ref, strip_ref, x_ref, rest_ref, lines_ref, ends_ref, rows_ref, cols_ref, in_sems, more_sems = refs
    y = pl.program_id(0)
    count, patches = x_ref.shape[:2]
    ny = strip_ref.shape[0]
    odd = tile_ref[0] % 2
    column = ((1 - odd) if toward_pair else odd) * (patches - HB)
    rest = (start + count) % ny
    fetch = lambda row: [pltpu.make_async_copy(x_hbm.at[0, start + row], x_ref.at[row], in_sems.at[row])]
    more = [
        pltpu.make_async_copy(rows_hbm, rows_ref, more_sems.at[0]),
        pltpu.make_async_copy(cols_hbm, cols_ref, more_sems.at[1]),
        pltpu.make_async_copy(
            x_hbm.at[0, pl.ds(rest, ny - count), pl.ds(column, HB)], rest_ref, more_sems.at[2]
        ),
    ]

    @pl.when(y == 0)
    def _():
        for copy in more[:2]:
            copy.start()

    ahead(fetch, count, min(DEPTH, count))

    @pl.when(y == 0)
    def _():
        for copy in more[:2]:
            copy.wait()
        more[2].start()

    @pl.when(y == count - 1)
    def _():
        more[2].wait()
        strip_ref[rest : rest + ny - count] = rest_ref[...].astype(jnp.bfloat16)

    for i in range(HB):
        strip_ref[start + y, i] = x_ref[y, column + i].astype(jnp.bfloat16)
    rows2 = rows_ref[...]
    cols = cols_ref[...]
    for pair in range(patches // 2):
        x = jnp.concatenate([x_ref[y, 2 * pair], x_ref[y, 2 * pair + 1]], axis=1)
        high, low = split(x)
        src_ref[start + y, 2 * pair] = high[:, :N]
        src_ref[start + y, 2 * pair + 1] = high[:, N:]
        both = dot(rows2, jnp.concatenate([high, low], axis=0))
        for side in range(2):
            here = both[:, side * N : (side + 1) * N]
            p = 2 * pair + side
            ends_ref[p : p + 1, :N] = here[:1]
            ends_ref[p : p + 1, N:] = here[HALF : HALF + 1]
            lines_ref[p * HALF : (p + 1) * HALF, :N] = here[:HALF].astype(jnp.bfloat16)
            lines_ref[p * HALF : (p + 1) * HALF, N:] = here[HALF:].astype(jnp.bfloat16)
    step = 4
    for first in range(0, patches, step):
        lines = lines_ref[first * HALF : (first + step) * HALF, :]
        freq = dot(lines, cols).reshape(step, HALF, 2 * N)
        spec_ref[pl.ds(y * patches + first, step)] = freq.astype(jnp.bfloat16)
    ends = ends_ref[...].astype(jnp.bfloat16)
    spec_ref[count * patches, pl.ds(pl.multiple_of(y * patches, patches), patches), :] = ends


def forward(tile, sections, start, count, toward_pair, source, rows, cols):
    _, ny, nx, _, _ = sections.shape
    rows2 = jnp.concatenate([rows, rows], axis=1).astype(jnp.bfloat16)
    spectra = (count * nx + 1, HALF, 2 * N)
    before = () if source is None else (in_vmem(source),)
    return pl.pallas_call(
        functools.partial(forward_kernel, start, toward_pair),
        grid=(count,),
        in_specs=[pl.BlockSpec(memory_space=pltpu.SMEM)]
        + [pl.BlockSpec(memory_space=pltpu.HBM)] * 3
        + [pl.BlockSpec(memory_space=pltpu.VMEM)] * len(before),
        out_specs=[pl.BlockSpec(memory_space=pltpu.VMEM)] * 3,
        out_shape=[
            pltpu.VMEM(spectra, jnp.bfloat16),
            pltpu.VMEM((ny, nx, N, N), jnp.bfloat16),
            pltpu.VMEM((ny, HB, N, N), jnp.bfloat16),
        ],
        scratch_shapes=[
            pltpu.VMEM((count, nx, N, N), jnp.float32),
            pltpu.VMEM((ny - count, HB, N, N), jnp.float32),
            pltpu.VMEM((nx * HALF, 2 * N), jnp.bfloat16),
            pltpu.VMEM((nx, 2 * N), jnp.float32),
            pltpu.VMEM((N, 2 * N), jnp.bfloat16),
            pltpu.VMEM((2 * N, 2 * N), jnp.bfloat16),
            pltpu.SemaphoreType.DMA((count,)),
            pltpu.SemaphoreType.DMA((3,)),
        ],
        input_output_aliases={4: 1} if before else {},
        compiler_params=pltpu.CompilerParams(vmem_limit_bytes=12 * MIB),
        cost_estimate=pl.CostEstimate(flops=2_000_000_000, bytes_accessed=6 * MIB, transcendentals=0),
        name="forward",
    )(tile, in_hbm(sections), in_hbm(rows2), in_hbm(cols.astype(jnp.bfloat16)), *before)


def times_conj(a, b, sign):
    ar, ai, br, bi = a[:, :N], a[:, N:], b[:, :N], b[:, N:]
    real = ar * br + ai * bi
    imag = ai * br - ar * bi if sign > 0 else ar * bi - ai * br
    return jnp.concatenate([real, imag], axis=1).astype(jnp.bfloat16)


def flow_kernel(sign, own, other, cols_ref, back_cols_ref, back_rows_ref, flow_ref, sides, sums, moments):
    y = pl.program_id(0)
    ny, patches = sums.shape[:2]
    last = ny * patches
    cols = cols_ref[...]
    back_cols = back_cols_ref[...]
    back_rows = back_rows_ref[...]

    @pl.when(y == 0)
    def _():
        lines = jnp.concatenate([own[last], other[last]], axis=0)
        edge = dot(jnp.concatenate([lines[:, :N], lines[:, N:]], axis=0), cols[:N])
        quarter = edge.reshape(4, last, 2 * N)
        low = times_conj(quarter[0], quarter[1], sign)
        high = times_conj(quarter[2], quarter[3], sign)
        back = dot(jnp.concatenate([low, high], axis=0), back_cols[:, :N])
        sides[...] = back.reshape(sides.shape)

    shift_rows = lax.broadcasted_iota(jnp.int32, (N, N), 0)
    offset_rows = (((shift_rows + HALF) % N) - HALF).astype(jnp.float32)
    offset_rows = jnp.concatenate([offset_rows, offset_rows], axis=1)
    step = 4
    for first in range(0, patches, step):
        here = pl.ds(y * patches + first, step)
        a = own[here].reshape(step * HALF, 2 * N).astype(jnp.float32)
        b = other[here].reshape(step * HALF, 2 * N).astype(jnp.float32)
        back = dot(times_conj(a, b, sign), back_cols)
        halves = []
        for i in range(step):
            p = first + i
            parts = []
            for side in range(2):
                part = back[i * HALF : (i + 1) * HALF, side * N : (side + 1) * N]
                top = jnp.where(first_row((16, N)), sides[side, y, p : p + 1, :], part[:16])
                parts += [top.astype(jnp.bfloat16), part[16:].astype(jnp.bfloat16)]
            halves.append(jnp.concatenate(parts, axis=0))
        for i in range(0, step, 2):
            corr = dot(back_rows, jnp.concatenate(halves[i : i + 2], axis=1))
            power = corr * corr
            total = power.sum(0, keepdims=True)
            moment = (power * offset_rows).sum(0, keepdims=True)
            for side in range(2):
                p = first + i + side
                sums[y, p : p + 1, :] = total[:, side * N : (side + 1) * N]
                moments[y, p : p + 1, :] = moment[:, side * N : (side + 1) * N]

    @pl.when(y == ny - 1)
    def _():
        lane = lax.broadcasted_iota(jnp.int32, (8, N), 1)
        row = lax.broadcasted_iota(jnp.int32, (8, N), 0)
        offset_cols = (((lane + HALF) % N) - HALF).astype(jnp.float32)
        reduce_by = jnp.where(row == 0, 1.0, jnp.where(row == 1, offset_cols, 0.0))
        over_lanes = lambda m: lax.dot_general(
            reduce_by, m.reshape(last, N), (((1,), (1,)), ((), ())),
            precision=lax.Precision.HIGHEST, preferred_element_type=jnp.float32,
        )
        by_sums = over_lanes(sums[...])
        by_moments = over_lanes(moments[...])
        total = by_sums[0:1] + EPS
        along_rows = by_moments[0:1] / total
        along_cols = by_sums[1:2] / total
        for row in range(ny):
            flow_ref[0, row : row + 1, :] = along_rows[:, row * patches : (row + 1) * patches]
            flow_ref[1, row : row + 1, :] = along_cols[:, row * patches : (row + 1) * patches]


def flow_of(own, other, sign, ny, nx, cols, back_cols, back_rows):
    whole = lambda shape: pl.BlockSpec(shape, lambda y: (0,) * len(shape))
    return pl.pallas_call(
        functools.partial(flow_kernel, sign),
        grid=(ny,),
        in_specs=[
            pl.BlockSpec(memory_space=pltpu.VMEM),
            pl.BlockSpec(memory_space=pltpu.VMEM),
            whole((2 * N, 2 * N)),
            whole((2 * N, 2 * N)),
            whole((N, N)),
        ],
        out_specs=whole((2, ny, nx)),
        out_shape=jax.ShapeDtypeStruct((2, ny, nx), jnp.float32),
        scratch_shapes=[
            pltpu.VMEM((2, ny, nx, N), jnp.float32),
            pltpu.VMEM((ny, nx, N), jnp.float32),
            pltpu.VMEM((ny, nx, N), jnp.float32),
        ],
        compiler_params=pltpu.CompilerParams(vmem_limit_bytes=8 * MIB),
        cost_estimate=pl.CostEstimate(flops=0 if sign < 0 else 50_000_000_000, bytes_accessed=0, transcendentals=0),
        name="flow",
    )(in_vmem(own), in_vmem(other), *(t.astype(jnp.bfloat16) for t in (cols, back_cols, back_rows)))


def slots_kernel(tile_ref, rows_ref, shifts_ref, count_ref, weight_ref, target_ref, share_ref):
    ny, _, nx = rows_ref.shape[1:]
    tile, tiles = tile_ref[0], tile_ref[1]
    live = [k < count_ref[0] for k in range(K)]
    weights = [jnp.where(live[k], weight_ref[0, :, k, :], 0.0) for k in range(K)]
    total = weights[0] + weights[1] + weights[2] + weights[3]
    share = [(w / total).astype(jnp.bfloat16).astype(jnp.float32) for w in weights]
    columns = [lax.broadcasted_iota(jnp.int32, (ny, nx), 1) + shifts_ref[0, :, k, :] for k in range(K)]
    rows = [rows_ref[0, :, k, :] * ROW for k in range(K)]
    low = [c < 0 for c in columns]
    high = [c >= nx for c in columns]
    first, last = tile == 0, tile == tiles - 1
    inside = [jnp.where(l | h, 0.0, s) for l, h, s in zip(low, high, share, strict=True)]
    share_low = [jnp.where(first, 0.0, jnp.where(l, s, 0.0)) for l, s in zip(low, share, strict=True)]
    share_high = [jnp.where(last, 0.0, jnp.where(h, s, 0.0)) for h, s in zip(high, share, strict=True)]
    beyond = [l + h for l, h in zip(share_low, share_high, strict=True)]
    share_ref[...] = jnp.concatenate(inside + beyond, axis=1)
    target = [r + jnp.where(l | h, 0, c) for r, c, l, h in zip(rows, columns, low, high, strict=True)]
    away = [
        r + jnp.where(l, c + HB, jnp.where(h, c - nx + HB, 0))
        for r, c, l, h in zip(rows, columns, low, high, strict=True)
    ]
    target_ref[...] = jnp.concatenate(target + away, axis=1)


def slots_of(tile, box_row, box_shift, box_count, blend_weight):
    ny = box_row.shape[1]
    slots_first = lambda x: jnp.transpose(x, (0, 1, 3, 2))
    return pl.pallas_call(
        slots_kernel,
        in_specs=[pl.BlockSpec(memory_space=pltpu.SMEM)] + [pl.BlockSpec(memory_space=pltpu.VMEM)] * 4,
        out_shape=[
            jax.ShapeDtypeStruct((ny, N), jnp.int32),
            jax.ShapeDtypeStruct((ny, N), jnp.float32),
        ],
        compiler_params=pltpu.CompilerParams(vmem_limit_bytes=4 * MIB),
        cost_estimate=pl.CostEstimate(flops=0, bytes_accessed=0, transcendentals=0),
        name="slots",
    )(tile, slots_first(box_row), slots_first(box_shift), box_count, slots_first(blend_weight))


def blend_cell(y, first, nx, target_ref, share_ref, window):
    total = None
    for k in range(K):
        spot = target_ref[y, first + k * nx]
        piece = window[spot // ROW, spot % ROW].astype(jnp.float32) * share_ref[y, first + k * nx]
        total = piece if total is None else total + piece
    return total


def blend_kernel(target_ref, share_ref, source, out_ref):
    y = pl.program_id(0)
    nx = source.shape[1]
    border = jnp.zeros((nx, PAD, N), jnp.float32)
    out_ref[y, :, :PAD] = border
    out_ref[y, :, PAD + N :] = border
    for x in range(nx):
        out_ref[y, x, PAD : PAD + N] = blend_cell(y, x, nx, target_ref, share_ref, source)


def blend(target, share, source):
    ny, nx = source.shape[:2]
    return pl.pallas_call(
        blend_kernel,
        grid=(ny,),
        in_specs=[pl.BlockSpec(memory_space=pltpu.SMEM)] * 2 + [pl.BlockSpec(memory_space=pltpu.VMEM)],
        out_specs=pl.BlockSpec(memory_space=pltpu.VMEM),
        out_shape=pltpu.VMEM((ny, nx, N + 2 * PAD, N), jnp.float32),
        compiler_params=pltpu.CompilerParams(vmem_limit_bytes=4 * MIB),
        cost_estimate=pl.CostEstimate(flops=20_000_000_000, bytes_accessed=4 * MIB, transcendentals=0),
        name="blend",
    )(target, share, in_vmem(source))


def relax(tile_ref, low_ref, high_ref, mask_ref, on_ref, off_ref):
    ny, nx = mask_ref.shape[1:]
    even = tile_ref[0] % 2 == 0
    left_ref = [jnp.where(even, off_ref[i], on_ref[i]) for i in range(3)]
    right_ref = [jnp.where(even, on_ref[i], off_ref[i]) for i in range(3)]
    rest = jnp.zeros((ny, N - nx - 2 * STEPS), jnp.float32)

    def across(left, own, right):
        return jnp.concatenate([left[:, nx - STEPS :], own, right[:, :STEPS], rest], axis=1)

    known = across(left_ref[2], mask_ref[0].astype(jnp.float32) + 1.0, right_ref[2])
    valid = jnp.where(known > 0.5, 1.0, 0.0)
    trust = jnp.where(known > 1.5, 1.0, 0.0)
    row = lax.broadcasted_iota(jnp.int32, trust.shape, 0)
    fields = []
    for component in range(2):
        own = jnp.concatenate([low_ref[component], high_ref[component]], axis=0)
        flow = across(left_ref[component], own, right_ref[component])
        field = trust * flow
        for _ in range(STEPS):
            below = jnp.where(row == 0, 0.0, pltpu.roll(field, 1, 0))
            above = jnp.where(row == ny - 1, 0.0, pltpu.roll(field, ny - 1, 0))
            beside = pltpu.roll(field, 1, 1) + pltpu.roll(field, N - 1, 1)
            lap = above + below + beside - 4.0 * field
            field = (field + SPRING * (lap + trust * (flow - field))) * valid
        fields.append(field)
    return fields


def halo_cell(y, x, nx, target_ref, share_ref, strip):
    total = None
    for k in range(K):
        at = (K + k) * nx + x
        spot = target_ref[y, at]
        piece = strip[spot // ROW, spot % HB].astype(jnp.float32) * share_ref[y, at]
        total = piece if total is None else total + piece
    return total


def beyond_kernel(tile_ref, target_ref, share_ref, strip, _, out_ref):
    y = pl.program_id(0)
    nx = out_ref.shape[1]
    first = tile_ref[0] % 2 * (nx - HB)
    for i in range(HB):
        x = first + i
        out_ref[y, x, PAD : PAD + N] += halo_cell(y, x, nx, target_ref, share_ref, strip)


def with_beyond(tile, target, share, off, blended):
    vmem = pl.BlockSpec(memory_space=pltpu.VMEM)
    return pl.pallas_call(
        beyond_kernel,
        grid=(blended.shape[0],),
        in_specs=[pl.BlockSpec(memory_space=pltpu.SMEM)] * 3 + [vmem] * 2,
        out_specs=vmem,
        out_shape=pltpu.VMEM(blended.shape, jnp.float32),
        input_output_aliases={4: 0},
        compiler_params=pltpu.CompilerParams(vmem_limit_bytes=4 * MIB),
        cost_estimate=pl.CostEstimate(flops=0, bytes_accessed=0, transcendentals=0),
        name="beyond",
    )(tile, target, share, in_vmem(off), in_vmem(blended))


def warped(cell, down_shift, right_shift):
    whole_of = lambda shift: (shift + 256.0).astype(jnp.int32) - 256
    line = lambda value: jnp.full((1, N), value, jnp.float32).astype(jnp.bfloat16)
    down = jnp.clip(whole_of(down_shift), 4 - PAD, PAD - 6)
    part = down_shift - down.astype(jnp.float32)
    upper = cell[pl.ds(PAD + down, N), :]
    lower = cell[pl.ds(PAD + 1 + down, N), :]
    image = upper + part * (lower - upper)
    right = whole_of(right_shift).astype(jnp.float32)
    apart = lax.broadcasted_iota(jnp.int32, (N, N), 0) - lax.broadcasted_iota(jnp.int32, (N, N), 1)
    apart = apart.astype(jnp.bfloat16) - line(right)
    one = jnp.bfloat16(1.0)
    hat = jnp.maximum(jnp.bfloat16(0.0), one - jnp.abs(apart - line(right_shift - right)))
    return dot(image.astype(jnp.bfloat16), hat).astype(jnp.bfloat16)


def warp_kernel(tile_ref, *refs):
    *flows, padded, out_hbm, field_ref, wide_ref, out, field, sem, out_sems = refs
    y = pl.program_id(0)
    ny, count = out.shape[:2]
    nx = padded.shape[1]
    first = tile_ref[0] % 2 * HB

    @pl.when(y == 0)
    def _():
        for component, values in enumerate(relax(tile_ref, *flows)):
            wide_ref[component] = values
            field_ref[0, component] = values[:, STEPS : STEPS + nx]
        scalars = pltpu.make_async_copy(wide_ref, field, sem)
        scalars.start()
        scalars.wait()

    for i in range(count):
        x = first + i
        out[y, i] = warped(padded.at[y, x], field[0, y, STEPS + x], field[1, y, STEPS + x])
    store = lambda row: pltpu.make_async_copy(
        out.at[row], out_hbm.at[0, row, pl.ds(first, count)], out_sems.at[row]
    )
    store(y).start()
    wait_all([store(row) for row in range(ny)])


def warp(tile, flows, blended):
    ny, nx = blended.shape[:2]
    whole = lambda shape: pl.BlockSpec(shape, lambda y: (0,) * len(shape))
    return pl.pallas_call(
        warp_kernel,
        grid=(ny,),
        in_specs=[pl.BlockSpec(memory_space=pltpu.SMEM)]
        + [whole(x.shape) for x in flows]
        + [pl.BlockSpec(memory_space=pltpu.VMEM)],
        out_specs=[
            pl.BlockSpec(memory_space=pltpu.HBM),
            whole((1, 2, ny, nx)),
            pl.BlockSpec(memory_space=pltpu.VMEM),
        ],
        out_shape=[
            jax.ShapeDtypeStruct((1, ny, nx, N, N), jnp.bfloat16),
            jax.ShapeDtypeStruct((1, 2, ny, nx), jnp.float32),
            pltpu.VMEM((2, ny, N), jnp.float32),
        ],
        scratch_shapes=[
            pltpu.VMEM((ny, nx - HB, N, N), jnp.bfloat16),
            pltpu.SMEM((2, ny, N), jnp.float32),
            pltpu.SemaphoreType.DMA,
            pltpu.SemaphoreType.DMA((ny,)),
        ],
        compiler_params=pltpu.CompilerParams(vmem_limit_bytes=8 * MIB),
        cost_estimate=pl.CostEstimate(flops=20_000_000, bytes_accessed=12 * MIB, transcendentals=0),
        name="warp",
    )(tile, *flows, in_vmem(blended))


def pair_kernel(tile_ref, target_ref, share_ref, wide, strip, padded, _, out_hbm, cells, out, field, sem, out_sems):
    step = pl.program_id(0)
    ny, nx = padded.shape[:2]
    rows = cells.shape[0] // HB
    first = (1 - tile_ref[0] % 2) * (nx - HB)
    scalars = pltpu.make_async_copy(wide, field, sem)

    @pl.when(step == 0)
    def _():
        scalars.start()
        border = jnp.zeros((rows * HB, PAD, N), jnp.float32)
        cells[:, :PAD] = border
        cells[:, PAD + N :] = border

    places = [(step * rows + row, i, row * HB + i) for row in range(rows) for i in range(HB)]
    for y, i, at in places:
        more = halo_cell(y, first + i, nx, target_ref, share_ref, strip)
        cells[at, PAD : PAD + N] = padded[y, first + i, PAD : PAD + N] + more

    @pl.when(step == 0)
    def _():
        scalars.wait()

    for y, i, at in places:
        column = STEPS + first + i
        out[y, i] = warped(cells.at[at], field[0, y, column], field[1, y, column])
    store = lambda row: pltpu.make_async_copy(
        out.at[row], out_hbm.at[0, row, pl.ds(first, HB)], out_sems.at[row]
    )
    for row in range(rows):
        store(step * rows + row).start()
    wait_all([store(row) for row in range(ny)])


def warp_pair(tile, target, share, wide, on, blended, rendered):
    ny, _, tall, _ = blended.shape
    rows = 2
    vmem = pl.BlockSpec(memory_space=pltpu.VMEM)
    hbm = pl.BlockSpec(memory_space=pltpu.HBM)
    return pl.pallas_call(
        pair_kernel,
        grid=(ny // rows,),
        in_specs=[pl.BlockSpec(memory_space=pltpu.SMEM)] * 3 + [vmem] * 3 + [hbm],
        out_specs=hbm,
        out_shape=jax.ShapeDtypeStruct(rendered.shape, rendered.dtype),
        scratch_shapes=[
            pltpu.VMEM((rows * HB, tall, N), jnp.float32),
            pltpu.VMEM((ny, HB, N, N), jnp.bfloat16),
            pltpu.SMEM((2, ny, N), jnp.float32),
            pltpu.SemaphoreType.DMA,
            pltpu.SemaphoreType.DMA((ny,)),
        ],
        input_output_aliases={6: 0},
        compiler_params=pltpu.CompilerParams(vmem_limit_bytes=8 * MIB),
        cost_estimate=pl.CostEstimate(flops=5_000_000, bytes_accessed=4 * MIB, transcendentals=0),
        name="pair",
    )(tile, target, share, in_vmem(wide), in_vmem(on), in_vmem(blended), rendered)


def from_behind(x, axis, by):
    length = lax.axis_size(axis)
    pairs = [(i, i + by) for i in range(length) if 0 <= i + by < length]
    return lax.ppermute(x, axis, pairs)


def swapped(x):
    return lax.ppermute(x, "tile", [(i, i ^ 1) for i in range(lax.axis_size("tile"))])


def hops(tiles, sections):
    pairs = ([], [])
    for section in range(sections):
        x_low, rest = divmod(section, sections // 2)
        way = 1 if rest < sections // 4 else -1
        for tile in range(tiles):
            z, x_high = divmod(tile, 2)
            ends = [section * tiles + tile]
            for hop in (1, 2):
                x = (2 * x_high + x_low + hop * way) % 4
                to_z = (z + 2 * x_high - 1) % (tiles // 2) if hop == 2 else z
                ends.append((x % 2 * (sections // 2) + rest) * tiles + 2 * to_z + x // 2)
            pairs[0].append((ends[0], ends[1]))
            pairs[1].append((ends[1], ends[2]))
    return pairs


def beyond(x):
    tiles = lax.axis_size("tile")
    pairs = [(i, i + 1) for i in range(1, tiles - 1, 2)]
    return lax.ppermute(x, "tile", pairs + [(j, i) for i, j in pairs])


def per_device(sections, node_mask, box_row, box_shift, box_count, blend_weight):
    ny, nx = sections.shape[1:3]
    rows, cols, back_cols, back_rows = tables()
    half = ny // 2
    tiles, count = lax.axis_size("tile"), lax.axis_size("sec")
    tile = jnp.stack([lax.axis_index("tile"), tiles]).astype(jnp.int32)
    off_hops = hops(tiles, count)
    hop = lambda x, pairs: lax.ppermute(x, ("sec", "tile"), pairs)

    spectra_high, source, off = forward(tile, sections, half, half, False, None, rows, cols)
    from_last = from_behind(spectra_high, "sec", 1)
    off = hop(off, off_hops[0])
    spectra_low, source, on = forward(tile, sections, 0, half, True, source, rows, cols)
    from_next = from_behind(spectra_low, "sec", -1)
    target, share = slots_of(tile, box_row, box_shift, box_count, blend_weight)
    off, source = lax.optimization_barrier((off, source))
    off = hop(off, off_hops[1])
    blended = blend(target, share, source)
    blended = with_beyond(tile, target, share, off, blended)
    from_last, blended = lax.optimization_barrier((from_last, blended))

    flow_high = flow_of(spectra_high, from_last, -1, half, nx, cols, back_cols, back_rows)
    on, flow_high = lax.optimization_barrier((on, flow_high))
    flow_high = from_behind(flow_high, "sec", -1)
    from_next, flow_high = lax.optimization_barrier((from_next, flow_high))
    flow_low = flow_of(spectra_low, from_next, 1, half, nx, cols, back_cols, back_rows)
    on = swapped(on)
    flow = jnp.concatenate([flow_low, flow_high], axis=1)
    flow = jnp.concatenate([flow, node_mask.astype(jnp.float32) + 1.0], axis=0)
    flow_off = beyond(flow)
    flow_on = swapped(flow)
    flows = (flow_low, flow_high, node_mask, flow_on, flow_off)
    rendered, field, wide = warp(tile, flows, blended)
    on, rendered = lax.optimization_barrier((on, rendered))
    return (warp_pair(tile, target, share, wide, on, blended, rendered), field)


def solution(mesh):
    return jax.shard_map(
        per_device,
        mesh=mesh,
        in_specs=(
            P("sec", None, "tile", None, None),
            P("sec", None, "tile"),
            P("sec", None, "tile", None),
            P("sec", None, "tile", None),
            P("sec", None, "tile"),
            P("sec", None, "tile", None),
        ),
        out_specs=(P("sec", None, "tile", None, None), P("sec", None, None, "tile")),
        check_vma=False,
    )
```

```python
import functools

import jax
import jax.numpy as jnp
import numpy as np
from jax import lax
from jax.experimental import pallas as pl
from jax.experimental.pallas import tpu as pltpu
from jax.sharding import PartitionSpec as P

K = 4
HB = 2
STEPS = 3
N = 128
HALF = N // 2
PAD = 72
ROW = 32
DEPTH = 2
SPRING = 0.2
EPS = 1e-06
MIB = 1024 * 1024


def split(x):
    high = x.astype(jnp.bfloat16)
    return high, (x - high.astype(jnp.float32)).astype(jnp.bfloat16)


def tables():
    grid = np.arange(N)[:, None] * np.arange(N)[None, :] % N
    cosine = np.cos(2.0 * np.pi * grid / N)
    sine = np.sin(2.0 * np.pi * grid / N)
    rows = np.concatenate([cosine[:HALF], sine[:HALF]])
    rows[HALF] = cosine[HALF]
    cols = np.block([[cosine, -sine], [-sine, -cosine]])
    back_cols = np.block([[cosine, sine], [-sine, cosine]]) / N
    weight = np.where(np.arange(HALF) == 0, 1.0, 2.0)
    back_rows = np.concatenate([cosine[:, :HALF] * weight, -2.0 * sine[:, :HALF]], axis=1) / N
    back_rows[:, HALF] = cosine[:, HALF] / N
    return [jnp.asarray(t, jnp.float32) for t in (rows, cols, back_cols, back_rows)]


def first_row(shape):
    return lax.broadcasted_iota(jnp.int32, shape, len(shape) - 2) == 0


def dot(a, b):
    return jnp.dot(a, b, preferred_element_type=jnp.float32)


def ahead(fetch, rows, depth):
    y = pl.program_id(0)

    @pl.when(y == 0)
    def _():
        for row in range(depth):
            for copy in fetch(row):
                copy.start()

    @pl.when(y + depth < rows)
    def _():
        for copy in fetch(y + depth):
            copy.start()

    for copy in fetch(y):
        copy.wait()


def in_hbm(x):
    return pltpu.with_memory_space_constraint(x, pltpu.HBM)


def in_vmem(x):
    return pltpu.with_memory_space_constraint(x, pltpu.VMEM)


def wait_all(copies):
    @pl.when(pl.program_id(0) == pl.num_programs(0) - 1)
    def _():
        for copy in copies:
            copy.wait()


def forward_kernel(start, toward_pair, tile_ref, x_hbm, rows_hbm, cols_hbm, *refs):
    *refs, x_ref, rest_ref, lines_ref, ends_ref, rows_ref, cols_ref, in_sems, more_sems = refs
    spec_ref, src_ref, *strip_refs = refs[-2 - (HB if toward_pair else 1) :]
    y = pl.program_id(0)
    count, patches = x_ref.shape[:2]
    ny = src_ref.shape[0]
    odd = tile_ref[0] % 2
    column = ((1 - odd) if toward_pair else odd) * (patches - HB)
    rest = (start + count) % ny
    fetch = lambda row: [pltpu.make_async_copy(x_hbm.at[0, start + row], x_ref.at[row], in_sems.at[row])]
    to_strip = lambda i: strip_refs[i].at[:, 0] if toward_pair else strip_refs[0].at[:, i]
    more = [
        pltpu.make_async_copy(rows_hbm, rows_ref, more_sems.at[0]),
        pltpu.make_async_copy(cols_hbm, cols_ref, more_sems.at[1]),
        pltpu.make_async_copy(
            x_hbm.at[0, pl.ds(rest, ny - count), pl.ds(column, HB)], rest_ref, more_sems.at[2]
        ),
    ]

    @pl.when(y == 0)
    def _():
        for copy in more[:2]:
            copy.start()

    ahead(fetch, count, min(DEPTH, count))

    @pl.when(y == 0)
    def _():
        for copy in more[:2]:
            copy.wait()
        more[2].start()

    @pl.when(y == count - 1)
    def _():
        more[2].wait()
        for i in range(HB):
            to_strip(i)[rest : rest + ny - count] = rest_ref[:, i].astype(jnp.bfloat16)

    for i in range(HB):
        to_strip(i)[start + y] = x_ref[y, column + i].astype(jnp.bfloat16)
    rows2 = rows_ref[...]
    cols = cols_ref[...]
    for pair in range(patches // 2):
        x = jnp.concatenate([x_ref[y, 2 * pair], x_ref[y, 2 * pair + 1]], axis=1)
        high, low = split(x)
        src_ref[start + y, 2 * pair] = high[:, :N]
        src_ref[start + y, 2 * pair + 1] = high[:, N:]
        both = dot(rows2, jnp.concatenate([high, low], axis=0))
        for side in range(2):
            here = both[:, side * N : (side + 1) * N]
            p = 2 * pair + side
            ends_ref[p : p + 1, :N] = here[:1]
            ends_ref[p : p + 1, N:] = here[HALF : HALF + 1]
            lines_ref[p * HALF : (p + 1) * HALF, :N] = here[:HALF].astype(jnp.bfloat16)
            lines_ref[p * HALF : (p + 1) * HALF, N:] = here[HALF:].astype(jnp.bfloat16)
    step = 4
    for first in range(0, patches, step):
        lines = lines_ref[first * HALF : (first + step) * HALF, :]
        freq = dot(lines, cols).reshape(step, HALF, 2 * N)
        spec_ref[pl.ds(y * patches + first, step)] = freq.astype(jnp.bfloat16)
    ends = ends_ref[...].astype(jnp.bfloat16)
    spec_ref[count * patches, pl.ds(pl.multiple_of(y * patches, patches), patches), :] = ends


def forward(tile, sections, start, count, toward_pair, source, rows, cols):
    _, ny, nx, _, _ = sections.shape
    rows2 = jnp.concatenate([rows, rows], axis=1).astype(jnp.bfloat16)
    spectra = (count * nx + 1, HALF, 2 * N)
    before = () if source is None else (in_vmem(source),)
    strips = (1,) * HB if toward_pair else (HB,)
    return pl.pallas_call(
        functools.partial(forward_kernel, start, toward_pair),
        grid=(count,),
        in_specs=[pl.BlockSpec(memory_space=pltpu.SMEM)]
        + [pl.BlockSpec(memory_space=pltpu.HBM)] * 3
        + [pl.BlockSpec(memory_space=pltpu.VMEM)] * len(before),
        out_specs=[pl.BlockSpec(memory_space=pltpu.VMEM)] * (2 + len(strips)),
        out_shape=[
            pltpu.VMEM(spectra, jnp.bfloat16),
            pltpu.VMEM((ny, nx, N, N), jnp.bfloat16),
            *(pltpu.VMEM((ny, wide, N, N), jnp.bfloat16) for wide in strips),
        ],
        scratch_shapes=[
            pltpu.VMEM((count, nx, N, N), jnp.float32),
            pltpu.VMEM((ny - count, HB, N, N), jnp.float32),
            pltpu.VMEM((nx * HALF, 2 * N), jnp.bfloat16),
            pltpu.VMEM((nx, 2 * N), jnp.float32),
            pltpu.VMEM((N, 2 * N), jnp.bfloat16),
            pltpu.VMEM((2 * N, 2 * N), jnp.bfloat16),
            pltpu.SemaphoreType.DMA((count,)),
            pltpu.SemaphoreType.DMA((3,)),
        ],
        input_output_aliases={4: 1} if before else {},
        compiler_params=pltpu.CompilerParams(vmem_limit_bytes=12 * MIB),
        cost_estimate=pl.CostEstimate(flops=2_000_000_000, bytes_accessed=6 * MIB, transcendentals=0),
        name="forward",
    )(tile, in_hbm(sections), in_hbm(rows2), in_hbm(cols.astype(jnp.bfloat16)), *before)


def times_conj(a, b, sign):
    ar, ai, br, bi = a[:, :N], a[:, N:], b[:, :N], b[:, N:]
    real = ar * br + ai * bi
    imag = ai * br - ar * bi if sign > 0 else ar * bi - ai * br
    return jnp.concatenate([real, imag], axis=1).astype(jnp.bfloat16)


def flow_kernel(sign, own, other, cols_ref, back_cols_ref, back_rows_ref, flow_ref, sides, sums, moments):
    y = pl.program_id(0)
    ny, patches = sums.shape[:2]
    last = ny * patches
    cols = cols_ref[...]
    back_cols = back_cols_ref[...]
    back_rows = back_rows_ref[...]

    @pl.when(y == 0)
    def _():
        lines = jnp.concatenate([own[last], other[last]], axis=0)
        edge = dot(jnp.concatenate([lines[:, :N], lines[:, N:]], axis=0), cols[:N])
        quarter = edge.reshape(4, last, 2 * N)
        low = times_conj(quarter[0], quarter[1], sign)
        high = times_conj(quarter[2], quarter[3], sign)
        back = dot(jnp.concatenate([low, high], axis=0), back_cols[:, :N])
        sides[...] = back.reshape(sides.shape)

    shift_rows = lax.broadcasted_iota(jnp.int32, (N, N), 0)
    offset_rows = (((shift_rows + HALF) % N) - HALF).astype(jnp.float32)
    offset_rows = jnp.concatenate([offset_rows, offset_rows], axis=1)
    step = 4
    for first in range(0, patches, step):
        here = pl.ds(y * patches + first, step)
        a = own[here].reshape(step * HALF, 2 * N).astype(jnp.float32)
        b = other[here].reshape(step * HALF, 2 * N).astype(jnp.float32)
        back = dot(times_conj(a, b, sign), back_cols)
        halves = []
        for i in range(step):
            p = first + i
            parts = []
            for side in range(2):
                part = back[i * HALF : (i + 1) * HALF, side * N : (side + 1) * N]
                top = jnp.where(first_row((16, N)), sides[side, y, p : p + 1, :], part[:16])
                parts += [top.astype(jnp.bfloat16), part[16:].astype(jnp.bfloat16)]
            halves.append(jnp.concatenate(parts, axis=0))
        for i in range(0, step, 2):
            corr = dot(back_rows, jnp.concatenate(halves[i : i + 2], axis=1))
            power = corr * corr
            total = power.sum(0, keepdims=True)
            moment = (power * offset_rows).sum(0, keepdims=True)
            for side in range(2):
                p = first + i + side
                sums[y, p : p + 1, :] = total[:, side * N : (side + 1) * N]
                moments[y, p : p + 1, :] = moment[:, side * N : (side + 1) * N]

    @pl.when(y == ny - 1)
    def _():
        lane = lax.broadcasted_iota(jnp.int32, (8, N), 1)
        row = lax.broadcasted_iota(jnp.int32, (8, N), 0)
        offset_cols = (((lane + HALF) % N) - HALF).astype(jnp.float32)
        reduce_by = jnp.where(row == 0, 1.0, jnp.where(row == 1, offset_cols, 0.0))
        over_lanes = lambda m: lax.dot_general(
            reduce_by, m.reshape(last, N), (((1,), (1,)), ((), ())),
            precision=lax.Precision.HIGHEST, preferred_element_type=jnp.float32,
        )
        by_sums = over_lanes(sums[...])
        by_moments = over_lanes(moments[...])
        total = by_sums[0:1] + EPS
        along_rows = by_moments[0:1] / total
        along_cols = by_sums[1:2] / total
        for row in range(ny):
            flow_ref[0, row : row + 1, :] = along_rows[:, row * patches : (row + 1) * patches]
            flow_ref[1, row : row + 1, :] = along_cols[:, row * patches : (row + 1) * patches]


def flow_of(own, other, sign, ny, nx, cols, back_cols, back_rows):
    whole = lambda shape: pl.BlockSpec(shape, lambda y: (0,) * len(shape))
    return pl.pallas_call(
        functools.partial(flow_kernel, sign),
        grid=(ny,),
        in_specs=[
            pl.BlockSpec(memory_space=pltpu.VMEM),
            pl.BlockSpec(memory_space=pltpu.VMEM),
            whole((2 * N, 2 * N)),
            whole((2 * N, 2 * N)),
            whole((N, N)),
        ],
        out_specs=whole((2, ny, nx)),
        out_shape=jax.ShapeDtypeStruct((2, ny, nx), jnp.float32),
        scratch_shapes=[
            pltpu.VMEM((2, ny, nx, N), jnp.float32),
            pltpu.VMEM((ny, nx, N), jnp.float32),
            pltpu.VMEM((ny, nx, N), jnp.float32),
        ],
        compiler_params=pltpu.CompilerParams(vmem_limit_bytes=8 * MIB),
        cost_estimate=pl.CostEstimate(flops=0 if sign < 0 else 50_000_000_000, bytes_accessed=0, transcendentals=0),
        name="flow",
    )(in_vmem(own), in_vmem(other), *(t.astype(jnp.bfloat16) for t in (cols, back_cols, back_rows)))


def slots_kernel(tile_ref, rows_ref, shifts_ref, count_ref, weight_ref, target_ref, share_ref):
    ny, _, nx = rows_ref.shape[1:]
    tile, tiles = tile_ref[0], tile_ref[1]
    live = [k < count_ref[0] for k in range(K)]
    weights = [jnp.where(live[k], weight_ref[0, :, k, :], 0.0) for k in range(K)]
    total = weights[0] + weights[1] + weights[2] + weights[3]
    share = [(w / total).astype(jnp.bfloat16).astype(jnp.float32) for w in weights]
    columns = [lax.broadcasted_iota(jnp.int32, (ny, nx), 1) + shifts_ref[0, :, k, :] for k in range(K)]
    rows = [rows_ref[0, :, k, :] * ROW for k in range(K)]
    low = [c < 0 for c in columns]
    high = [c >= nx for c in columns]
    first, last = tile == 0, tile == tiles - 1
    inside = [jnp.where(l | h, 0.0, s) for l, h, s in zip(low, high, share, strict=True)]
    share_low = [jnp.where(first, 0.0, jnp.where(l, s, 0.0)) for l, s in zip(low, share, strict=True)]
    share_high = [jnp.where(last, 0.0, jnp.where(h, s, 0.0)) for h, s in zip(high, share, strict=True)]
    beyond = [l + h for l, h in zip(share_low, share_high, strict=True)]
    share_ref[...] = jnp.concatenate(inside + beyond, axis=1)
    target = [r + jnp.where(l | h, 0, c) for r, c, l, h in zip(rows, columns, low, high, strict=True)]
    away = [
        r + jnp.where(l, c + HB, jnp.where(h, c - nx + HB, 0))
        for r, c, l, h in zip(rows, columns, low, high, strict=True)
    ]
    target_ref[...] = jnp.concatenate(target + away, axis=1)


def slots_of(tile, box_row, box_shift, box_count, blend_weight):
    ny = box_row.shape[1]
    slots_first = lambda x: jnp.transpose(x, (0, 1, 3, 2))
    return pl.pallas_call(
        slots_kernel,
        in_specs=[pl.BlockSpec(memory_space=pltpu.SMEM)] + [pl.BlockSpec(memory_space=pltpu.VMEM)] * 4,
        out_shape=[
            jax.ShapeDtypeStruct((ny, N), jnp.int32),
            jax.ShapeDtypeStruct((ny, N), jnp.float32),
        ],
        compiler_params=pltpu.CompilerParams(vmem_limit_bytes=4 * MIB),
        cost_estimate=pl.CostEstimate(flops=0, bytes_accessed=0, transcendentals=0),
        name="slots",
    )(tile, slots_first(box_row), slots_first(box_shift), box_count, slots_first(blend_weight))


def blend_cell(y, first, nx, target_ref, share_ref, window):
    total = None
    for k in range(K):
        spot = target_ref[y, first + k * nx]
        piece = window[spot // ROW, spot % ROW].astype(jnp.float32) * share_ref[y, first + k * nx]
        total = piece if total is None else total + piece
    return total


def blend_kernel(target_ref, share_ref, source, out_ref):
    y = pl.program_id(0)
    nx = source.shape[1]
    border = jnp.zeros((nx, PAD, N), jnp.float32)
    out_ref[y, :, :PAD] = border
    out_ref[y, :, PAD + N :] = border
    for x in range(nx):
        out_ref[y, x, PAD : PAD + N] = blend_cell(y, x, nx, target_ref, share_ref, source)


def blend(target, share, source):
    ny, nx = source.shape[:2]
    return pl.pallas_call(
        blend_kernel,
        grid=(ny,),
        in_specs=[pl.BlockSpec(memory_space=pltpu.SMEM)] * 2 + [pl.BlockSpec(memory_space=pltpu.VMEM)],
        out_specs=pl.BlockSpec(memory_space=pltpu.VMEM),
        out_shape=pltpu.VMEM((ny, nx, N + 2 * PAD, N), jnp.float32),
        compiler_params=pltpu.CompilerParams(vmem_limit_bytes=4 * MIB),
        cost_estimate=pl.CostEstimate(flops=16_000_000_000, bytes_accessed=4 * MIB, transcendentals=0),
        name="blend",
    )(target, share, in_vmem(source))


def relax(tile_ref, low_ref, high_ref, mask_ref, on_ref, off_ref):
    ny, nx = mask_ref.shape[1:]
    even = tile_ref[0] % 2 == 0
    left_ref = [jnp.where(even, off_ref[i], on_ref[i]) for i in range(3)]
    right_ref = [jnp.where(even, on_ref[i], off_ref[i]) for i in range(3)]
    rest = jnp.zeros((ny, N - nx - 2 * STEPS), jnp.float32)

    def across(left, own, right):
        return jnp.concatenate([left[:, nx - STEPS :], own, right[:, :STEPS], rest], axis=1)

    known = across(left_ref[2], mask_ref[0].astype(jnp.float32) + 1.0, right_ref[2])
    valid = jnp.where(known > 0.5, 1.0, 0.0)
    trust = jnp.where(known > 1.5, 1.0, 0.0)
    row = lax.broadcasted_iota(jnp.int32, trust.shape, 0)
    fields = []
    for component in range(2):
        own = jnp.concatenate([low_ref[component], high_ref[component]], axis=0)
        flow = across(left_ref[component], own, right_ref[component])
        field = trust * flow
        for _ in range(STEPS):
            below = jnp.where(row == 0, 0.0, pltpu.roll(field, 1, 0))
            above = jnp.where(row == ny - 1, 0.0, pltpu.roll(field, ny - 1, 0))
            beside = pltpu.roll(field, 1, 1) + pltpu.roll(field, N - 1, 1)
            lap = above + below + beside - 4.0 * field
            field = (field + SPRING * (lap + trust * (flow - field))) * valid
        fields.append(field)
    return fields


def edge_kernel(tile_ref, target_ref, share_ref, first_ref, second_ref, off_ref, padded, out_ref, window, sems):
    y = pl.program_id(0)
    ny, nx = padded.shape[:2]
    even = tile_ref[0] % 2 == 0
    halos = {
        side: ((first_ref, on_at), (second_ref, on_at + 1), (off_ref, HB - on_at))
        for side, on_at in ((True, HB), (False, 0))
    }
    copies = {
        side: [
            pltpu.make_async_copy(ref, window.at[:, into : into + ref.shape[1]], sems.at[i])
            for i, (ref, into) in enumerate(places)
        ]
        for side, places in halos.items()
    }

    @pl.when((y == 0) & even)
    def _():
        for copy in copies[True]:
            copy.start()

    @pl.when((y == 0) & jnp.logical_not(even))
    def _():
        for copy in copies[False]:
            copy.start()

    border = jnp.zeros((2 * HB, PAD, N), jnp.float32)
    out_ref[y, :, :PAD] = border
    out_ref[y, :, PAD + N :] = border

    @pl.when(y == 0)
    def _():
        for copy in copies[True]:
            copy.wait()

    for i, x in enumerate((*range(HB), *range(nx - HB, nx))):
        more = blend_cell(y, K * nx + x, nx, target_ref, share_ref, window)
        out_ref[y, i, PAD : PAD + N] = padded[y, x, PAD : PAD + N] + more


def edges_of(tile, target, share, first, second, off, blended):
    ny, _, tall, _ = blended.shape
    vmem = pl.BlockSpec(memory_space=pltpu.VMEM)
    return pl.pallas_call(
        edge_kernel,
        grid=(ny,),
        in_specs=[pl.BlockSpec(memory_space=pltpu.SMEM)] * 3 + [vmem] * 4,
        out_specs=vmem,
        out_shape=pltpu.VMEM((ny, 2 * HB, tall, N), jnp.float32),
        scratch_shapes=[pltpu.VMEM((ny, 2 * HB, N, N), jnp.bfloat16), pltpu.SemaphoreType.DMA((3,))],
        compiler_params=pltpu.CompilerParams(vmem_limit_bytes=4 * MIB),
        cost_estimate=pl.CostEstimate(flops=5_000_000, bytes_accessed=4 * MIB, transcendentals=0),
        name="edges",
    )(tile, target, share, in_vmem(first), in_vmem(second), in_vmem(off), in_vmem(blended))


def warped(cell, down_shift, right_shift):
    whole_of = lambda shift: (shift + 256.0).astype(jnp.int32) - 256
    line = lambda value: jnp.full((1, N), value, jnp.float32).astype(jnp.bfloat16)
    down = jnp.clip(whole_of(down_shift), 4 - PAD, PAD - 6)
    part = down_shift - down.astype(jnp.float32)
    upper = cell[pl.ds(PAD + down, N), :]
    lower = cell[pl.ds(PAD + 1 + down, N), :]
    image = upper + part * (lower - upper)
    right = whole_of(right_shift).astype(jnp.float32)
    apart = lax.broadcasted_iota(jnp.int32, (N, N), 0) - lax.broadcasted_iota(jnp.int32, (N, N), 1)
    apart = apart.astype(jnp.bfloat16) - line(right)
    one = jnp.bfloat16(1.0)
    hat = jnp.maximum(jnp.bfloat16(0.0), one - jnp.abs(apart - line(right_shift - right)))
    return dot(image.astype(jnp.bfloat16), hat).astype(jnp.bfloat16)


def warp_kernel(tile_ref, *refs):
    *flows, padded, edges, out_hbm, field_ref, out, wide, field, sem, out_sems = refs
    y = pl.program_id(0)
    ny, nx = out.shape[:2]

    @pl.when(y == 0)
    def _():
        for component, values in enumerate(relax(tile_ref, *flows)):
            wide[component] = values
            field_ref[0, component] = values[:, STEPS : STEPS + nx]
        scalars = pltpu.make_async_copy(wide, field, sem)
        scalars.start()
        scalars.wait()

    borders = (*range(HB), *range(nx - HB, nx))
    for x in range(nx):
        cell = edges.at[y, borders.index(x)] if x in borders else padded.at[y, x]
        out[y, x] = warped(cell, field[0, y, STEPS + x], field[1, y, STEPS + x])
    store = lambda row: pltpu.make_async_copy(out.at[row], out_hbm.at[0, row], out_sems.at[row])
    store(y).start()
    wait_all([store(row) for row in range(ny)])


def warp(tile, flows, blended, edges):
    ny, nx = blended.shape[:2]
    whole = lambda shape: pl.BlockSpec(shape, lambda y: (0,) * len(shape))
    return pl.pallas_call(
        warp_kernel,
        grid=(ny,),
        in_specs=[pl.BlockSpec(memory_space=pltpu.SMEM)]
        + [whole(x.shape) for x in flows]
        + [pl.BlockSpec(memory_space=pltpu.VMEM)] * 2,
        out_specs=[pl.BlockSpec(memory_space=pl.ANY), whole((1, 2, ny, nx))],
        out_shape=[
            jax.ShapeDtypeStruct((1, ny, nx, N, N), jnp.bfloat16),
            jax.ShapeDtypeStruct((1, 2, ny, nx), jnp.float32),
        ],
        scratch_shapes=[
            pltpu.VMEM((ny, nx, N, N), jnp.bfloat16),
            pltpu.VMEM((2, ny, N), jnp.float32),
            pltpu.SMEM((2, ny, N), jnp.float32),
            pltpu.SemaphoreType.DMA,
            pltpu.SemaphoreType.DMA((ny,)),
        ],
        compiler_params=pltpu.CompilerParams(vmem_limit_bytes=8 * MIB),
        cost_estimate=pl.CostEstimate(flops=20_000_000, bytes_accessed=12 * MIB, transcendentals=0),
        name="warp",
    )(tile, *flows, in_vmem(blended), in_vmem(edges))


def from_behind(x, axis, by):
    length = lax.axis_size(axis)
    pairs = [(i, i + by) for i in range(length) if 0 <= i + by < length]
    return lax.ppermute(x, axis, pairs)


def swapped(x):
    return lax.ppermute(x, "tile", [(i, i ^ 1) for i in range(lax.axis_size("tile"))])


def hops(tiles, sections, far):
    pairs = ([], [])
    for section in range(sections):
        x_low, rest = divmod(section, sections // 2)
        way = 1 if rest < sections // 4 else -1
        for tile in range(tiles):
            z, x_high = divmod(tile, 2)
            ends = [section * tiles + tile]
            for hop in (1, 2):
                x = (2 * x_high + x_low + hop * way) % 4
                to_z = (z + 2 * x_high - 1) % (tiles // 2) if far and hop == 2 else z
                ends.append((x % 2 * (sections // 2) + rest) * tiles + 2 * to_z + x // 2)
            pairs[0].append((ends[0], ends[1]))
            pairs[1].append((ends[1], ends[2]))
    return pairs


def beyond(x):
    tiles = lax.axis_size("tile")
    pairs = [(i, i + 1) for i in range(1, tiles - 1, 2)]
    return lax.ppermute(x, "tile", pairs + [(j, i) for i, j in pairs])


def per_device(sections, node_mask, box_row, box_shift, box_count, blend_weight):
    ny, nx = sections.shape[1:3]
    rows, cols, back_cols, back_rows = tables()
    half = ny // 2
    tiles, count = lax.axis_size("tile"), lax.axis_size("sec")
    tile = jnp.stack([lax.axis_index("tile"), tiles]).astype(jnp.int32)
    on_hops, off_hops = hops(tiles, count, False), hops(tiles, count, True)
    hop = lambda x, pairs: lax.ppermute(x, ("sec", "tile"), pairs)

    spectra_high, source, off = forward(tile, sections, half, half, False, None, rows, cols)
    from_last = from_behind(spectra_high, "sec", 1)
    off = hop(off, off_hops[0])
    spectra_low, source, first, second = forward(tile, sections, 0, half, True, source, rows, cols)
    from_next = from_behind(spectra_low, "sec", -1)
    first = hop(first, on_hops[0])
    target, share = slots_of(tile, box_row, box_shift, box_count, blend_weight)
    off, source = lax.optimization_barrier((off, source))
    off = hop(off, off_hops[1])
    blended = blend(target, share, source)
    first, blended = lax.optimization_barrier((first, blended))
    first = hop(first, on_hops[1])
    from_last, blended = lax.optimization_barrier((from_last, blended))

    flow_high = flow_of(spectra_high, from_last, -1, half, nx, cols, back_cols, back_rows)
    second, flow_high = lax.optimization_barrier((second, flow_high))
    flow_high = from_behind(flow_high, "sec", -1)
    second = swapped(second)
    from_next, flow_high, off, first = lax.optimization_barrier((from_next, flow_high, off, first))
    flow_low = flow_of(spectra_low, from_next, 1, half, nx, cols, back_cols, back_rows)
    flow = jnp.concatenate([flow_low, flow_high], axis=1)
    flow = jnp.concatenate([flow, node_mask.astype(jnp.float32) + 1.0], axis=0)
    flow_off = beyond(flow)
    flow_on = swapped(flow)
    flows = (flow_low, flow_high, node_mask, flow_on, flow_off)
    edges = edges_of(tile, target, share, first, second, off, blended)
    return tuple(warp(tile, flows, blended, edges))


def solution(mesh):
    return jax.shard_map(
        per_device,
        mesh=mesh,
        in_specs=(
            P("sec", None, "tile", None, None),
            P("sec", None, "tile"),
            P("sec", None, "tile", None),
            P("sec", None, "tile", None),
            P("sec", None, "tile"),
            P("sec", None, "tile", None),
        ),
        out_specs=(P("sec", None, "tile", None, None), P("sec", None, None, "tile")),
        check_vma=False,
    )
```

```python
import functools

import jax
import jax.numpy as jnp
import numpy as np
from jax import lax
from jax.experimental import pallas as pl
from jax.experimental.pallas import tpu as pltpu
from jax.sharding import PartitionSpec as P

K = 4
HB = 2
STEPS = 3
N = 128
HALF = N // 2
PAD = 72
ROW = 32
DEPTH = 2
SPRING = 0.2
EPS = 1e-06
MIB = 1024 * 1024


def split(x):
    high = x.astype(jnp.bfloat16)
    return high, (x - high.astype(jnp.float32)).astype(jnp.bfloat16)


def tables():
    grid = np.arange(N)[:, None] * np.arange(N)[None, :] % N
    cosine = np.cos(2.0 * np.pi * grid / N)
    sine = np.sin(2.0 * np.pi * grid / N)
    rows = np.concatenate([cosine[:HALF], sine[:HALF]])
    rows[HALF] = cosine[HALF]
    cols = np.block([[cosine, -sine], [-sine, -cosine]])
    back_cols = np.block([[cosine, sine], [-sine, cosine]]) / N
    weight = np.where(np.arange(HALF) == 0, 1.0, 2.0)
    back_rows = np.concatenate([cosine[:, :HALF] * weight, -2.0 * sine[:, :HALF]], axis=1) / N
    back_rows[:, HALF] = cosine[:, HALF] / N
    return [jnp.asarray(t, jnp.float32) for t in (rows, cols, back_cols, back_rows)]


def first_row(shape):
    return lax.broadcasted_iota(jnp.int32, shape, len(shape) - 2) == 0


def dot(a, b):
    return jnp.dot(a, b, preferred_element_type=jnp.float32)


def ahead(fetch, rows, depth):
    y = pl.program_id(0)

    @pl.when(y == 0)
    def _():
        for row in range(depth):
            for copy in fetch(row):
                copy.start()

    @pl.when(y + depth < rows)
    def _():
        for copy in fetch(y + depth):
            copy.start()

    for copy in fetch(y):
        copy.wait()


def in_hbm(x):
    return pltpu.with_memory_space_constraint(x, pltpu.HBM)


def in_vmem(x):
    return pltpu.with_memory_space_constraint(x, pltpu.VMEM)


def wait_all(copies):
    @pl.when(pl.program_id(0) == pl.num_programs(0) - 1)
    def _():
        for copy in copies:
            copy.wait()


def forward_kernel(start, toward_pair, tile_ref, x_hbm, rows_hbm, cols_hbm, *refs):
    *refs, x_ref, rest_ref, lines_ref, ends_ref, rows_ref, cols_ref, in_sems, more_sems = refs
    spec_ref, src_ref, *strip_refs = refs[-2 - (HB if toward_pair else 1) :]
    y = pl.program_id(0)
    count, patches = x_ref.shape[:2]
    ny = src_ref.shape[0]
    odd = tile_ref[0] % 2
    column = ((1 - odd) if toward_pair else odd) * (patches - HB)
    rest = (start + count) % ny
    fetch = lambda row: [pltpu.make_async_copy(x_hbm.at[0, start + row], x_ref.at[row], in_sems.at[row])]
    to_strip = lambda i: strip_refs[i].at[:, 0] if toward_pair else strip_refs[0].at[:, i]
    more = [
        pltpu.make_async_copy(rows_hbm, rows_ref, more_sems.at[0]),
        pltpu.make_async_copy(cols_hbm, cols_ref, more_sems.at[1]),
        pltpu.make_async_copy(
            x_hbm.at[0, pl.ds(rest, ny - count), pl.ds(column, HB)], rest_ref, more_sems.at[2]
        ),
    ]

    @pl.when(y == 0)
    def _():
        for copy in more[:2]:
            copy.start()

    ahead(fetch, count, min(DEPTH, count))

    @pl.when(y == 0)
    def _():
        for copy in more[:2]:
            copy.wait()
        more[2].start()

    @pl.when(y == count - 1)
    def _():
        more[2].wait()
        for i in range(HB):
            to_strip(i)[rest : rest + ny - count] = rest_ref[:, i].astype(jnp.bfloat16)

    for i in range(HB):
        to_strip(i)[start + y] = x_ref[y, column + i].astype(jnp.bfloat16)
    rows2 = rows_ref[...]
    cols = cols_ref[...]
    for pair in range(patches // 2):
        x = jnp.concatenate([x_ref[y, 2 * pair], x_ref[y, 2 * pair + 1]], axis=1)
        high, low = split(x)
        src_ref[start + y, 2 * pair] = high[:, :N]
        src_ref[start + y, 2 * pair + 1] = high[:, N:]
        both = dot(rows2, jnp.concatenate([high, low], axis=0))
        for side in range(2):
            here = both[:, side * N : (side + 1) * N]
            p = 2 * pair + side
            ends_ref[p : p + 1, :N] = here[:1]
            ends_ref[p : p + 1, N:] = here[HALF : HALF + 1]
            lines_ref[p * HALF : (p + 1) * HALF, :N] = here[:HALF].astype(jnp.bfloat16)
            lines_ref[p * HALF : (p + 1) * HALF, N:] = here[HALF:].astype(jnp.bfloat16)
    step = 4
    for first in range(0, patches, step):
        lines = lines_ref[first * HALF : (first + step) * HALF, :]
        freq = dot(lines, cols).reshape(step, HALF, 2 * N)
        spec_ref[pl.ds(y * patches + first, step)] = freq.astype(jnp.bfloat16)
    ends = ends_ref[...].astype(jnp.bfloat16)
    spec_ref[count * patches, pl.ds(pl.multiple_of(y * patches, patches), patches), :] = ends


def forward(tile, sections, start, count, toward_pair, source, rows, cols):
    _, ny, nx, _, _ = sections.shape
    rows2 = jnp.concatenate([rows, rows], axis=1).astype(jnp.bfloat16)
    spectra = (count * nx + 1, HALF, 2 * N)
    before = () if source is None else (in_vmem(source),)
    strips = (1,) * HB if toward_pair else (HB,)
    return pl.pallas_call(
        functools.partial(forward_kernel, start, toward_pair),
        grid=(count,),
        in_specs=[pl.BlockSpec(memory_space=pltpu.SMEM)]
        + [pl.BlockSpec(memory_space=pltpu.HBM)] * 3
        + [pl.BlockSpec(memory_space=pltpu.VMEM)] * len(before),
        out_specs=[pl.BlockSpec(memory_space=pltpu.VMEM)] * (2 + len(strips)),
        out_shape=[
            pltpu.VMEM(spectra, jnp.bfloat16),
            pltpu.VMEM((ny, nx, N, N), jnp.bfloat16),
            *(pltpu.VMEM((ny, wide, N, N), jnp.bfloat16) for wide in strips),
        ],
        scratch_shapes=[
            pltpu.VMEM((count, nx, N, N), jnp.float32),
            pltpu.VMEM((ny - count, HB, N, N), jnp.float32),
            pltpu.VMEM((nx * HALF, 2 * N), jnp.bfloat16),
            pltpu.VMEM((nx, 2 * N), jnp.float32),
            pltpu.VMEM((N, 2 * N), jnp.bfloat16),
            pltpu.VMEM((2 * N, 2 * N), jnp.bfloat16),
            pltpu.SemaphoreType.DMA((count,)),
            pltpu.SemaphoreType.DMA((3,)),
        ],
        input_output_aliases={4: 1} if before else {},
        compiler_params=pltpu.CompilerParams(vmem_limit_bytes=12 * MIB),
        cost_estimate=pl.CostEstimate(flops=2_000_000_000, bytes_accessed=6 * MIB, transcendentals=0),
        name="forward",
    )(tile, in_hbm(sections), in_hbm(rows2), in_hbm(cols.astype(jnp.bfloat16)), *before)


def times_conj(a, b, sign):
    ar, ai, br, bi = a[:, :N], a[:, N:], b[:, :N], b[:, N:]
    real = ar * br + ai * bi
    imag = ai * br - ar * bi if sign > 0 else ar * bi - ai * br
    return jnp.concatenate([real, imag], axis=1).astype(jnp.bfloat16)


def flow_kernel(sign, own, other, cols_ref, back_cols_ref, back_rows_ref, flow_ref, sides, sums, moments):
    y = pl.program_id(0)
    ny, patches = sums.shape[:2]
    last = ny * patches
    cols = cols_ref[...]
    back_cols = back_cols_ref[...]
    back_rows = back_rows_ref[...]

    @pl.when(y == 0)
    def _():
        lines = jnp.concatenate([own[last], other[last]], axis=0)
        edge = dot(jnp.concatenate([lines[:, :N], lines[:, N:]], axis=0), cols[:N])
        quarter = edge.reshape(4, last, 2 * N)
        low = times_conj(quarter[0], quarter[1], sign)
        high = times_conj(quarter[2], quarter[3], sign)
        back = dot(jnp.concatenate([low, high], axis=0), back_cols[:, :N])
        sides[...] = back.reshape(sides.shape)

    shift_rows = lax.broadcasted_iota(jnp.int32, (N, N), 0)
    offset_rows = (((shift_rows + HALF) % N) - HALF).astype(jnp.float32)
    offset_rows = jnp.concatenate([offset_rows, offset_rows], axis=1)
    step = 4
    for first in range(0, patches, step):
        here = pl.ds(y * patches + first, step)
        a = own[here].reshape(step * HALF, 2 * N).astype(jnp.float32)
        b = other[here].reshape(step * HALF, 2 * N).astype(jnp.float32)
        back = dot(times_conj(a, b, sign), back_cols)
        halves = []
        for i in range(step):
            p = first + i
            parts = []
            for side in range(2):
                part = back[i * HALF : (i + 1) * HALF, side * N : (side + 1) * N]
                top = jnp.where(first_row((16, N)), sides[side, y, p : p + 1, :], part[:16])
                parts += [top.astype(jnp.bfloat16), part[16:].astype(jnp.bfloat16)]
            halves.append(jnp.concatenate(parts, axis=0))
        for i in range(0, step, 2):
            corr = dot(back_rows, jnp.concatenate(halves[i : i + 2], axis=1))
            power = corr * corr
            total = power.sum(0, keepdims=True)
            moment = (power * offset_rows).sum(0, keepdims=True)
            for side in range(2):
                p = first + i + side
                sums[y, p : p + 1, :] = total[:, side * N : (side + 1) * N]
                moments[y, p : p + 1, :] = moment[:, side * N : (side + 1) * N]

    @pl.when(y == ny - 1)
    def _():
        lane = lax.broadcasted_iota(jnp.int32, (8, N), 1)
        row = lax.broadcasted_iota(jnp.int32, (8, N), 0)
        offset_cols = (((lane + HALF) % N) - HALF).astype(jnp.float32)
        reduce_by = jnp.where(row == 0, 1.0, jnp.where(row == 1, offset_cols, 0.0))
        over_lanes = lambda m: lax.dot_general(
            reduce_by, m.reshape(last, N), (((1,), (1,)), ((), ())),
            precision=lax.Precision.HIGHEST, preferred_element_type=jnp.float32,
        )
        by_sums = over_lanes(sums[...])
        by_moments = over_lanes(moments[...])
        total = by_sums[0:1] + EPS
        along_rows = by_moments[0:1] / total
        along_cols = by_sums[1:2] / total
        for row in range(ny):
            flow_ref[0, row : row + 1, :] = along_rows[:, row * patches : (row + 1) * patches]
            flow_ref[1, row : row + 1, :] = along_cols[:, row * patches : (row + 1) * patches]


def flow_of(own, other, sign, ny, nx, cols, back_cols, back_rows):
    whole = lambda shape: pl.BlockSpec(shape, lambda y: (0,) * len(shape))
    return pl.pallas_call(
        functools.partial(flow_kernel, sign),
        grid=(ny,),
        in_specs=[
            pl.BlockSpec(memory_space=pltpu.VMEM),
            pl.BlockSpec(memory_space=pltpu.VMEM),
            whole((2 * N, 2 * N)),
            whole((2 * N, 2 * N)),
            whole((N, N)),
        ],
        out_specs=whole((2, ny, nx)),
        out_shape=jax.ShapeDtypeStruct((2, ny, nx), jnp.float32),
        scratch_shapes=[
            pltpu.VMEM((2, ny, nx, N), jnp.float32),
            pltpu.VMEM((ny, nx, N), jnp.float32),
            pltpu.VMEM((ny, nx, N), jnp.float32),
        ],
        compiler_params=pltpu.CompilerParams(vmem_limit_bytes=8 * MIB),
        cost_estimate=pl.CostEstimate(flops=0 if sign < 0 else 0, bytes_accessed=0, transcendentals=0),
        name="flow",
    )(in_vmem(own), in_vmem(other), *(t.astype(jnp.bfloat16) for t in (cols, back_cols, back_rows)))


def slots_kernel(tile_ref, rows_ref, shifts_ref, count_ref, weight_ref, target_ref, share_ref):
    ny, _, nx = rows_ref.shape[1:]
    tile, tiles = tile_ref[0], tile_ref[1]
    live = [k < count_ref[0] for k in range(K)]
    weights = [jnp.where(live[k], weight_ref[0, :, k, :], 0.0) for k in range(K)]
    total = weights[0] + weights[1] + weights[2] + weights[3]
    share = [(w / total).astype(jnp.bfloat16).astype(jnp.float32) for w in weights]
    columns = [lax.broadcasted_iota(jnp.int32, (ny, nx), 1) + shifts_ref[0, :, k, :] for k in range(K)]
    rows = [rows_ref[0, :, k, :] * ROW for k in range(K)]
    low = [c < 0 for c in columns]
    high = [c >= nx for c in columns]
    first, last = tile == 0, tile == tiles - 1
    inside = [jnp.where(l | h, 0.0, s) for l, h, s in zip(low, high, share, strict=True)]
    share_low = [jnp.where(first, 0.0, jnp.where(l, s, 0.0)) for l, s in zip(low, share, strict=True)]
    share_high = [jnp.where(last, 0.0, jnp.where(h, s, 0.0)) for h, s in zip(high, share, strict=True)]
    beyond = [l + h for l, h in zip(share_low, share_high, strict=True)]
    share_ref[...] = jnp.concatenate(inside + beyond, axis=1)
    target = [r + jnp.where(l | h, 0, c) for r, c, l, h in zip(rows, columns, low, high, strict=True)]
    away = [
        r + jnp.where(l, c + HB, jnp.where(h, c - nx + HB, 0))
        for r, c, l, h in zip(rows, columns, low, high, strict=True)
    ]
    target_ref[...] = jnp.concatenate(target + away, axis=1)


def slots_of(tile, box_row, box_shift, box_count, blend_weight):
    ny = box_row.shape[1]
    slots_first = lambda x: jnp.transpose(x, (0, 1, 3, 2))
    return pl.pallas_call(
        slots_kernel,
        in_specs=[pl.BlockSpec(memory_space=pltpu.SMEM)] + [pl.BlockSpec(memory_space=pltpu.VMEM)] * 4,
        out_shape=[
            jax.ShapeDtypeStruct((ny, N), jnp.int32),
            jax.ShapeDtypeStruct((ny, N), jnp.float32),
        ],
        compiler_params=pltpu.CompilerParams(vmem_limit_bytes=4 * MIB),
        cost_estimate=pl.CostEstimate(flops=0, bytes_accessed=0, transcendentals=0),
        name="slots",
    )(tile, slots_first(box_row), slots_first(box_shift), box_count, slots_first(blend_weight))


def blend_cell(y, first, nx, target_ref, share_ref, window):
    total = None
    for k in range(K):
        spot = target_ref[y, first + k * nx]
        piece = window[spot // ROW, spot % ROW].astype(jnp.float32) * share_ref[y, first + k * nx]
        total = piece if total is None else total + piece
    return total


def blend_kernel(target_ref, share_ref, source, out_ref):
    y = pl.program_id(0)
    nx = source.shape[1]
    border = jnp.zeros((nx, PAD, N), jnp.float32)
    out_ref[y, :, :PAD] = border
    out_ref[y, :, PAD + N :] = border
    for x in range(nx):
        out_ref[y, x, PAD : PAD + N] = blend_cell(y, x, nx, target_ref, share_ref, source)


def blend(target, share, source):
    ny, nx = source.shape[:2]
    return pl.pallas_call(
        blend_kernel,
        grid=(ny,),
        in_specs=[pl.BlockSpec(memory_space=pltpu.SMEM)] * 2 + [pl.BlockSpec(memory_space=pltpu.VMEM)],
        out_specs=pl.BlockSpec(memory_space=pltpu.VMEM),
        out_shape=pltpu.VMEM((ny, nx, N + 2 * PAD, N), jnp.float32),
        compiler_params=pltpu.CompilerParams(vmem_limit_bytes=4 * MIB),
        cost_estimate=pl.CostEstimate(flops=16_000_000_000, bytes_accessed=4 * MIB, transcendentals=0),
        name="blend",
    )(target, share, in_vmem(source))


def relax(tile_ref, low_ref, high_ref, mask_ref, on_ref, off_ref):
    ny, nx = mask_ref.shape[1:]
    even = tile_ref[0] % 2 == 0
    left_ref = [jnp.where(even, off_ref[i], on_ref[i]) for i in range(3)]
    right_ref = [jnp.where(even, on_ref[i], off_ref[i]) for i in range(3)]
    rest = jnp.zeros((ny, N - nx - 2 * STEPS), jnp.float32)

    def across(left, own, right):
        return jnp.concatenate([left[:, nx - STEPS :], own, right[:, :STEPS], rest], axis=1)

    known = across(left_ref[2], mask_ref[0].astype(jnp.float32) + 1.0, right_ref[2])
    valid = jnp.where(known > 0.5, 1.0, 0.0)
    trust = jnp.where(known > 1.5, 1.0, 0.0)
    row = lax.broadcasted_iota(jnp.int32, trust.shape, 0)
    fields = []
    for component in range(2):
        own = jnp.concatenate([low_ref[component], high_ref[component]], axis=0)
        flow = across(left_ref[component], own, right_ref[component])
        field = trust * flow
        for _ in range(STEPS):
            below = jnp.where(row == 0, 0.0, pltpu.roll(field, 1, 0))
            above = jnp.where(row == ny - 1, 0.0, pltpu.roll(field, ny - 1, 0))
            beside = pltpu.roll(field, 1, 1) + pltpu.roll(field, N - 1, 1)
            lap = above + below + beside - 4.0 * field
            field = (field + SPRING * (lap + trust * (flow - field))) * valid
        fields.append(field)
    return fields


def edge_kernel(tile_ref, target_ref, share_ref, first_ref, second_ref, off_ref, padded, out_ref, window, sems):
    y = pl.program_id(0)
    ny, nx = padded.shape[:2]
    even = tile_ref[0] % 2 == 0
    halos = {
        side: ((first_ref, on_at), (second_ref, on_at + 1), (off_ref, HB - on_at))
        for side, on_at in ((True, HB), (False, 0))
    }
    copies = {
        side: [
            pltpu.make_async_copy(ref, window.at[:, into : into + ref.shape[1]], sems.at[i])
            for i, (ref, into) in enumerate(places)
        ]
        for side, places in halos.items()
    }

    @pl.when((y == 0) & even)
    def _():
        for copy in copies[True]:
            copy.start()

    @pl.when((y == 0) & jnp.logical_not(even))
    def _():
        for copy in copies[False]:
            copy.start()

    border = jnp.zeros((2 * HB, PAD, N), jnp.float32)
    out_ref[y, :, :PAD] = border
    out_ref[y, :, PAD + N :] = border

    @pl.when(y == 0)
    def _():
        for copy in copies[True]:
            copy.wait()

    for i, x in enumerate((*range(HB), *range(nx - HB, nx))):
        more = blend_cell(y, K * nx + x, nx, target_ref, share_ref, window)
        out_ref[y, i, PAD : PAD + N] = padded[y, x, PAD : PAD + N] + more


def edges_of(tile, target, share, first, second, off, blended):
    ny, _, tall, _ = blended.shape
    vmem = pl.BlockSpec(memory_space=pltpu.VMEM)
    return pl.pallas_call(
        edge_kernel,
        grid=(ny,),
        in_specs=[pl.BlockSpec(memory_space=pltpu.SMEM)] * 3 + [vmem] * 4,
        out_specs=vmem,
        out_shape=pltpu.VMEM((ny, 2 * HB, tall, N), jnp.float32),
        scratch_shapes=[pltpu.VMEM((ny, 2 * HB, N, N), jnp.bfloat16), pltpu.SemaphoreType.DMA((3,))],
        compiler_params=pltpu.CompilerParams(vmem_limit_bytes=4 * MIB),
        cost_estimate=pl.CostEstimate(flops=5_000_000, bytes_accessed=4 * MIB, transcendentals=0),
        name="edges",
    )(tile, target, share, in_vmem(first), in_vmem(second), in_vmem(off), in_vmem(blended))


def warped(cell, down_shift, right_shift):
    whole_of = lambda shift: (shift + 256.0).astype(jnp.int32) - 256
    line = lambda value: jnp.full((1, N), value, jnp.float32).astype(jnp.bfloat16)
    down = jnp.clip(whole_of(down_shift), 4 - PAD, PAD - 6)
    part = down_shift - down.astype(jnp.float32)
    upper = cell[pl.ds(PAD + down, N), :]
    lower = cell[pl.ds(PAD + 1 + down, N), :]
    image = upper + part * (lower - upper)
    right = whole_of(right_shift).astype(jnp.float32)
    apart = lax.broadcasted_iota(jnp.int32, (N, N), 0) - lax.broadcasted_iota(jnp.int32, (N, N), 1)
    apart = apart.astype(jnp.bfloat16) - line(right)
    one = jnp.bfloat16(1.0)
    hat = jnp.maximum(jnp.bfloat16(0.0), one - jnp.abs(apart - line(right_shift - right)))
    return dot(image.astype(jnp.bfloat16), hat).astype(jnp.bfloat16)


def warp_kernel(tile_ref, *refs):
    *flows, padded, edges, out_hbm, field_ref, out, wide, field, sem, out_sems = refs
    y = pl.program_id(0)
    ny, nx = out.shape[:2]

    @pl.when(y == 0)
    def _():
        for component, values in enumerate(relax(tile_ref, *flows)):
            wide[component] = values
            field_ref[0, component] = values[:, STEPS : STEPS + nx]
        scalars = pltpu.make_async_copy(wide, field, sem)
        scalars.start()
        scalars.wait()

    borders = (*range(HB), *range(nx - HB, nx))
    for x in range(nx):
        cell = edges.at[y, borders.index(x)] if x in borders else padded.at[y, x]
        out[y, x] = warped(cell, field[0, y, STEPS + x], field[1, y, STEPS + x])
    store = lambda row: pltpu.make_async_copy(out.at[row], out_hbm.at[0, row], out_sems.at[row])
    store(y).start()
    wait_all([store(row) for row in range(ny)])


def warp(tile, flows, blended, edges):
    ny, nx = blended.shape[:2]
    whole = lambda shape: pl.BlockSpec(shape, lambda y: (0,) * len(shape))
    return pl.pallas_call(
        warp_kernel,
        grid=(ny,),
        in_specs=[pl.BlockSpec(memory_space=pltpu.SMEM)]
        + [whole(x.shape) for x in flows]
        + [pl.BlockSpec(memory_space=pltpu.VMEM)] * 2,
        out_specs=[pl.BlockSpec(memory_space=pl.ANY), whole((1, 2, ny, nx))],
        out_shape=[
            jax.ShapeDtypeStruct((1, ny, nx, N, N), jnp.bfloat16),
            jax.ShapeDtypeStruct((1, 2, ny, nx), jnp.float32),
        ],
        scratch_shapes=[
            pltpu.VMEM((ny, nx, N, N), jnp.bfloat16),
            pltpu.VMEM((2, ny, N), jnp.float32),
            pltpu.SMEM((2, ny, N), jnp.float32),
            pltpu.SemaphoreType.DMA,
            pltpu.SemaphoreType.DMA((ny,)),
        ],
        compiler_params=pltpu.CompilerParams(vmem_limit_bytes=8 * MIB),
        cost_estimate=pl.CostEstimate(flops=20_000_000, bytes_accessed=12 * MIB, transcendentals=0),
        name="warp",
    )(tile, *flows, in_vmem(blended), in_vmem(edges))


def from_behind(x, axis, by):
    length = lax.axis_size(axis)
    pairs = [(i, i + by) for i in range(length) if 0 <= i + by < length]
    return lax.ppermute(x, axis, pairs)


def swapped(x):
    return lax.ppermute(x, "tile", [(i, i ^ 1) for i in range(lax.axis_size("tile"))])


def hops(tiles, sections, far):
    pairs = ([], [])
    for section in range(sections):
        x_low, rest = divmod(section, sections // 2)
        way = 1 if rest < sections // 4 else -1
        for tile in range(tiles):
            z, x_high = divmod(tile, 2)
            if far and not 0 <= z + 2 * x_high - 1 < tiles // 2:
                continue
            ends = [section * tiles + tile]
            for hop in (1, 2):
                x = (2 * x_high + x_low + hop * way) % 4
                to_z = z + 2 * x_high - 1 if far and hop == 2 else z
                ends.append((x % 2 * (sections // 2) + rest) * tiles + 2 * to_z + x // 2)
            pairs[0].append((ends[0], ends[1]))
            pairs[1].append((ends[1], ends[2]))
    return pairs


def beyond(x):
    tiles = lax.axis_size("tile")
    pairs = [(i, i + 1) for i in range(1, tiles - 1, 2)]
    return lax.ppermute(x, "tile", pairs + [(j, i) for i, j in pairs])


def per_device(sections, node_mask, box_row, box_shift, box_count, blend_weight):
    ny, nx = sections.shape[1:3]
    rows, cols, back_cols, back_rows = tables()
    half = ny // 2
    tiles, count = lax.axis_size("tile"), lax.axis_size("sec")
    tile = jnp.stack([lax.axis_index("tile"), tiles]).astype(jnp.int32)
    on_hops, off_hops = hops(tiles, count, False), hops(tiles, count, True)
    hop = lambda x, pairs: lax.ppermute(x, ("sec", "tile"), pairs)

    spectra_high, source, off = forward(tile, sections, half, half, False, None, rows, cols)
    from_last = from_behind(spectra_high, "sec", 1)
    off = hop(off, off_hops[0])
    spectra_low, source, first, second = forward(tile, sections, 0, half, True, source, rows, cols)
    from_next = from_behind(spectra_low, "sec", -1)
    first = hop(first, on_hops[0])
    target, share = slots_of(tile, box_row, box_shift, box_count, blend_weight)
    off, source = lax.optimization_barrier((off, source))
    off = hop(off, off_hops[1])
    blended = blend(target, share, source)
    first, blended = lax.optimization_barrier((first, blended))
    first = hop(first, on_hops[1])
    from_last, blended = lax.optimization_barrier((from_last, blended))

    flow_high = flow_of(spectra_high, from_last, -1, half, nx, cols, back_cols, back_rows)
    second, flow_high = lax.optimization_barrier((second, flow_high))
    flow_high = from_behind(flow_high, "sec", -1)
    second = swapped(second)
    from_next, flow_high, off = lax.optimization_barrier((from_next, flow_high, off))
    flow_low = flow_of(spectra_low, from_next, 1, half, nx, cols, back_cols, back_rows)
    flow = jnp.concatenate([flow_low, flow_high], axis=1)
    flow = jnp.concatenate([flow, node_mask.astype(jnp.float32) + 1.0], axis=0)
    flow_off = beyond(flow)
    flow_on = swapped(flow)
    flows = (flow_low, flow_high, node_mask, flow_on, flow_off)
    edges = edges_of(tile, target, share, first, second, off, blended)
    return tuple(warp(tile, flows, blended, edges))


def solution(mesh):
    return jax.shard_map(
        per_device,
        mesh=mesh,
        in_specs=(
            P("sec", None, "tile", None, None),
            P("sec", None, "tile"),
            P("sec", None, "tile", None),
            P("sec", None, "tile", None),
            P("sec", None, "tile"),
            P("sec", None, "tile", None),
        ),
        out_specs=(P("sec", None, "tile", None, None), P("sec", None, None, "tile")),
        check_vma=False,
    )
```

```python
import functools

import jax
import jax.numpy as jnp
import numpy as np
from jax import lax
from jax.experimental import pallas as pl
from jax.experimental.pallas import tpu as pltpu
from jax.sharding import PartitionSpec as P

K = 4
HB = 2
STEPS = 3
N = 128
HALF = N // 2
PAD = 72
ROW = 32
DEPTH = 2
SPRING = 0.2
EPS = 1e-06
MIB = 1024 * 1024


def split(x):
    high = x.astype(jnp.bfloat16)
    return high, (x - high.astype(jnp.float32)).astype(jnp.bfloat16)


def tables():
    grid = np.arange(N)[:, None] * np.arange(N)[None, :] % N
    cosine = np.cos(2.0 * np.pi * grid / N)
    sine = np.sin(2.0 * np.pi * grid / N)
    rows = np.concatenate([cosine[:HALF], sine[:HALF]])
    rows[HALF] = cosine[HALF]
    cols = np.block([[cosine, -sine], [-sine, -cosine]])
    back_cols = np.block([[cosine, sine], [-sine, cosine]]) / N
    weight = np.where(np.arange(HALF) == 0, 1.0, 2.0)
    back_rows = np.concatenate([cosine[:, :HALF] * weight, -2.0 * sine[:, :HALF]], axis=1) / N
    back_rows[:, HALF] = cosine[:, HALF] / N
    return [jnp.asarray(t, jnp.float32) for t in (rows, cols, back_cols, back_rows)]


def first_row(shape):
    return lax.broadcasted_iota(jnp.int32, shape, len(shape) - 2) == 0


def dot(a, b):
    return jnp.dot(a, b, preferred_element_type=jnp.float32)


def ahead(fetch, rows, depth):
    y = pl.program_id(0)

    @pl.when(y == 0)
    def _():
        for row in range(depth):
            for copy in fetch(row):
                copy.start()

    @pl.when(y + depth < rows)
    def _():
        for copy in fetch(y + depth):
            copy.start()

    for copy in fetch(y):
        copy.wait()


def in_hbm(x):
    return pltpu.with_memory_space_constraint(x, pltpu.HBM)


def in_vmem(x):
    return pltpu.with_memory_space_constraint(x, pltpu.VMEM)


def wait_all(copies):
    @pl.when(pl.program_id(0) == pl.num_programs(0) - 1)
    def _():
        for copy in copies:
            copy.wait()


def forward_kernel(start, toward_pair, tile_ref, x_hbm, rows_hbm, cols_hbm, *refs):
    *refs, x_ref, rest_ref, lines_ref, ends_ref, rows_ref, cols_ref, in_sems, more_sems = refs
    spec_ref, src_ref, *strip_refs = refs[-2 - (HB if toward_pair else 1) :]
    y = pl.program_id(0)
    count, patches = x_ref.shape[:2]
    ny = src_ref.shape[0]
    odd = tile_ref[0] % 2
    column = ((1 - odd) if toward_pair else odd) * (patches - HB)
    rest = (start + count) % ny
    fetch = lambda row: [pltpu.make_async_copy(x_hbm.at[0, start + row], x_ref.at[row], in_sems.at[row])]
    to_strip = lambda i: strip_refs[i].at[:, 0] if toward_pair else strip_refs[0].at[:, i]
    more = [
        pltpu.make_async_copy(rows_hbm, rows_ref, more_sems.at[0]),
        pltpu.make_async_copy(cols_hbm, cols_ref, more_sems.at[1]),
        pltpu.make_async_copy(
            x_hbm.at[0, pl.ds(rest, ny - count), pl.ds(column, HB)], rest_ref, more_sems.at[2]
        ),
    ]

    @pl.when(y == 0)
    def _():
        for copy in more[:2]:
            copy.start()

    ahead(fetch, count, min(DEPTH, count))

    @pl.when(y == 0)
    def _():
        for copy in more[:2]:
            copy.wait()
        more[2].start()

    @pl.when(y == count - 1)
    def _():
        more[2].wait()
        for i in range(HB):
            to_strip(i)[rest : rest + ny - count] = rest_ref[:, i].astype(jnp.bfloat16)

    for i in range(HB):
        to_strip(i)[start + y] = x_ref[y, column + i].astype(jnp.bfloat16)
    rows2 = rows_ref[...]
    cols = cols_ref[...]
    for pair in range(patches // 2):
        x = jnp.concatenate([x_ref[y, 2 * pair], x_ref[y, 2 * pair + 1]], axis=1)
        high, low = split(x)
        src_ref[start + y, 2 * pair] = high[:, :N]
        src_ref[start + y, 2 * pair + 1] = high[:, N:]
        both = dot(rows2, jnp.concatenate([high, low], axis=0))
        for side in range(2):
            here = both[:, side * N : (side + 1) * N]
            p = 2 * pair + side
            ends_ref[p : p + 1, :N] = here[:1]
            ends_ref[p : p + 1, N:] = here[HALF : HALF + 1]
            lines_ref[p * HALF : (p + 1) * HALF, :N] = here[:HALF].astype(jnp.bfloat16)
            lines_ref[p * HALF : (p + 1) * HALF, N:] = here[HALF:].astype(jnp.bfloat16)
    step = 4
    for first in range(0, patches, step):
        lines = lines_ref[first * HALF : (first + step) * HALF, :]
        freq = dot(lines, cols).reshape(step, HALF, 2 * N)
        spec_ref[pl.ds(y * patches + first, step)] = freq.astype(jnp.bfloat16)
    ends = ends_ref[...].astype(jnp.bfloat16)
    spec_ref[count * patches, pl.ds(pl.multiple_of(y * patches, patches), patches), :] = ends


def forward(tile, sections, start, count, toward_pair, source, rows, cols):
    _, ny, nx, _, _ = sections.shape
    rows2 = jnp.concatenate([rows, rows], axis=1).astype(jnp.bfloat16)
    spectra = (count * nx + 1, HALF, 2 * N)
    before = () if source is None else (in_vmem(source),)
    strips = (1,) * HB if toward_pair else (HB,)
    return pl.pallas_call(
        functools.partial(forward_kernel, start, toward_pair),
        grid=(count,),
        in_specs=[pl.BlockSpec(memory_space=pltpu.SMEM)]
        + [pl.BlockSpec(memory_space=pltpu.HBM)] * 3
        + [pl.BlockSpec(memory_space=pltpu.VMEM)] * len(before),
        out_specs=[pl.BlockSpec(memory_space=pltpu.VMEM)] * (2 + len(strips)),
        out_shape=[
            pltpu.VMEM(spectra, jnp.bfloat16),
            pltpu.VMEM((ny, nx, N, N), jnp.bfloat16),
            *(pltpu.VMEM((ny, wide, N, N), jnp.bfloat16) for wide in strips),
        ],
        scratch_shapes=[
            pltpu.VMEM((count, nx, N, N), jnp.float32),
            pltpu.VMEM((ny - count, HB, N, N), jnp.float32),
            pltpu.VMEM((nx * HALF, 2 * N), jnp.bfloat16),
            pltpu.VMEM((nx, 2 * N), jnp.float32),
            pltpu.VMEM((N, 2 * N), jnp.bfloat16),
            pltpu.VMEM((2 * N, 2 * N), jnp.bfloat16),
            pltpu.SemaphoreType.DMA((count,)),
            pltpu.SemaphoreType.DMA((3,)),
        ],
        input_output_aliases={4: 1} if before else {},
        compiler_params=pltpu.CompilerParams(vmem_limit_bytes=12 * MIB),
        cost_estimate=pl.CostEstimate(flops=2_000_000_000, bytes_accessed=6 * MIB, transcendentals=0),
        name="forward",
    )(tile, in_hbm(sections), in_hbm(rows2), in_hbm(cols.astype(jnp.bfloat16)), *before)


def times_conj(a, b, sign):
    ar, ai, br, bi = a[:, :N], a[:, N:], b[:, :N], b[:, N:]
    real = ar * br + ai * bi
    imag = ai * br - ar * bi if sign > 0 else ar * bi - ai * br
    return jnp.concatenate([real, imag], axis=1).astype(jnp.bfloat16)


def flow_kernel(sign, own, other, cols_ref, back_cols_ref, back_rows_ref, flow_ref, sides, sums, moments):
    y = pl.program_id(0)
    ny, patches = sums.shape[:2]
    last = ny * patches
    cols = cols_ref[...]
    back_cols = back_cols_ref[...]
    back_rows = back_rows_ref[...]

    @pl.when(y == 0)
    def _():
        lines = jnp.concatenate([own[last], other[last]], axis=0)
        edge = dot(jnp.concatenate([lines[:, :N], lines[:, N:]], axis=0), cols[:N])
        quarter = edge.reshape(4, last, 2 * N)
        low = times_conj(quarter[0], quarter[1], sign)
        high = times_conj(quarter[2], quarter[3], sign)
        back = dot(jnp.concatenate([low, high], axis=0), back_cols[:, :N])
        sides[...] = back.reshape(sides.shape)

    shift_rows = lax.broadcasted_iota(jnp.int32, (N, N), 0)
    offset_rows = (((shift_rows + HALF) % N) - HALF).astype(jnp.float32)
    offset_rows = jnp.concatenate([offset_rows, offset_rows], axis=1)
    step = 4
    for first in range(0, patches, step):
        here = pl.ds(y * patches + first, step)
        a = own[here].reshape(step * HALF, 2 * N).astype(jnp.float32)
        b = other[here].reshape(step * HALF, 2 * N).astype(jnp.float32)
        back = dot(times_conj(a, b, sign), back_cols)
        halves = []
        for i in range(step):
            p = first + i
            parts = []
            for side in range(2):
                part = back[i * HALF : (i + 1) * HALF, side * N : (side + 1) * N]
                top = jnp.where(first_row((16, N)), sides[side, y, p : p + 1, :], part[:16])
                parts += [top.astype(jnp.bfloat16), part[16:].astype(jnp.bfloat16)]
            halves.append(jnp.concatenate(parts, axis=0))
        for i in range(0, step, 2):
            corr = dot(back_rows, jnp.concatenate(halves[i : i + 2], axis=1))
            power = corr * corr
            total = power.sum(0, keepdims=True)
            moment = (power * offset_rows).sum(0, keepdims=True)
            for side in range(2):
                p = first + i + side
                sums[y, p : p + 1, :] = total[:, side * N : (side + 1) * N]
                moments[y, p : p + 1, :] = moment[:, side * N : (side + 1) * N]

    @pl.when(y == ny - 1)
    def _():
        lane = lax.broadcasted_iota(jnp.int32, (8, N), 1)
        row = lax.broadcasted_iota(jnp.int32, (8, N), 0)
        offset_cols = (((lane + HALF) % N) - HALF).astype(jnp.float32)
        reduce_by = jnp.where(row == 0, 1.0, jnp.where(row == 1, offset_cols, 0.0))
        over_lanes = lambda m: lax.dot_general(
            reduce_by, m.reshape(last, N), (((1,), (1,)), ((), ())),
            precision=lax.Precision.HIGHEST, preferred_element_type=jnp.float32,
        )
        by_sums = over_lanes(sums[...])
        by_moments = over_lanes(moments[...])
        total = by_sums[0:1] + EPS
        along_rows = by_moments[0:1] / total
        along_cols = by_sums[1:2] / total
        for row in range(ny):
            flow_ref[0, row : row + 1, :] = along_rows[:, row * patches : (row + 1) * patches]
            flow_ref[1, row : row + 1, :] = along_cols[:, row * patches : (row + 1) * patches]


def flow_of(own, other, sign, ny, nx, cols, back_cols, back_rows):
    whole = lambda shape: pl.BlockSpec(shape, lambda y: (0,) * len(shape))
    return pl.pallas_call(
        functools.partial(flow_kernel, sign),
        grid=(ny,),
        in_specs=[
            pl.BlockSpec(memory_space=pltpu.VMEM),
            pl.BlockSpec(memory_space=pltpu.VMEM),
            whole((2 * N, 2 * N)),
            whole((2 * N, 2 * N)),
            whole((N, N)),
        ],
        out_specs=whole((2, ny, nx)),
        out_shape=jax.ShapeDtypeStruct((2, ny, nx), jnp.float32),
        scratch_shapes=[
            pltpu.VMEM((2, ny, nx, N), jnp.float32),
            pltpu.VMEM((ny, nx, N), jnp.float32),
            pltpu.VMEM((ny, nx, N), jnp.float32),
        ],
        compiler_params=pltpu.CompilerParams(vmem_limit_bytes=8 * MIB),
        cost_estimate=pl.CostEstimate(flops=0 if sign < 0 else 0, bytes_accessed=0, transcendentals=0),
        name="flow",
    )(in_vmem(own), in_vmem(other), *(t.astype(jnp.bfloat16) for t in (cols, back_cols, back_rows)))


def slots_kernel(tile_ref, rows_ref, shifts_ref, count_ref, weight_ref, target_ref, share_ref):
    ny, _, nx = rows_ref.shape[1:]
    tile, tiles = tile_ref[0], tile_ref[1]
    live = [k < count_ref[0] for k in range(K)]
    weights = [jnp.where(live[k], weight_ref[0, :, k, :], 0.0) for k in range(K)]
    total = weights[0] + weights[1] + weights[2] + weights[3]
    share = [(w / total).astype(jnp.bfloat16).astype(jnp.float32) for w in weights]
    columns = [lax.broadcasted_iota(jnp.int32, (ny, nx), 1) + shifts_ref[0, :, k, :] for k in range(K)]
    rows = [rows_ref[0, :, k, :] * ROW for k in range(K)]
    low = [c < 0 for c in columns]
    high = [c >= nx for c in columns]
    first, last = tile == 0, tile == tiles - 1
    inside = [jnp.where(l | h, 0.0, s) for l, h, s in zip(low, high, share, strict=True)]
    share_low = [jnp.where(first, 0.0, jnp.where(l, s, 0.0)) for l, s in zip(low, share, strict=True)]
    share_high = [jnp.where(last, 0.0, jnp.where(h, s, 0.0)) for h, s in zip(high, share, strict=True)]
    beyond = [l + h for l, h in zip(share_low, share_high, strict=True)]
    share_ref[...] = jnp.concatenate(inside + beyond, axis=1)
    target = [r + jnp.where(l | h, 0, c) for r, c, l, h in zip(rows, columns, low, high, strict=True)]
    away = [
        r + jnp.where(l, c + HB, jnp.where(h, c - nx + HB, 0))
        for r, c, l, h in zip(rows, columns, low, high, strict=True)
    ]
    target_ref[...] = jnp.concatenate(target + away, axis=1)


def slots_of(tile, box_row, box_shift, box_count, blend_weight):
    ny = box_row.shape[1]
    slots_first = lambda x: jnp.transpose(x, (0, 1, 3, 2))
    return pl.pallas_call(
        slots_kernel,
        in_specs=[pl.BlockSpec(memory_space=pltpu.SMEM)] + [pl.BlockSpec(memory_space=pltpu.VMEM)] * 4,
        out_shape=[
            jax.ShapeDtypeStruct((ny, N), jnp.int32),
            jax.ShapeDtypeStruct((ny, N), jnp.float32),
        ],
        compiler_params=pltpu.CompilerParams(vmem_limit_bytes=4 * MIB),
        cost_estimate=pl.CostEstimate(flops=0, bytes_accessed=0, transcendentals=0),
        name="slots",
    )(tile, slots_first(box_row), slots_first(box_shift), box_count, slots_first(blend_weight))


def blend_cell(y, first, nx, target_ref, share_ref, window):
    total = None
    for k in range(K):
        spot = target_ref[y, first + k * nx]
        piece = window[spot // ROW, spot % ROW].astype(jnp.float32) * share_ref[y, first + k * nx]
        total = piece if total is None else total + piece
    return total


def blend_kernel(target_ref, share_ref, source, out_ref):
    y = pl.program_id(0)
    nx = source.shape[1]
    border = jnp.zeros((nx, PAD, N), jnp.float32)
    out_ref[y, :, :PAD] = border
    out_ref[y, :, PAD + N :] = border
    for x in range(nx):
        out_ref[y, x, PAD : PAD + N] = blend_cell(y, x, nx, target_ref, share_ref, source)


def blend(target, share, source):
    ny, nx = source.shape[:2]
    return pl.pallas_call(
        blend_kernel,
        grid=(ny,),
        in_specs=[pl.BlockSpec(memory_space=pltpu.SMEM)] * 2 + [pl.BlockSpec(memory_space=pltpu.VMEM)],
        out_specs=pl.BlockSpec(memory_space=pltpu.VMEM),
        out_shape=pltpu.VMEM((ny, nx, N + 2 * PAD, N), jnp.float32),
        compiler_params=pltpu.CompilerParams(vmem_limit_bytes=4 * MIB),
        cost_estimate=pl.CostEstimate(flops=16_000_000_000, bytes_accessed=4 * MIB, transcendentals=0),
        name="blend",
    )(target, share, in_vmem(source))


def relax(tile_ref, low_ref, high_ref, mask_ref, on_ref, off_ref):
    ny, nx = mask_ref.shape[1:]
    even = tile_ref[0] % 2 == 0
    left_ref = [jnp.where(even, off_ref[i], on_ref[i]) for i in range(3)]
    right_ref = [jnp.where(even, on_ref[i], off_ref[i]) for i in range(3)]
    rest = jnp.zeros((ny, N - nx - 2 * STEPS), jnp.float32)

    def across(left, own, right):
        return jnp.concatenate([left[:, nx - STEPS :], own, right[:, :STEPS], rest], axis=1)

    known = across(left_ref[2], mask_ref[0].astype(jnp.float32) + 1.0, right_ref[2])
    valid = jnp.where(known > 0.5, 1.0, 0.0)
    trust = jnp.where(known > 1.5, 1.0, 0.0)
    row = lax.broadcasted_iota(jnp.int32, trust.shape, 0)
    fields = []
    for component in range(2):
        own = jnp.concatenate([low_ref[component], high_ref[component]], axis=0)
        flow = across(left_ref[component], own, right_ref[component])
        field = trust * flow
        for _ in range(STEPS):
            below = jnp.where(row == 0, 0.0, pltpu.roll(field, 1, 0))
            above = jnp.where(row == ny - 1, 0.0, pltpu.roll(field, ny - 1, 0))
            beside = pltpu.roll(field, 1, 1) + pltpu.roll(field, N - 1, 1)
            lap = above + below + beside - 4.0 * field
            field = (field + SPRING * (lap + trust * (flow - field))) * valid
        fields.append(field)
    return fields


def edge_kernel(tile_ref, target_ref, share_ref, first_ref, second_ref, off_ref, padded, out_ref, window, sems):
    y = pl.program_id(0)
    ny, nx = padded.shape[:2]
    even = tile_ref[0] % 2 == 0
    halos = {
        side: ((first_ref, on_at), (second_ref, on_at + 1), (off_ref, HB - on_at))
        for side, on_at in ((True, HB), (False, 0))
    }
    copies = {
        side: [
            pltpu.make_async_copy(ref, window.at[:, into : into + ref.shape[1]], sems.at[i])
            for i, (ref, into) in enumerate(places)
        ]
        for side, places in halos.items()
    }

    @pl.when((y == 0) & even)
    def _():
        for copy in copies[True]:
            copy.start()

    @pl.when((y == 0) & jnp.logical_not(even))
    def _():
        for copy in copies[False]:
            copy.start()

    border = jnp.zeros((2 * HB, PAD, N), jnp.float32)
    out_ref[y, :, :PAD] = border
    out_ref[y, :, PAD + N :] = border

    @pl.when(y == 0)
    def _():
        for copy in copies[True]:
            copy.wait()

    for i, x in enumerate((*range(HB), *range(nx - HB, nx))):
        more = blend_cell(y, K * nx + x, nx, target_ref, share_ref, window)
        out_ref[y, i, PAD : PAD + N] = padded[y, x, PAD : PAD + N] + more


def edges_of(tile, target, share, first, second, off, blended):
    ny, _, tall, _ = blended.shape
    vmem = pl.BlockSpec(memory_space=pltpu.VMEM)
    return pl.pallas_call(
        edge_kernel,
        grid=(ny,),
        in_specs=[pl.BlockSpec(memory_space=pltpu.SMEM)] * 3 + [vmem] * 4,
        out_specs=vmem,
        out_shape=pltpu.VMEM((ny, 2 * HB, tall, N), jnp.float32),
        scratch_shapes=[pltpu.VMEM((ny, 2 * HB, N, N), jnp.bfloat16), pltpu.SemaphoreType.DMA((3,))],
        compiler_params=pltpu.CompilerParams(vmem_limit_bytes=4 * MIB),
        cost_estimate=pl.CostEstimate(flops=5_000_000, bytes_accessed=4 * MIB, transcendentals=0),
        name="edges",
    )(tile, target, share, in_vmem(first), in_vmem(second), in_vmem(off), in_vmem(blended))


def warped(cell, down_shift, right_shift):
    whole_of = lambda shift: (shift + 256.0).astype(jnp.int32) - 256
    line = lambda value: jnp.full((1, N), value, jnp.float32).astype(jnp.bfloat16)
    down = jnp.clip(whole_of(down_shift), 4 - PAD, PAD - 6)
    part = down_shift - down.astype(jnp.float32)
    upper = cell[pl.ds(PAD + down, N), :]
    lower = cell[pl.ds(PAD + 1 + down, N), :]
    image = upper + part * (lower - upper)
    right = whole_of(right_shift).astype(jnp.float32)
    apart = lax.broadcasted_iota(jnp.int32, (N, N), 0) - lax.broadcasted_iota(jnp.int32, (N, N), 1)
    apart = apart.astype(jnp.bfloat16) - line(right)
    one = jnp.bfloat16(1.0)
    hat = jnp.maximum(jnp.bfloat16(0.0), one - jnp.abs(apart - line(right_shift - right)))
    return dot(image.astype(jnp.bfloat16), hat).astype(jnp.bfloat16)


def warp_kernel(tile_ref, *refs):
    *flows, padded, edges, out_hbm, field_ref, out, wide, field, sem, out_sems = refs
    y = pl.program_id(0)
    ny, nx = out.shape[:2]

    @pl.when(y == 0)
    def _():
        for component, values in enumerate(relax(tile_ref, *flows)):
            wide[component] = values
            field_ref[0, component] = values[:, STEPS : STEPS + nx]
        scalars = pltpu.make_async_copy(wide, field, sem)
        scalars.start()
        scalars.wait()

    borders = (*range(HB), *range(nx - HB, nx))
    for x in range(nx):
        cell = edges.at[y, borders.index(x)] if x in borders else padded.at[y, x]
        out[y, x] = warped(cell, field[0, y, STEPS + x], field[1, y, STEPS + x])
    store = lambda row: pltpu.make_async_copy(out.at[row], out_hbm.at[0, row], out_sems.at[row])
    store(y).start()
    wait_all([store(row) for row in range(ny)])


def warp(tile, flows, blended, edges):
    ny, nx = blended.shape[:2]
    whole = lambda shape: pl.BlockSpec(shape, lambda y: (0,) * len(shape))
    return pl.pallas_call(
        warp_kernel,
        grid=(ny,),
        in_specs=[pl.BlockSpec(memory_space=pltpu.SMEM)]
        + [whole(x.shape) for x in flows]
        + [pl.BlockSpec(memory_space=pltpu.VMEM)] * 2,
        out_specs=[pl.BlockSpec(memory_space=pl.ANY), whole((1, 2, ny, nx))],
        out_shape=[
            jax.ShapeDtypeStruct((1, ny, nx, N, N), jnp.bfloat16),
            jax.ShapeDtypeStruct((1, 2, ny, nx), jnp.float32),
        ],
        scratch_shapes=[
            pltpu.VMEM((ny, nx, N, N), jnp.bfloat16),
            pltpu.VMEM((2, ny, N), jnp.float32),
            pltpu.SMEM((2, ny, N), jnp.float32),
            pltpu.SemaphoreType.DMA,
            pltpu.SemaphoreType.DMA((ny,)),
        ],
        compiler_params=pltpu.CompilerParams(vmem_limit_bytes=8 * MIB),
        cost_estimate=pl.CostEstimate(flops=20_000_000, bytes_accessed=12 * MIB, transcendentals=0),
        name="warp",
    )(tile, *flows, in_vmem(blended), in_vmem(edges))


def from_behind(x, axis, by):
    length = lax.axis_size(axis)
    pairs = [(i, i + by) for i in range(length) if 0 <= i + by < length]
    return lax.ppermute(x, axis, pairs)


def swapped(x):
    return lax.ppermute(x, "tile", [(i, i ^ 1) for i in range(lax.axis_size("tile"))])


def hops(tiles, sections, far):
    pairs = ([], [])
    for section in range(sections):
        x_low, rest = divmod(section, sections // 2)
        way = 1 if rest < sections // 4 else -1
        for tile in range(tiles):
            z, x_high = divmod(tile, 2)
            to_z = z + 2 * x_high - 1 if far else z
            ends = [section * tiles + tile]
            for hop in (1, 2):
                x = (2 * x_high + x_low + hop * way) % 4
                ends.append((x % 2 * (sections // 2) + rest) * tiles + 2 * (to_z if hop == 2 else z) + x // 2)
            pairs[0].append((ends[0], ends[1]))
            if 0 <= to_z < tiles // 2:
                pairs[1].append((ends[1], ends[2]))
    return pairs


def beyond(x):
    tiles = lax.axis_size("tile")
    pairs = [(i, i + 1) for i in range(1, tiles - 1, 2)]
    return lax.ppermute(x, "tile", pairs + [(j, i) for i, j in pairs])


def per_device(sections, node_mask, box_row, box_shift, box_count, blend_weight):
    ny, nx = sections.shape[1:3]
    rows, cols, back_cols, back_rows = tables()
    half = ny // 2
    tiles, count = lax.axis_size("tile"), lax.axis_size("sec")
    tile = jnp.stack([lax.axis_index("tile"), tiles]).astype(jnp.int32)
    on_hops, off_hops = hops(tiles, count, False), hops(tiles, count, True)
    hop = lambda x, pairs: lax.ppermute(x, ("sec", "tile"), pairs)

    spectra_high, source, off = forward(tile, sections, half, half, False, None, rows, cols)
    from_last = from_behind(spectra_high, "sec", 1)
    off = hop(off, off_hops[0])
    spectra_low, source, first, second = forward(tile, sections, 0, half, True, source, rows, cols)
    from_next = from_behind(spectra_low, "sec", -1)
    first = hop(first, on_hops[0])
    target, share = slots_of(tile, box_row, box_shift, box_count, blend_weight)
    off, source = lax.optimization_barrier((off, source))
    off = hop(off, off_hops[1])
    blended = blend(target, share, source)
    first, blended = lax.optimization_barrier((first, blended))
    first = hop(first, on_hops[1])
    from_last, blended = lax.optimization_barrier((from_last, blended))

    flow_high = flow_of(spectra_high, from_last, -1, half, nx, cols, back_cols, back_rows)
    second, flow_high = lax.optimization_barrier((second, flow_high))
    flow_high = from_behind(flow_high, "sec", -1)
    second = swapped(second)
    from_next, flow_high, off = lax.optimization_barrier((from_next, flow_high, off))
    flow_low = flow_of(spectra_low, from_next, 1, half, nx, cols, back_cols, back_rows)
    flow = jnp.concatenate([flow_low, flow_high], axis=1)
    flow = jnp.concatenate([flow, node_mask.astype(jnp.float32) + 1.0], axis=0)
    flow_off = beyond(flow)
    flow_on = swapped(flow)
    flows = (flow_low, flow_high, node_mask, flow_on, flow_off)
    edges = edges_of(tile, target, share, first, second, off, blended)
    return tuple(warp(tile, flows, blended, edges))


def solution(mesh):
    return jax.shard_map(
        per_device,
        mesh=mesh,
        in_specs=(
            P("sec", None, "tile", None, None),
            P("sec", None, "tile"),
            P("sec", None, "tile", None),
            P("sec", None, "tile", None),
            P("sec", None, "tile"),
            P("sec", None, "tile", None),
        ),
        out_specs=(P("sec", None, "tile", None, None), P("sec", None, None, "tile")),
        check_vma=False,
    )
```

```python
import functools

import jax
import jax.numpy as jnp
import numpy as np
from jax import lax
from jax.experimental import pallas as pl
from jax.experimental.pallas import tpu as pltpu
from jax.sharding import PartitionSpec as P

K = 4
HB = 2
STEPS = 3
N = 128
HALF = N // 2
PAD = 72
ROW = 32
DEPTH = 2
SPRING = 0.2
EPS = 1e-06
MIB = 1024 * 1024


def split(x):
    high = x.astype(jnp.bfloat16)
    return high, (x - high.astype(jnp.float32)).astype(jnp.bfloat16)


def tables():
    grid = np.arange(N)[:, None] * np.arange(N)[None, :] % N
    cosine = np.cos(2.0 * np.pi * grid / N)
    sine = np.sin(2.0 * np.pi * grid / N)
    rows = np.concatenate([cosine[:HALF], sine[:HALF]])
    rows[HALF] = cosine[HALF]
    cols = np.block([[cosine, -sine], [-sine, -cosine]])
    back_cols = np.block([[cosine, sine], [-sine, cosine]]) / N
    weight = np.where(np.arange(HALF) == 0, 1.0, 2.0)
    back_rows = np.concatenate([cosine[:, :HALF] * weight, -2.0 * sine[:, :HALF]], axis=1) / N
    back_rows[:, HALF] = cosine[:, HALF] / N
    return [jnp.asarray(t, jnp.float32) for t in (rows, cols, back_cols, back_rows)]


def first_row(shape):
    return lax.broadcasted_iota(jnp.int32, shape, len(shape) - 2) == 0


def dot(a, b):
    return jnp.dot(a, b, preferred_element_type=jnp.float32)


def ahead(fetch, rows, depth):
    y = pl.program_id(0)

    @pl.when(y == 0)
    def _():
        for row in range(depth):
            for copy in fetch(row):
                copy.start()

    @pl.when(y + depth < rows)
    def _():
        for copy in fetch(y + depth):
            copy.start()

    for copy in fetch(y):
        copy.wait()


def in_hbm(x):
    return pltpu.with_memory_space_constraint(x, pltpu.HBM)


def in_vmem(x):
    return pltpu.with_memory_space_constraint(x, pltpu.VMEM)


def wait_all(copies):
    @pl.when(pl.program_id(0) == pl.num_programs(0) - 1)
    def _():
        for copy in copies:
            copy.wait()


def forward_kernel(start, toward_pair, tile_ref, x_hbm, rows_hbm, cols_hbm, *refs):
    *refs, x_ref, rest_ref, lines_ref, ends_ref, rows_ref, cols_ref, in_sems, more_sems = refs
    spec_ref, src_ref, *strip_refs = refs[-2 - (HB if toward_pair else 1) :]
    y = pl.program_id(0)
    count, patches = x_ref.shape[:2]
    ny = src_ref.shape[0]
    odd = tile_ref[0] % 2
    column = ((1 - odd) if toward_pair else odd) * (patches - HB)
    rest = (start + count) % ny
    fetch = lambda row: [pltpu.make_async_copy(x_hbm.at[0, start + row], x_ref.at[row], in_sems.at[row])]
    to_strip = lambda i: strip_refs[i].at[:, 0] if toward_pair else strip_refs[0].at[:, i]
    more = [
        pltpu.make_async_copy(rows_hbm, rows_ref, more_sems.at[0]),
        pltpu.make_async_copy(cols_hbm, cols_ref, more_sems.at[1]),
        pltpu.make_async_copy(
            x_hbm.at[0, pl.ds(rest, ny - count), pl.ds(column, HB)], rest_ref, more_sems.at[2]
        ),
    ]

    @pl.when(y == 0)
    def _():
        for copy in more[:2]:
            copy.start()

    ahead(fetch, count, min(DEPTH, count))

    @pl.when(y == 0)
    def _():
        for copy in more[:2]:
            copy.wait()
        more[2].start()

    @pl.when(y == count - 1)
    def _():
        more[2].wait()
        for i in range(HB):
            to_strip(i)[rest : rest + ny - count] = rest_ref[:, i].astype(jnp.bfloat16)

    for i in range(HB):
        to_strip(i)[start + y] = x_ref[y, column + i].astype(jnp.bfloat16)
    rows2 = rows_ref[...]
    cols = cols_ref[...]
    for pair in range(patches // 2):
        x = jnp.concatenate([x_ref[y, 2 * pair], x_ref[y, 2 * pair + 1]], axis=1)
        high, low = split(x)
        src_ref[start + y, 2 * pair] = high[:, :N]
        src_ref[start + y, 2 * pair + 1] = high[:, N:]
        both = dot(rows2, jnp.concatenate([high, low], axis=0))
        for side in range(2):
            here = both[:, side * N : (side + 1) * N]
            p = 2 * pair + side
            ends_ref[p : p + 1, :N] = here[:1]
            ends_ref[p : p + 1, N:] = here[HALF : HALF + 1]
            lines_ref[p * HALF : (p + 1) * HALF, :N] = here[:HALF].astype(jnp.bfloat16)
            lines_ref[p * HALF : (p + 1) * HALF, N:] = here[HALF:].astype(jnp.bfloat16)
    step = 4
    for first in range(0, patches, step):
        lines = lines_ref[first * HALF : (first + step) * HALF, :]
        freq = dot(lines, cols).reshape(step, HALF, 2 * N)
        spec_ref[pl.ds(y * patches + first, step)] = freq.astype(jnp.bfloat16)
    ends = ends_ref[...].astype(jnp.bfloat16)
    spec_ref[count * patches, pl.ds(pl.multiple_of(y * patches, patches), patches), :] = ends


def forward(tile, sections, start, count, toward_pair, source, rows, cols):
    _, ny, nx, _, _ = sections.shape
    rows2 = jnp.concatenate([rows, rows], axis=1).astype(jnp.bfloat16)
    spectra = (count * nx + 1, HALF, 2 * N)
    before = () if source is None else (in_vmem(source),)
    strips = (1,) * HB if toward_pair else (HB,)
    return pl.pallas_call(
        functools.partial(forward_kernel, start, toward_pair),
        grid=(count,),
        in_specs=[pl.BlockSpec(memory_space=pltpu.SMEM)]
        + [pl.BlockSpec(memory_space=pltpu.HBM)] * 3
        + [pl.BlockSpec(memory_space=pltpu.VMEM)] * len(before),
        out_specs=[pl.BlockSpec(memory_space=pltpu.VMEM)] * (2 + len(strips)),
        out_shape=[
            pltpu.VMEM(spectra, jnp.bfloat16),
            pltpu.VMEM((ny, nx, N, N), jnp.bfloat16),
            *(pltpu.VMEM((ny, wide, N, N), jnp.bfloat16) for wide in strips),
        ],
        scratch_shapes=[
            pltpu.VMEM((count, nx, N, N), jnp.float32),
            pltpu.VMEM((ny - count, HB, N, N), jnp.float32),
            pltpu.VMEM((nx * HALF, 2 * N), jnp.bfloat16),
            pltpu.VMEM((nx, 2 * N), jnp.float32),
            pltpu.VMEM((N, 2 * N), jnp.bfloat16),
            pltpu.VMEM((2 * N, 2 * N), jnp.bfloat16),
            pltpu.SemaphoreType.DMA((count,)),
            pltpu.SemaphoreType.DMA((3,)),
        ],
        input_output_aliases={4: 1} if before else {},
        compiler_params=pltpu.CompilerParams(vmem_limit_bytes=12 * MIB),
        cost_estimate=pl.CostEstimate(flops=2_000_000_000, bytes_accessed=6 * MIB, transcendentals=0),
        name="forward",
    )(tile, in_hbm(sections), in_hbm(rows2), in_hbm(cols.astype(jnp.bfloat16)), *before)


def times_conj(a, b, sign):
    ar, ai, br, bi = a[:, :N], a[:, N:], b[:, :N], b[:, N:]
    real = ar * br + ai * bi
    imag = ai * br - ar * bi if sign > 0 else ar * bi - ai * br
    return jnp.concatenate([real, imag], axis=1).astype(jnp.bfloat16)


def flow_kernel(sign, own, other, cols_ref, back_cols_ref, back_rows_ref, flow_ref, sides, sums, moments):
    y = pl.program_id(0)
    ny, patches = sums.shape[:2]
    last = ny * patches
    cols = cols_ref[...]
    back_cols = back_cols_ref[...]
    back_rows = back_rows_ref[...]

    @pl.when(y == 0)
    def _():
        lines = jnp.concatenate([own[last], other[last]], axis=0)
        edge = dot(jnp.concatenate([lines[:, :N], lines[:, N:]], axis=0), cols[:N])
        quarter = edge.reshape(4, last, 2 * N)
        low = times_conj(quarter[0], quarter[1], sign)
        high = times_conj(quarter[2], quarter[3], sign)
        back = dot(jnp.concatenate([low, high], axis=0), back_cols[:, :N])
        sides[...] = back.reshape(sides.shape)

    shift_rows = lax.broadcasted_iota(jnp.int32, (N, N), 0)
    offset_rows = (((shift_rows + HALF) % N) - HALF).astype(jnp.float32)
    offset_rows = jnp.concatenate([offset_rows, offset_rows], axis=1)
    step = 4
    for first in range(0, patches, step):
        here = pl.ds(y * patches + first, step)
        a = own[here].reshape(step * HALF, 2 * N).astype(jnp.float32)
        b = other[here].reshape(step * HALF, 2 * N).astype(jnp.float32)
        back = dot(times_conj(a, b, sign), back_cols)
        halves = []
        for i in range(step):
            p = first + i
            parts = []
            for side in range(2):
                part = back[i * HALF : (i + 1) * HALF, side * N : (side + 1) * N]
                top = jnp.where(first_row((16, N)), sides[side, y, p : p + 1, :], part[:16])
                parts += [top.astype(jnp.bfloat16), part[16:].astype(jnp.bfloat16)]
            halves.append(jnp.concatenate(parts, axis=0))
        for i in range(0, step, 2):
            corr = dot(back_rows, jnp.concatenate(halves[i : i + 2], axis=1))
            power = corr * corr
            total = power.sum(0, keepdims=True)
            moment = (power * offset_rows).sum(0, keepdims=True)
            for side in range(2):
                p = first + i + side
                sums[y, p : p + 1, :] = total[:, side * N : (side + 1) * N]
                moments[y, p : p + 1, :] = moment[:, side * N : (side + 1) * N]

    @pl.when(y == ny - 1)
    def _():
        lane = lax.broadcasted_iota(jnp.int32, (8, N), 1)
        row = lax.broadcasted_iota(jnp.int32, (8, N), 0)
        offset_cols = (((lane + HALF) % N) - HALF).astype(jnp.float32)
        reduce_by = jnp.where(row == 0, 1.0, jnp.where(row == 1, offset_cols, 0.0))
        over_lanes = lambda m: lax.dot_general(
            reduce_by, m.reshape(last, N), (((1,), (1,)), ((), ())),
            precision=lax.Precision.HIGHEST, preferred_element_type=jnp.float32,
        )
        by_sums = over_lanes(sums[...])
        by_moments = over_lanes(moments[...])
        total = by_sums[0:1] + EPS
        along_rows = by_moments[0:1] / total
        along_cols = by_sums[1:2] / total
        for row in range(ny):
            flow_ref[0, row : row + 1, :] = along_rows[:, row * patches : (row + 1) * patches]
            flow_ref[1, row : row + 1, :] = along_cols[:, row * patches : (row + 1) * patches]


def flow_of(own, other, sign, ny, nx, cols, back_cols, back_rows):
    whole = lambda shape: pl.BlockSpec(shape, lambda y: (0,) * len(shape))
    return pl.pallas_call(
        functools.partial(flow_kernel, sign),
        grid=(ny,),
        in_specs=[
            pl.BlockSpec(memory_space=pltpu.VMEM),
            pl.BlockSpec(memory_space=pltpu.VMEM),
            whole((2 * N, 2 * N)),
            whole((2 * N, 2 * N)),
            whole((N, N)),
        ],
        out_specs=whole((2, ny, nx)),
        out_shape=jax.ShapeDtypeStruct((2, ny, nx), jnp.float32),
        scratch_shapes=[
            pltpu.VMEM((2, ny, nx, N), jnp.float32),
            pltpu.VMEM((ny, nx, N), jnp.float32),
            pltpu.VMEM((ny, nx, N), jnp.float32),
        ],
        compiler_params=pltpu.CompilerParams(vmem_limit_bytes=8 * MIB),
        cost_estimate=pl.CostEstimate(flops=0 if sign < 0 else 0, bytes_accessed=0, transcendentals=0),
        name="flow",
    )(in_vmem(own), in_vmem(other), *(t.astype(jnp.bfloat16) for t in (cols, back_cols, back_rows)))


def slots_kernel(tile_ref, rows_ref, shifts_ref, count_ref, weight_ref, target_ref, share_ref):
    ny, _, nx = rows_ref.shape[1:]
    tile, tiles = tile_ref[0], tile_ref[1]
    live = [k < count_ref[0] for k in range(K)]
    weights = [jnp.where(live[k], weight_ref[0, :, k, :], 0.0) for k in range(K)]
    total = weights[0] + weights[1] + weights[2] + weights[3]
    share = [(w / total).astype(jnp.bfloat16).astype(jnp.float32) for w in weights]
    columns = [lax.broadcasted_iota(jnp.int32, (ny, nx), 1) + shifts_ref[0, :, k, :] for k in range(K)]
    rows = [rows_ref[0, :, k, :] * ROW for k in range(K)]
    low = [c < 0 for c in columns]
    high = [c >= nx for c in columns]
    first, last = tile == 0, tile == tiles - 1
    inside = [jnp.where(l | h, 0.0, s) for l, h, s in zip(low, high, share, strict=True)]
    share_low = [jnp.where(first, 0.0, jnp.where(l, s, 0.0)) for l, s in zip(low, share, strict=True)]
    share_high = [jnp.where(last, 0.0, jnp.where(h, s, 0.0)) for h, s in zip(high, share, strict=True)]
    beyond = [l + h for l, h in zip(share_low, share_high, strict=True)]
    share_ref[...] = jnp.concatenate(inside + beyond, axis=1)
    target = [r + jnp.where(l | h, 0, c) for r, c, l, h in zip(rows, columns, low, high, strict=True)]
    away = [
        r + jnp.where(l, c + HB, jnp.where(h, c - nx + HB, 0))
        for r, c, l, h in zip(rows, columns, low, high, strict=True)
    ]
    target_ref[...] = jnp.concatenate(target + away, axis=1)


def slots_of(tile, box_row, box_shift, box_count, blend_weight):
    ny = box_row.shape[1]
    slots_first = lambda x: jnp.transpose(x, (0, 1, 3, 2))
    return pl.pallas_call(
        slots_kernel,
        in_specs=[pl.BlockSpec(memory_space=pltpu.SMEM)] + [pl.BlockSpec(memory_space=pltpu.VMEM)] * 4,
        out_shape=[
            jax.ShapeDtypeStruct((ny, N), jnp.int32),
            jax.ShapeDtypeStruct((ny, N), jnp.float32),
        ],
        compiler_params=pltpu.CompilerParams(vmem_limit_bytes=4 * MIB),
        cost_estimate=pl.CostEstimate(flops=0, bytes_accessed=0, transcendentals=0),
        name="slots",
    )(tile, slots_first(box_row), slots_first(box_shift), box_count, slots_first(blend_weight))


def blend_cell(y, first, nx, target_ref, share_ref, window):
    total = None
    for k in range(K):
        spot = target_ref[y, first + k * nx]
        piece = window[spot // ROW, spot % ROW].astype(jnp.float32) * share_ref[y, first + k * nx]
        total = piece if total is None else total + piece
    return total


def blend_kernel(target_ref, share_ref, source, out_ref):
    y = pl.program_id(0)
    nx = source.shape[1]
    border = jnp.zeros((nx, PAD, N), jnp.float32)
    out_ref[y, :, :PAD] = border
    out_ref[y, :, PAD + N :] = border
    for x in range(nx):
        out_ref[y, x, PAD : PAD + N] = blend_cell(y, x, nx, target_ref, share_ref, source)


def blend(target, share, source):
    ny, nx = source.shape[:2]
    return pl.pallas_call(
        blend_kernel,
        grid=(ny,),
        in_specs=[pl.BlockSpec(memory_space=pltpu.SMEM)] * 2 + [pl.BlockSpec(memory_space=pltpu.VMEM)],
        out_specs=pl.BlockSpec(memory_space=pltpu.VMEM),
        out_shape=pltpu.VMEM((ny, nx, N + 2 * PAD, N), jnp.float32),
        compiler_params=pltpu.CompilerParams(vmem_limit_bytes=4 * MIB),
        cost_estimate=pl.CostEstimate(flops=16_000_000_000, bytes_accessed=4 * MIB, transcendentals=0),
        name="blend",
    )(target, share, in_vmem(source))


def relax(tile_ref, low_ref, high_ref, mask_ref, on_ref, off_ref):
    ny, nx = mask_ref.shape[1:]
    even = tile_ref[0] % 2 == 0
    inner = jnp.where((tile_ref[0] == 0) | (tile_ref[0] == tile_ref[1] - 1), 0.0, 1.0)
    left_ref = [jnp.where(even, off_ref[i] * inner, on_ref[i]) for i in range(3)]
    right_ref = [jnp.where(even, on_ref[i], off_ref[i] * inner) for i in range(3)]
    rest = jnp.zeros((ny, N - nx - 2 * STEPS), jnp.float32)

    def across(left, own, right):
        return jnp.concatenate([left[:, nx - STEPS :], own, right[:, :STEPS], rest], axis=1)

    known = across(left_ref[2], mask_ref[0].astype(jnp.float32) + 1.0, right_ref[2])
    valid = jnp.where(known > 0.5, 1.0, 0.0)
    trust = jnp.where(known > 1.5, 1.0, 0.0)
    row = lax.broadcasted_iota(jnp.int32, trust.shape, 0)
    fields = []
    for component in range(2):
        own = jnp.concatenate([low_ref[component], high_ref[component]], axis=0)
        flow = across(left_ref[component], own, right_ref[component])
        field = trust * flow
        for _ in range(STEPS):
            below = jnp.where(row == 0, 0.0, pltpu.roll(field, 1, 0))
            above = jnp.where(row == ny - 1, 0.0, pltpu.roll(field, ny - 1, 0))
            beside = pltpu.roll(field, 1, 1) + pltpu.roll(field, N - 1, 1)
            lap = above + below + beside - 4.0 * field
            field = (field + SPRING * (lap + trust * (flow - field))) * valid
        fields.append(field)
    return fields


def edge_kernel(tile_ref, target_ref, share_ref, first_ref, second_ref, off_ref, padded, out_ref, window, sems):
    y = pl.program_id(0)
    ny, nx = padded.shape[:2]
    even = tile_ref[0] % 2 == 0
    halos = {
        side: ((first_ref, on_at), (second_ref, on_at + 1), (off_ref, HB - on_at))
        for side, on_at in ((True, HB), (False, 0))
    }
    copies = {
        side: [
            pltpu.make_async_copy(ref, window.at[:, into : into + ref.shape[1]], sems.at[i])
            for i, (ref, into) in enumerate(places)
        ]
        for side, places in halos.items()
    }

    @pl.when((y == 0) & even)
    def _():
        for copy in copies[True]:
            copy.start()

    @pl.when((y == 0) & jnp.logical_not(even))
    def _():
        for copy in copies[False]:
            copy.start()

    border = jnp.zeros((2 * HB, PAD, N), jnp.float32)
    out_ref[y, :, :PAD] = border
    out_ref[y, :, PAD + N :] = border

    @pl.when(y == 0)
    def _():
        for copy in copies[True]:
            copy.wait()

    for i, x in enumerate((*range(HB), *range(nx - HB, nx))):
        more = blend_cell(y, K * nx + x, nx, target_ref, share_ref, window)
        out_ref[y, i, PAD : PAD + N] = padded[y, x, PAD : PAD + N] + more


def edges_of(tile, target, share, first, second, off, blended):
    ny, _, tall, _ = blended.shape
    vmem = pl.BlockSpec(memory_space=pltpu.VMEM)
    return pl.pallas_call(
        edge_kernel,
        grid=(ny,),
        in_specs=[pl.BlockSpec(memory_space=pltpu.SMEM)] * 3 + [vmem] * 4,
        out_specs=vmem,
        out_shape=pltpu.VMEM((ny, 2 * HB, tall, N), jnp.float32),
        scratch_shapes=[pltpu.VMEM((ny, 2 * HB, N, N), jnp.bfloat16), pltpu.SemaphoreType.DMA((3,))],
        compiler_params=pltpu.CompilerParams(vmem_limit_bytes=4 * MIB),
        cost_estimate=pl.CostEstimate(flops=5_000_000, bytes_accessed=4 * MIB, transcendentals=0),
        name="edges",
    )(tile, target, share, in_vmem(first), in_vmem(second), in_vmem(off), in_vmem(blended))


def warped(cell, down_shift, right_shift):
    whole_of = lambda shift: (shift + 256.0).astype(jnp.int32) - 256
    line = lambda value: jnp.full((1, N), value, jnp.float32).astype(jnp.bfloat16)
    down = jnp.clip(whole_of(down_shift), 4 - PAD, PAD - 6)
    part = down_shift - down.astype(jnp.float32)
    upper = cell[pl.ds(PAD + down, N), :]
    lower = cell[pl.ds(PAD + 1 + down, N), :]
    image = upper + part * (lower - upper)
    right = whole_of(right_shift).astype(jnp.float32)
    apart = lax.broadcasted_iota(jnp.int32, (N, N), 0) - lax.broadcasted_iota(jnp.int32, (N, N), 1)
    apart = apart.astype(jnp.bfloat16) - line(right)
    one = jnp.bfloat16(1.0)
    hat = jnp.maximum(jnp.bfloat16(0.0), one - jnp.abs(apart - line(right_shift - right)))
    return dot(image.astype(jnp.bfloat16), hat).astype(jnp.bfloat16)


def warp_kernel(tile_ref, *refs):
    *flows, padded, edges, out_hbm, field_ref, out, wide, field, sem, out_sems = refs
    y = pl.program_id(0)
    ny, nx = out.shape[:2]

    @pl.when(y == 0)
    def _():
        for component, values in enumerate(relax(tile_ref, *flows)):
            wide[component] = values
            field_ref[0, component] = values[:, STEPS : STEPS + nx]
        scalars = pltpu.make_async_copy(wide, field, sem)
        scalars.start()
        scalars.wait()

    borders = (*range(HB), *range(nx - HB, nx))
    for x in range(nx):
        cell = edges.at[y, borders.index(x)] if x in borders else padded.at[y, x]
        out[y, x] = warped(cell, field[0, y, STEPS + x], field[1, y, STEPS + x])
    store = lambda row: pltpu.make_async_copy(out.at[row], out_hbm.at[0, row], out_sems.at[row])
    store(y).start()
    wait_all([store(row) for row in range(ny)])


def warp(tile, flows, blended, edges):
    ny, nx = blended.shape[:2]
    whole = lambda shape: pl.BlockSpec(shape, lambda y: (0,) * len(shape))
    return pl.pallas_call(
        warp_kernel,
        grid=(ny,),
        in_specs=[pl.BlockSpec(memory_space=pltpu.SMEM)]
        + [whole(x.shape) for x in flows]
        + [pl.BlockSpec(memory_space=pltpu.VMEM)] * 2,
        out_specs=[pl.BlockSpec(memory_space=pl.ANY), whole((1, 2, ny, nx))],
        out_shape=[
            jax.ShapeDtypeStruct((1, ny, nx, N, N), jnp.bfloat16),
            jax.ShapeDtypeStruct((1, 2, ny, nx), jnp.float32),
        ],
        scratch_shapes=[
            pltpu.VMEM((ny, nx, N, N), jnp.bfloat16),
            pltpu.VMEM((2, ny, N), jnp.float32),
            pltpu.SMEM((2, ny, N), jnp.float32),
            pltpu.SemaphoreType.DMA,
            pltpu.SemaphoreType.DMA((ny,)),
        ],
        compiler_params=pltpu.CompilerParams(vmem_limit_bytes=8 * MIB),
        cost_estimate=pl.CostEstimate(flops=20_000_000, bytes_accessed=12 * MIB, transcendentals=0),
        name="warp",
    )(tile, *flows, in_vmem(blended), in_vmem(edges))


def from_behind(x, axis, by):
    length = lax.axis_size(axis)
    pairs = [(i, i + by) for i in range(length) if 0 <= i + by < length]
    return lax.ppermute(x, axis, pairs)


def swapped(x):
    return lax.ppermute(x, "tile", [(i, i ^ 1) for i in range(lax.axis_size("tile"))])


def hops(tiles, sections, far):
    pairs = ([], [])
    for section in range(sections):
        x_low, rest = divmod(section, sections // 2)
        way = 1 if rest < sections // 4 else -1
        for tile in range(tiles):
            z, x_high = divmod(tile, 2)
            to_z = z + 2 * x_high - 1 if far else z
            ends = [section * tiles + tile]
            for hop in (1, 2):
                x = (2 * x_high + x_low + hop * way) % 4
                ends.append((x % 2 * (sections // 2) + rest) * tiles + 2 * (to_z if hop == 2 else z) + x // 2)
            pairs[0].append((ends[0], ends[1]))
            if 0 <= to_z < tiles // 2:
                pairs[1].append((ends[1], ends[2]))
    return pairs


def beyond(x):
    tiles = lax.axis_size("tile")
    pairs = [(i, i + 1) for i in range(1, tiles - 1, 2)]
    ends = [(i, i) for i in (0, tiles - 1)]
    return lax.ppermute(x, "tile", ends + pairs + [(j, i) for i, j in pairs])


def per_device(sections, node_mask, box_row, box_shift, box_count, blend_weight):
    ny, nx = sections.shape[1:3]
    rows, cols, back_cols, back_rows = tables()
    half = ny // 2
    tiles, count = lax.axis_size("tile"), lax.axis_size("sec")
    tile = jnp.stack([lax.axis_index("tile"), tiles]).astype(jnp.int32)
    on_hops, off_hops = hops(tiles, count, False), hops(tiles, count, True)
    hop = lambda x, pairs: lax.ppermute(x, ("sec", "tile"), pairs)

    spectra_high, source, off = forward(tile, sections, half, half, False, None, rows, cols)
    from_last = from_behind(spectra_high, "sec", 1)
    off = hop(off, off_hops[0])
    spectra_low, source, first, second = forward(tile, sections, 0, half, True, source, rows, cols)
    from_next = from_behind(spectra_low, "sec", -1)
    first = hop(first, on_hops[0])
    target, share = slots_of(tile, box_row, box_shift, box_count, blend_weight)
    off, source = lax.optimization_barrier((off, source))
    off = hop(off, off_hops[1])
    blended = blend(target, share, source)
    first, blended = lax.optimization_barrier((first, blended))
    first = hop(first, on_hops[1])
    from_last, blended = lax.optimization_barrier((from_last, blended))

    flow_high = flow_of(spectra_high, from_last, -1, half, nx, cols, back_cols, back_rows)
    second, flow_high = lax.optimization_barrier((second, flow_high))
    flow_high = lax.ppermute(flow_high, "sec", [(i, (i - 1) % count) for i in range(count)])
    second = swapped(second)
    from_next, flow_high, off = lax.optimization_barrier((from_next, flow_high, off))
    flow_low = flow_of(spectra_low, from_next, 1, half, nx, cols, back_cols, back_rows)
    flow = jnp.concatenate([flow_low, flow_high], axis=1)
    flow = jnp.concatenate([flow, node_mask.astype(jnp.float32) + 1.0], axis=0)
    flow_off = beyond(flow)
    flow_on = swapped(flow)
    flows = (flow_low, flow_high, node_mask, flow_on, flow_off)
    edges = edges_of(tile, target, share, first, second, off, blended)
    return tuple(warp(tile, flows, blended, edges))


def solution(mesh):
    return jax.shard_map(
        per_device,
        mesh=mesh,
        in_specs=(
            P("sec", None, "tile", None, None),
            P("sec", None, "tile"),
            P("sec", None, "tile", None),
            P("sec", None, "tile", None),
            P("sec", None, "tile"),
            P("sec", None, "tile", None),
        ),
        out_specs=(P("sec", None, "tile", None, None), P("sec", None, None, "tile")),
        check_vma=False,
    )
```

```python
import functools

import jax
import jax.numpy as jnp
import numpy as np
from jax import lax
from jax.experimental import pallas as pl
from jax.experimental.pallas import tpu as pltpu
from jax.sharding import PartitionSpec as P

K = 4
HB = 2
STEPS = 3
N = 128
HALF = N // 2
PAD = 72
ROW = 32
DEPTH = 2
SPRING = 0.2
EPS = 1e-06
MIB = 1024 * 1024


def split(x):
    high = x.astype(jnp.bfloat16)
    return high, (x - high.astype(jnp.float32)).astype(jnp.bfloat16)


def tables():
    grid = np.arange(N)[:, None] * np.arange(N)[None, :] % N
    cosine = np.cos(2.0 * np.pi * grid / N)
    sine = np.sin(2.0 * np.pi * grid / N)
    rows = np.concatenate([cosine[:HALF], sine[:HALF]])
    rows[HALF] = cosine[HALF]
    cols = np.block([[cosine, -sine], [-sine, -cosine]])
    back_cols = np.block([[cosine, sine], [-sine, cosine]]) / N
    weight = np.where(np.arange(HALF) == 0, 1.0, 2.0)
    back_rows = np.concatenate([cosine[:, :HALF] * weight, -2.0 * sine[:, :HALF]], axis=1) / N
    back_rows[:, HALF] = cosine[:, HALF] / N
    return [jnp.asarray(t, jnp.float32) for t in (rows, cols, back_cols, back_rows)]


def first_row(shape):
    return lax.broadcasted_iota(jnp.int32, shape, len(shape) - 2) == 0


def dot(a, b):
    return jnp.dot(a, b, preferred_element_type=jnp.float32)


def ahead(fetch, rows, depth):
    y = pl.program_id(0)

    @pl.when(y == 0)
    def _():
        for row in range(depth):
            for copy in fetch(row):
                copy.start()

    @pl.when(y + depth < rows)
    def _():
        for copy in fetch(y + depth):
            copy.start()

    for copy in fetch(y):
        copy.wait()


def in_hbm(x):
    return pltpu.with_memory_space_constraint(x, pltpu.HBM)


def in_vmem(x):
    return pltpu.with_memory_space_constraint(x, pltpu.VMEM)


def wait_all(copies):
    @pl.when(pl.program_id(0) == pl.num_programs(0) - 1)
    def _():
        for copy in copies:
            copy.wait()


def forward_kernel(start, toward_pair, tile_ref, x_hbm, rows_hbm, cols_hbm, *refs):
    *refs, x_ref, rest_ref, lines_ref, ends_ref, rows_ref, cols_ref, in_sems, more_sems = refs
    spec_ref, src_ref, *strip_refs = refs[-2 - (HB if toward_pair else 1) :]
    y = pl.program_id(0)
    count, patches = x_ref.shape[:2]
    ny = src_ref.shape[0]
    odd = tile_ref[0] % 2
    column = ((1 - odd) if toward_pair else odd) * (patches - HB)
    rest = (start + count) % ny
    fetch = lambda row: [pltpu.make_async_copy(x_hbm.at[0, start + row], x_ref.at[row], in_sems.at[row])]
    to_strip = lambda i: strip_refs[i].at[:, 0] if toward_pair else strip_refs[0].at[:, i]
    more = [
        pltpu.make_async_copy(rows_hbm, rows_ref, more_sems.at[0]),
        pltpu.make_async_copy(cols_hbm, cols_ref, more_sems.at[1]),
        pltpu.make_async_copy(
            x_hbm.at[0, pl.ds(rest, ny - count), pl.ds(column, HB)], rest_ref, more_sems.at[2]
        ),
    ]

    @pl.when(y == 0)
    def _():
        for copy in more[:2]:
            copy.start()

    ahead(fetch, count, min(DEPTH, count))

    @pl.when(y == 0)
    def _():
        for copy in more[:2]:
            copy.wait()
        more[2].start()

    @pl.when(y == count - 1)
    def _():
        more[2].wait()
        for i in range(HB):
            to_strip(i)[rest : rest + ny - count] = rest_ref[:, i].astype(jnp.bfloat16)

    for i in range(HB):
        to_strip(i)[start + y] = x_ref[y, column + i].astype(jnp.bfloat16)
    rows2 = rows_ref[...]
    cols = cols_ref[...]
    for pair in range(patches // 2):
        x = jnp.concatenate([x_ref[y, 2 * pair], x_ref[y, 2 * pair + 1]], axis=1)
        high = x.astype(jnp.bfloat16)
        src_ref[start + y, 2 * pair] = high[:, :N]
        src_ref[start + y, 2 * pair + 1] = high[:, N:]
        both = dot(rows2[:, :N], high)
        for side in range(2):
            here = both[:, side * N : (side + 1) * N]
            p = 2 * pair + side
            ends_ref[p : p + 1, :N] = here[:1]
            ends_ref[p : p + 1, N:] = here[HALF : HALF + 1]
            lines_ref[p * HALF : (p + 1) * HALF, :N] = here[:HALF].astype(jnp.bfloat16)
            lines_ref[p * HALF : (p + 1) * HALF, N:] = here[HALF:].astype(jnp.bfloat16)
    step = 4
    for first in range(0, patches, step):
        lines = lines_ref[first * HALF : (first + step) * HALF, :]
        freq = dot(lines, cols).reshape(step, HALF, 2 * N)
        spec_ref[pl.ds(y * patches + first, step)] = freq.astype(jnp.bfloat16)
    ends = ends_ref[...].astype(jnp.bfloat16)
    spec_ref[count * patches, pl.ds(pl.multiple_of(y * patches, patches), patches), :] = ends


def forward(tile, sections, start, count, toward_pair, source, rows, cols):
    _, ny, nx, _, _ = sections.shape
    rows2 = jnp.concatenate([rows, rows], axis=1).astype(jnp.bfloat16)
    spectra = (count * nx + 1, HALF, 2 * N)
    before = () if source is None else (in_vmem(source),)
    strips = (1,) * HB if toward_pair else (HB,)
    return pl.pallas_call(
        functools.partial(forward_kernel, start, toward_pair),
        grid=(count,),
        in_specs=[pl.BlockSpec(memory_space=pltpu.SMEM)]
        + [pl.BlockSpec(memory_space=pltpu.HBM)] * 3
        + [pl.BlockSpec(memory_space=pltpu.VMEM)] * len(before),
        out_specs=[pl.BlockSpec(memory_space=pltpu.VMEM)] * (2 + len(strips)),
        out_shape=[
            pltpu.VMEM(spectra, jnp.bfloat16),
            pltpu.VMEM((ny, nx, N, N), jnp.bfloat16),
            *(pltpu.VMEM((ny, wide, N, N), jnp.bfloat16) for wide in strips),
        ],
        scratch_shapes=[
            pltpu.VMEM((count, nx, N, N), jnp.float32),
            pltpu.VMEM((ny - count, HB, N, N), jnp.float32),
            pltpu.VMEM((nx * HALF, 2 * N), jnp.bfloat16),
            pltpu.VMEM((nx, 2 * N), jnp.float32),
            pltpu.VMEM((N, 2 * N), jnp.bfloat16),
            pltpu.VMEM((2 * N, 2 * N), jnp.bfloat16),
            pltpu.SemaphoreType.DMA((count,)),
            pltpu.SemaphoreType.DMA((3,)),
        ],
        input_output_aliases={4: 1} if before else {},
        compiler_params=pltpu.CompilerParams(vmem_limit_bytes=12 * MIB),
        cost_estimate=pl.CostEstimate(flops=2_000_000_000, bytes_accessed=6 * MIB, transcendentals=0),
        name="forward",
    )(tile, in_hbm(sections), in_hbm(rows2), in_hbm(cols.astype(jnp.bfloat16)), *before)


def times_conj(a, b, sign):
    ar, ai, br, bi = a[:, :N], a[:, N:], b[:, :N], b[:, N:]
    real = ar * br + ai * bi
    imag = ai * br - ar * bi if sign > 0 else ar * bi - ai * br
    return jnp.concatenate([real, imag], axis=1).astype(jnp.bfloat16)


def flow_kernel(sign, own, other, cols_ref, back_cols_ref, back_rows_ref, flow_ref, sides, sums, moments):
    y = pl.program_id(0)
    ny, patches = sums.shape[:2]
    last = ny * patches
    cols = cols_ref[...]
    back_cols = back_cols_ref[...]
    back_rows = back_rows_ref[...]

    @pl.when(y == 0)
    def _():
        lines = jnp.concatenate([own[last], other[last]], axis=0)
        edge = dot(jnp.concatenate([lines[:, :N], lines[:, N:]], axis=0), cols[:N])
        quarter = edge.reshape(4, last, 2 * N)
        low = times_conj(quarter[0], quarter[1], sign)
        high = times_conj(quarter[2], quarter[3], sign)
        back = dot(jnp.concatenate([low, high], axis=0), back_cols[:, :N])
        sides[...] = back.reshape(sides.shape)

    shift_rows = lax.broadcasted_iota(jnp.int32, (N, N), 0)
    offset_rows = (((shift_rows + HALF) % N) - HALF).astype(jnp.float32)
    offset_rows = jnp.concatenate([offset_rows, offset_rows], axis=1)
    step = 4
    for first in range(0, patches, step):
        here = pl.ds(y * patches + first, step)
        a = own[here].reshape(step * HALF, 2 * N).astype(jnp.float32)
        b = other[here].reshape(step * HALF, 2 * N).astype(jnp.float32)
        back = dot(times_conj(a, b, sign), back_cols)
        halves = []
        for i in range(step):
            p = first + i
            parts = []
            for side in range(2):
                part = back[i * HALF : (i + 1) * HALF, side * N : (side + 1) * N]
                top = jnp.where(first_row((16, N)), sides[side, y, p : p + 1, :], part[:16])
                parts += [top.astype(jnp.bfloat16), part[16:].astype(jnp.bfloat16)]
            halves.append(jnp.concatenate(parts, axis=0))
        for i in range(0, step, 2):
            corr = dot(back_rows, jnp.concatenate(halves[i : i + 2], axis=1))
            power = corr * corr
            total = power.sum(0, keepdims=True)
            moment = (power * offset_rows).sum(0, keepdims=True)
            for side in range(2):
                p = first + i + side
                sums[y, p : p + 1, :] = total[:, side * N : (side + 1) * N]
                moments[y, p : p + 1, :] = moment[:, side * N : (side + 1) * N]

    @pl.when(y == ny - 1)
    def _():
        lane = lax.broadcasted_iota(jnp.int32, (8, N), 1)
        row = lax.broadcasted_iota(jnp.int32, (8, N), 0)
        offset_cols = (((lane + HALF) % N) - HALF).astype(jnp.float32)
        reduce_by = jnp.where(row == 0, 1.0, jnp.where(row == 1, offset_cols, 0.0))
        over_lanes = lambda m: lax.dot_general(
            reduce_by, m.reshape(last, N), (((1,), (1,)), ((), ())),
            precision=lax.Precision.HIGHEST, preferred_element_type=jnp.float32,
        )
        by_sums = over_lanes(sums[...])
        by_moments = over_lanes(moments[...])
        total = by_sums[0:1] + EPS
        along_rows = by_moments[0:1] / total
        along_cols = by_sums[1:2] / total
        for row in range(ny):
            flow_ref[0, row : row + 1, :] = along_rows[:, row * patches : (row + 1) * patches]
            flow_ref[1, row : row + 1, :] = along_cols[:, row * patches : (row + 1) * patches]


def flow_of(own, other, sign, ny, nx, cols, back_cols, back_rows):
    whole = lambda shape: pl.BlockSpec(shape, lambda y: (0,) * len(shape))
    return pl.pallas_call(
        functools.partial(flow_kernel, sign),
        grid=(ny,),
        in_specs=[
            pl.BlockSpec(memory_space=pltpu.VMEM),
            pl.BlockSpec(memory_space=pltpu.VMEM),
            whole((2 * N, 2 * N)),
            whole((2 * N, 2 * N)),
            whole((N, N)),
        ],
        out_specs=whole((2, ny, nx)),
        out_shape=jax.ShapeDtypeStruct((2, ny, nx), jnp.float32),
        scratch_shapes=[
            pltpu.VMEM((2, ny, nx, N), jnp.float32),
            pltpu.VMEM((ny, nx, N), jnp.float32),
            pltpu.VMEM((ny, nx, N), jnp.float32),
        ],
        compiler_params=pltpu.CompilerParams(vmem_limit_bytes=8 * MIB),
        cost_estimate=pl.CostEstimate(flops=0 if sign < 0 else 0, bytes_accessed=0, transcendentals=0),
        name="flow",
    )(in_vmem(own), in_vmem(other), *(t.astype(jnp.bfloat16) for t in (cols, back_cols, back_rows)))


def slots_kernel(tile_ref, rows_ref, shifts_ref, count_ref, weight_ref, target_ref, share_ref):
    ny, _, nx = rows_ref.shape[1:]
    tile, tiles = tile_ref[0], tile_ref[1]
    live = [k < count_ref[0] for k in range(K)]
    weights = [jnp.where(live[k], weight_ref[0, :, k, :], 0.0) for k in range(K)]
    total = weights[0] + weights[1] + weights[2] + weights[3]
    share = [(w / total).astype(jnp.bfloat16).astype(jnp.float32) for w in weights]
    columns = [lax.broadcasted_iota(jnp.int32, (ny, nx), 1) + shifts_ref[0, :, k, :] for k in range(K)]
    rows = [rows_ref[0, :, k, :] * ROW for k in range(K)]
    low = [c < 0 for c in columns]
    high = [c >= nx for c in columns]
    first, last = tile == 0, tile == tiles - 1
    inside = [jnp.where(l | h, 0.0, s) for l, h, s in zip(low, high, share, strict=True)]
    share_low = [jnp.where(first, 0.0, jnp.where(l, s, 0.0)) for l, s in zip(low, share, strict=True)]
    share_high = [jnp.where(last, 0.0, jnp.where(h, s, 0.0)) for h, s in zip(high, share, strict=True)]
    beyond = [l + h for l, h in zip(share_low, share_high, strict=True)]
    share_ref[...] = jnp.concatenate(inside + beyond, axis=1)
    target = [r + jnp.where(l | h, 0, c) for r, c, l, h in zip(rows, columns, low, high, strict=True)]
    away = [
        r + jnp.where(l, c + HB, jnp.where(h, c - nx + HB, 0))
        for r, c, l, h in zip(rows, columns, low, high, strict=True)
    ]
    target_ref[...] = jnp.concatenate(target + away, axis=1)


def slots_of(tile, box_row, box_shift, box_count, blend_weight):
    ny = box_row.shape[1]
    slots_first = lambda x: jnp.transpose(x, (0, 1, 3, 2))
    return pl.pallas_call(
        slots_kernel,
        in_specs=[pl.BlockSpec(memory_space=pltpu.SMEM)] + [pl.BlockSpec(memory_space=pltpu.VMEM)] * 4,
        out_shape=[
            jax.ShapeDtypeStruct((ny, N), jnp.int32),
            jax.ShapeDtypeStruct((ny, N), jnp.float32),
        ],
        compiler_params=pltpu.CompilerParams(vmem_limit_bytes=4 * MIB),
        cost_estimate=pl.CostEstimate(flops=0, bytes_accessed=0, transcendentals=0),
        name="slots",
    )(tile, slots_first(box_row), slots_first(box_shift), box_count, slots_first(blend_weight))


def blend_cell(y, first, nx, target_ref, share_ref, window):
    total = None
    for k in range(K):
        spot = target_ref[y, first + k * nx]
        piece = window[spot // ROW, spot % ROW].astype(jnp.float32) * share_ref[y, first + k * nx]
        total = piece if total is None else total + piece
    return total


def blend_kernel(target_ref, share_ref, source, out_ref):
    y = pl.program_id(0)
    nx = source.shape[1]
    border = jnp.zeros((nx, PAD, N), jnp.float32)
    out_ref[y, :, :PAD] = border
    out_ref[y, :, PAD + N :] = border
    for x in range(nx):
        out_ref[y, x, PAD : PAD + N] = blend_cell(y, x, nx, target_ref, share_ref, source)


def blend(target, share, source):
    ny, nx = source.shape[:2]
    return pl.pallas_call(
        blend_kernel,
        grid=(ny,),
        in_specs=[pl.BlockSpec(memory_space=pltpu.SMEM)] * 2 + [pl.BlockSpec(memory_space=pltpu.VMEM)],
        out_specs=pl.BlockSpec(memory_space=pltpu.VMEM),
        out_shape=pltpu.VMEM((ny, nx, N + 2 * PAD, N), jnp.float32),
        compiler_params=pltpu.CompilerParams(vmem_limit_bytes=4 * MIB),
        cost_estimate=pl.CostEstimate(flops=16_000_000_000, bytes_accessed=4 * MIB, transcendentals=0),
        name="blend",
    )(target, share, in_vmem(source))


def relax(tile_ref, low_ref, high_ref, mask_ref, on_ref, off_ref):
    ny, nx = mask_ref.shape[1:]
    even = tile_ref[0] % 2 == 0
    left_ref = [jnp.where(even, off_ref[i], on_ref[i]) for i in range(3)]
    right_ref = [jnp.where(even, on_ref[i], off_ref[i]) for i in range(3)]
    rest = jnp.zeros((ny, N - nx - 2 * STEPS), jnp.float32)

    def across(left, own, right):
        return jnp.concatenate([left[:, nx - STEPS :], own, right[:, :STEPS], rest], axis=1)

    known = across(left_ref[2], mask_ref[0].astype(jnp.float32) + 1.0, right_ref[2])
    valid = jnp.where(known > 0.5, 1.0, 0.0)
    trust = jnp.where(known > 1.5, 1.0, 0.0)
    row = lax.broadcasted_iota(jnp.int32, trust.shape, 0)
    fields = []
    for component in range(2):
        own = jnp.concatenate([low_ref[component], high_ref[component]], axis=0)
        flow = across(left_ref[component], own, right_ref[component])
        field = trust * flow
        for _ in range(STEPS):
            below = jnp.where(row == 0, 0.0, pltpu.roll(field, 1, 0))
            above = jnp.where(row == ny - 1, 0.0, pltpu.roll(field, ny - 1, 0))
            beside = pltpu.roll(field, 1, 1) + pltpu.roll(field, N - 1, 1)
            lap = above + below + beside - 4.0 * field
            field = (field + SPRING * (lap + trust * (flow - field))) * valid
        fields.append(field)
    return fields


def edge_kernel(tile_ref, target_ref, share_ref, first_ref, second_ref, off_ref, padded, out_ref, window, sems):
    y = pl.program_id(0)
    ny, nx = padded.shape[:2]
    even = tile_ref[0] % 2 == 0
    halos = {
        side: ((first_ref, on_at), (second_ref, on_at + 1), (off_ref, HB - on_at))
        for side, on_at in ((True, HB), (False, 0))
    }
    copies = {
        side: [
            pltpu.make_async_copy(ref, window.at[:, into : into + ref.shape[1]], sems.at[i])
            for i, (ref, into) in enumerate(places)
        ]
        for side, places in halos.items()
    }

    @pl.when((y == 0) & even)
    def _():
        for copy in copies[True]:
            copy.start()

    @pl.when((y == 0) & jnp.logical_not(even))
    def _():
        for copy in copies[False]:
            copy.start()

    border = jnp.zeros((2 * HB, PAD, N), jnp.float32)
    out_ref[y, :, :PAD] = border
    out_ref[y, :, PAD + N :] = border

    @pl.when(y == 0)
    def _():
        for copy in copies[True]:
            copy.wait()

    for i, x in enumerate((*range(HB), *range(nx - HB, nx))):
        more = blend_cell(y, K * nx + x, nx, target_ref, share_ref, window)
        out_ref[y, i, PAD : PAD + N] = padded[y, x, PAD : PAD + N] + more


def edges_of(tile, target, share, first, second, off, blended):
    ny, _, tall, _ = blended.shape
    vmem = pl.BlockSpec(memory_space=pltpu.VMEM)
    return pl.pallas_call(
        edge_kernel,
        grid=(ny,),
        in_specs=[pl.BlockSpec(memory_space=pltpu.SMEM)] * 3 + [vmem] * 4,
        out_specs=vmem,
        out_shape=pltpu.VMEM((ny, 2 * HB, tall, N), jnp.float32),
        scratch_shapes=[pltpu.VMEM((ny, 2 * HB, N, N), jnp.bfloat16), pltpu.SemaphoreType.DMA((3,))],
        compiler_params=pltpu.CompilerParams(vmem_limit_bytes=4 * MIB),
        cost_estimate=pl.CostEstimate(flops=5_000_000, bytes_accessed=4 * MIB, transcendentals=0),
        name="edges",
    )(tile, target, share, in_vmem(first), in_vmem(second), in_vmem(off), in_vmem(blended))


def warped(cell, down_shift, right_shift):
    whole_of = lambda shift: (shift + 256.0).astype(jnp.int32) - 256
    line = lambda value: jnp.full((1, N), value, jnp.float32).astype(jnp.bfloat16)
    down = jnp.clip(whole_of(down_shift), 4 - PAD, PAD - 6)
    part = down_shift - down.astype(jnp.float32)
    upper = cell[pl.ds(PAD + down, N), :]
    lower = cell[pl.ds(PAD + 1 + down, N), :]
    image = upper + part * (lower - upper)
    right = whole_of(right_shift).astype(jnp.float32)
    apart = lax.broadcasted_iota(jnp.int32, (N, N), 0) - lax.broadcasted_iota(jnp.int32, (N, N), 1)
    apart = apart.astype(jnp.bfloat16) - line(right)
    one = jnp.bfloat16(1.0)
    hat = jnp.maximum(jnp.bfloat16(0.0), one - jnp.abs(apart - line(right_shift - right)))
    return dot(image.astype(jnp.bfloat16), hat).astype(jnp.bfloat16)


def warp_kernel(tile_ref, *refs):
    *flows, padded, edges, out_hbm, field_ref, out, wide, field, sem, out_sems = refs
    y = pl.program_id(0)
    ny, nx = out.shape[:2]

    @pl.when(y == 0)
    def _():
        for component, values in enumerate(relax(tile_ref, *flows)):
            wide[component] = values
            field_ref[0, component] = values[:, STEPS : STEPS + nx]
        scalars = pltpu.make_async_copy(wide, field, sem)
        scalars.start()
        scalars.wait()

    borders = (*range(HB), *range(nx - HB, nx))
    for x in range(nx):
        cell = edges.at[y, borders.index(x)] if x in borders else padded.at[y, x]
        out[y, x] = warped(cell, field[0, y, STEPS + x], field[1, y, STEPS + x])
    store = lambda row: pltpu.make_async_copy(out.at[row], out_hbm.at[0, row], out_sems.at[row])
    store(y).start()
    wait_all([store(row) for row in range(ny)])


def warp(tile, flows, blended, edges):
    ny, nx = blended.shape[:2]
    whole = lambda shape: pl.BlockSpec(shape, lambda y: (0,) * len(shape))
    return pl.pallas_call(
        warp_kernel,
        grid=(ny,),
        in_specs=[pl.BlockSpec(memory_space=pltpu.SMEM)]
        + [whole(x.shape) for x in flows]
        + [pl.BlockSpec(memory_space=pltpu.VMEM)] * 2,
        out_specs=[pl.BlockSpec(memory_space=pl.ANY), whole((1, 2, ny, nx))],
        out_shape=[
            jax.ShapeDtypeStruct((1, ny, nx, N, N), jnp.bfloat16),
            jax.ShapeDtypeStruct((1, 2, ny, nx), jnp.float32),
        ],
        scratch_shapes=[
            pltpu.VMEM((ny, nx, N, N), jnp.bfloat16),
            pltpu.VMEM((2, ny, N), jnp.float32),
            pltpu.SMEM((2, ny, N), jnp.float32),
            pltpu.SemaphoreType.DMA,
            pltpu.SemaphoreType.DMA((ny,)),
        ],
        compiler_params=pltpu.CompilerParams(vmem_limit_bytes=8 * MIB),
        cost_estimate=pl.CostEstimate(flops=20_000_000, bytes_accessed=12 * MIB, transcendentals=0),
        name="warp",
    )(tile, *flows, in_vmem(blended), in_vmem(edges))


def from_behind(x, axis, by):
    length = lax.axis_size(axis)
    pairs = [(i, i + by) for i in range(length) if 0 <= i + by < length]
    return lax.ppermute(x, axis, pairs)


def swapped(x):
    return lax.ppermute(x, "tile", [(i, i ^ 1) for i in range(lax.axis_size("tile"))])


def hops(tiles, sections, far):
    pairs = ([], [])
    for section in range(sections):
        x_low, rest = divmod(section, sections // 2)
        way = 1 if rest < sections // 4 else -1
        for tile in range(tiles):
            z, x_high = divmod(tile, 2)
            to_z = z + 2 * x_high - 1 if far else z
            ends = [section * tiles + tile]
            for hop in (1, 2):
                x = (2 * x_high + x_low + hop * way) % 4
                ends.append((x % 2 * (sections // 2) + rest) * tiles + 2 * (to_z if hop == 2 else z) + x // 2)
            pairs[0].append((ends[0], ends[1]))
            if 0 <= to_z < tiles // 2:
                pairs[1].append((ends[1], ends[2]))
    return pairs


def beyond(x):
    tiles = lax.axis_size("tile")
    pairs = [(i, i + 1) for i in range(1, tiles - 1, 2)]
    return lax.ppermute(x, "tile", pairs + [(j, i) for i, j in pairs])


def per_device(sections, node_mask, box_row, box_shift, box_count, blend_weight):
    ny, nx = sections.shape[1:3]
    rows, cols, back_cols, back_rows = tables()
    half = ny // 2
    tiles, count = lax.axis_size("tile"), lax.axis_size("sec")
    tile = jnp.stack([lax.axis_index("tile"), tiles]).astype(jnp.int32)
    on_hops, off_hops = hops(tiles, count, False), hops(tiles, count, True)
    hop = lambda x, pairs: lax.ppermute(x, ("sec", "tile"), pairs)

    spectra_high, source, off = forward(tile, sections, half, half, False, None, rows, cols)
    from_last = from_behind(spectra_high, "sec", 1)
    off = hop(off, off_hops[0])
    spectra_low, source, first, second = forward(tile, sections, 0, half, True, source, rows, cols)
    from_next = from_behind(spectra_low, "sec", -1)
    first = hop(first, on_hops[0])
    target, share = slots_of(tile, box_row, box_shift, box_count, blend_weight)
    off, source = lax.optimization_barrier((off, source))
    off = hop(off, off_hops[1])
    blended = blend(target, share, source)
    first, blended = lax.optimization_barrier((first, blended))
    first = hop(first, on_hops[1])
    from_last, blended = lax.optimization_barrier((from_last, blended))

    flow_high = flow_of(spectra_high, from_last, -1, half, nx, cols, back_cols, back_rows)
    second, flow_high = lax.optimization_barrier((second, flow_high))
    flow_high = from_behind(flow_high, "sec", -1)
    second = swapped(second)
    from_next, flow_high, off = lax.optimization_barrier((from_next, flow_high, off))
    flow_low = flow_of(spectra_low, from_next, 1, half, nx, cols, back_cols, back_rows)
    flow = jnp.concatenate([flow_low, flow_high], axis=1)
    flow = jnp.concatenate([flow, node_mask.astype(jnp.float32) + 1.0], axis=0)
    flow_off = beyond(flow)
    flow_on = swapped(flow)
    flows = (flow_low, flow_high, node_mask, flow_on, flow_off)
    edges = edges_of(tile, target, share, first, second, off, blended)
    return tuple(warp(tile, flows, blended, edges))


def solution(mesh):
    return jax.shard_map(
        per_device,
        mesh=mesh,
        in_specs=(
            P("sec", None, "tile", None, None),
            P("sec", None, "tile"),
            P("sec", None, "tile", None),
            P("sec", None, "tile", None),
            P("sec", None, "tile"),
            P("sec", None, "tile", None),
        ),
        out_specs=(P("sec", None, "tile", None, None), P("sec", None, None, "tile")),
        check_vma=False,
    )
```
